32 devices in a mesh: ctx: 16 (over z, x, core), head: 2 (over y).
Axes of the slice: x: 2, y: 2, z: 4, core: 2. Of those that a mesh axis runs over, the one named last changes fastest.
Arguments:
- q_ret: bfloat16 [2048, 1024], P('ctx', 'head'), may hold values from -6 to 6
- k_ret: bfloat16 [2048, 1024], P('ctx', 'head'), may hold values from -6 to 6
- v_ret: bfloat16 [2048, 1024], P('ctx', 'head'), may hold values from -6 to 6
- gate_ret: bfloat16 [2048, 1024], P('ctx', 'head'), may hold values from -6 to 6
- log_decay: float32 [2048, 4], P('ctx', 'head'), may hold values from -2 to 0
- q_cross: bfloat16 [2048, 1024], P('ctx', 'head'), may hold values from -32 to 32
- cache_k: bfloat16 [2048, 512], P(('ctx', 'head')), may hold values from -16 to 16
- cache_v: bfloat16 [2048, 512], P(('ctx', 'head')), may hold values from -6 to 6
Outputs:
- o_ret: bfloat16 [2048, 1024], P('ctx', 'head')
- o_cross: bfloat16 [2048, 1024], P('ctx', 'head')
The draws below stay inside these ranges and needn't reach their ends.
All inputs are finite; a program needn't handle non-finite values.
Results may differ from the reference program's by a relative error of at most 0.0039.
Values may be sent and summed in bfloat16 or wider, within the bound.
No kernel may reach another device: no remote copies, remote signals or barrier semaphores. Data moves between devices by JAX's collectives and lax.ppermute only.
A program may use at most 128 MiB of HBM per device.

```python
import math
import jax
import jax.numpy as jnp
from jax import lax

TOK_DEV = 128
HD = 256
RETENTION_HEADS = 4
CACHE_HEADS = 2
PROMPT_TOKENS = 2048


def draw_q_cross(key, part):
    drawn_base = jnp.clip(2.5 * jax.random.normal(jax.random.fold_in(key, 1), (PROMPT_TOKENS, RETENTION_HEADS * HD), jnp.float32), -15.0, 15.0)
    return drawn_base.astype(jnp.bfloat16)


def draw_cache_k(key, part):
    drawn_base = jnp.clip(jax.random.normal(jax.random.fold_in(key, 2), (PROMPT_TOKENS, CACHE_HEADS * HD), jnp.float32), -6.0, 6.0)
    return drawn_base.astype(jnp.bfloat16)


def draw_log_decay(key, part):
    fast_count = 8
    quick_heads = jax.random.randint(jax.random.fold_in(key, 21), (RETENTION_HEADS,), 0, 16) < fast_count
    fast_rate = jnp.exp(jax.random.uniform(jax.random.fold_in(key, 22), (RETENTION_HEADS,), jnp.float32, math.log(3.0 / TOK_DEV), math.log(4.0 / TOK_DEV)))
    slow_rate = jnp.exp(jax.random.uniform(jax.random.fold_in(key, 23), (RETENTION_HEADS,), jnp.float32, math.log(1.0 / (64.0 * PROMPT_TOKENS)), math.log(1.0 / (8.0 * PROMPT_TOKENS))))
    head_rate = jnp.where(quick_heads, fast_rate, slow_rate)
    block_count = PROMPT_TOKENS // TOK_DEV
    block_factor = jnp.exp(jax.random.uniform(jax.random.fold_in(key, 24), (block_count, RETENTION_HEADS), jnp.float32, math.log(0.5), math.log(2.0)))
    block_factor = jnp.repeat(block_factor, TOK_DEV, axis=0)
    row_factor = jnp.exp(jax.random.uniform(jax.random.fold_in(key, 25), (PROMPT_TOKENS, RETENTION_HEADS), jnp.float32, math.log(0.5), math.log(2.0)))
    value_matrix = -head_rate[None, :] * block_factor * row_factor
    group_rows = jax.random.randint(jax.random.fold_in(key, 26), (2,), 0, PROMPT_TOKENS)
    group_length = jax.random.uniform(jax.random.fold_in(key, 27), (2, RETENTION_HEADS), jnp.float32, math.log(0.5), math.log(0.8))
    value_matrix = value_matrix.at[group_rows].add(group_length)
    return value_matrix


def steps_of(rng, dims, cuts, least, top_value):
    loudness, own = 1.0, jax.random.fold_in(rng, 6)
    for dim, parts in cuts:
        draws = jnp.exp(jax.random.uniform(jax.random.fold_in(own, dim), (parts,), jnp.float32, least / len(cuts), top_value / len(cuts)))
        loudness = loudness * jnp.repeat(draws, dims[dim] // parts).reshape([-1 if axis == dim else 1 for axis in range(len(dims))])
    return loudness


def bell_draw(rng, dims, scale, bound, split=(), held_as=jnp.bfloat16):
    result = jax.random.normal(rng, dims, jnp.float32) * scale
    if len(split) > 0:
        result = steps_of(rng, dims, split, -0.22, 0.18) * result
    return jnp.clip(result, min=-bound, max=bound).astype(held_as)


def setup_inputs(seed: int = 0) -> dict:
    key_of = jax.random.split(jax.random.key(seed), 9)
    q_ret = bell_draw(key_of[0], (PROMPT_TOKENS, RETENTION_HEADS * HD), 1.0, 6.0, ((0, 16), (1, 2)))
    k_ret = bell_draw(key_of[1], (PROMPT_TOKENS, RETENTION_HEADS * HD), 1.0, 6.0, ((0, 16), (1, 2)))
    v_ret = bell_draw(key_of[2], (PROMPT_TOKENS, RETENTION_HEADS * HD), 1.0, 6.0, ((0, 16), (1, 2)))
    gate_ret = bell_draw(key_of[3], (PROMPT_TOKENS, RETENTION_HEADS * HD), 1.0, 6.0, ((0, 16), (1, 2)))
    log_decay = draw_log_decay(jax.random.fold_in(key_of[8], 71), 0)
    q_cross = draw_q_cross(jax.random.fold_in(key_of[8], 71), 0)
    cache_k = draw_cache_k(jax.random.fold_in(key_of[8], 71), 0)
    cache_v = bell_draw(key_of[7], (PROMPT_TOKENS, CACHE_HEADS * HD), 1.0, 6.0, ((0, 32),))
    return {"q_ret": q_ret, "k_ret": k_ret, "v_ret": v_ret, "gate_ret": gate_ret, "log_decay": log_decay, "q_cross": q_cross, "cache_k": cache_k, "cache_v": cache_v}


norm_eps = 1e-06
highest = lax.Precision.HIGHEST

def by_heads(matrix_in):
    return matrix_in.reshape(matrix_in.shape[0], matrix_in.shape[1] // HD, HD).transpose(1, 0, 2)

def from_heads(stacked):
    return stacked.transpose(1, 0, 2).reshape(stacked.shape[1], stacked.shape[0] * HD)

def retention_all(q_ret, k_ret, v_ret, gate_ret, log_decay):
    span_len = TOK_DEV
    blocks = PROMPT_TOKENS // span_len

    def to_blocks(matrix_in):
        heads_first = by_heads(matrix_in)
        return heads_first.reshape(RETENTION_HEADS, blocks, span_len, HD).transpose(1, 0, 2, 3)
    queries = to_blocks(q_ret)
    key_heads = to_blocks(k_ret)
    value_heads = to_blocks(v_ret)
    decay_blocks = log_decay.reshape(blocks, span_len, RETENTION_HEADS)
    position = jnp.arange(span_len, dtype=jnp.int32)
    causal = position[:, None] >= position[None, :]

    def doubling_step(state_now, inputs):
        query_b, key_b, value_b, decay_b = inputs
        decay_sum = jnp.cumsum(decay_b, axis=0).T
        scores = jnp.einsum('hrd,hsd->hrs', query_b, key_b, preferred_element_type=jnp.float32)
        spread = jnp.minimum(decay_sum[:, :, None] - decay_sum[:, None, :], 0.0)
        weight_matrix = jnp.where(causal[None], jnp.exp(spread) * scores, 0.0).astype(jnp.bfloat16)
        within_block = jnp.einsum('hrs,hsd->hrd', weight_matrix, value_b, preferred_element_type=jnp.float32)
        from_before = jnp.exp(decay_sum)[:, :, None] * jnp.einsum('hrd,hde->hre', query_b.astype(jnp.float32), state_now, precision=highest)
        final_sum = decay_sum[:, -1]
        carried = (key_b.astype(jnp.float32) * jnp.exp(final_sum[:, None] - decay_sum)[:, :, None]).astype(jnp.bfloat16)
        summary = jnp.einsum('hsd,hse->hde', carried, value_b, preferred_element_type=jnp.float32)
        new_state = jnp.exp(final_sum)[:, None, None] * state_now + summary
        return (new_state, within_block + from_before)
    initial = jnp.zeros((RETENTION_HEADS, HD, HD), jnp.float32)
    unused, retained = lax.scan(doubling_step, initial, (queries, key_heads, value_heads, decay_blocks))
    retained = retained.transpose(1, 0, 2, 3).reshape(RETENTION_HEADS, PROMPT_TOKENS, HD)
    normed = retained * lax.rsqrt(lax.optimization_barrier(jnp.mean(retained * retained, axis=2, keepdims=True)) + norm_eps)
    gated_out = normed * jax.nn.silu(by_heads(gate_ret).astype(jnp.float32))
    return from_heads(gated_out).astype(jnp.bfloat16)

def cross_all(q_cross, cache_k, cache_v):
    span_len = math.gcd(PROMPT_TOKENS, 512)
    group_size = RETENTION_HEADS // CACHE_HEADS
    score_scale = 1.0 / math.sqrt(HD)
    queries = by_heads(q_cross)
    key_heads = jnp.repeat(by_heads(cache_k), group_size, axis=0)
    value_heads = jnp.repeat(by_heads(cache_v), group_size, axis=0)

    def one_head(inputs):
        query_h, key_h, value_h = inputs
        pieces = []
        for first_row in range(0, PROMPT_TOKENS, span_len):
            end_row = first_row + span_len
            scores = jnp.dot(query_h[first_row:end_row], key_h[:end_row].T, preferred_element_type=jnp.float32) * score_scale
            row_position = jnp.arange(first_row, end_row, dtype=jnp.int32)
            key_position = jnp.arange(0, end_row, dtype=jnp.int32)
            allowed = row_position[:, None] >= key_position[None, :]
            masked = jnp.where(allowed, scores, -jnp.inf)
            top_score = lax.optimization_barrier(jnp.max(masked, axis=1, keepdims=True))
            weight_matrix = jnp.where(allowed, jnp.exp(masked - top_score), 0.0)
            run_total = lax.optimization_barrier(jnp.sum(weight_matrix, axis=1, keepdims=True))
            mixed_out = jnp.dot(weight_matrix.astype(jnp.bfloat16), value_h[:end_row], preferred_element_type=jnp.float32)
            pieces.append(mixed_out / run_total)
        return jnp.concatenate(pieces, axis=0)
    stacked = lax.map(one_head, (queries, key_heads, value_heads))
    return from_heads(stacked).astype(jnp.bfloat16)

def reference(q_ret, k_ret, v_ret, gate_ret, log_decay, q_cross, cache_k, cache_v):
    o_ret = retention_all(q_ret, k_ret, v_ret, gate_ret, log_decay)
    o_cross = cross_all(q_cross, cache_k, cache_v)
    return (o_ret, o_cross)
```

```python
import functools
import math

import jax
import jax.numpy as jnp
from jax import lax
from jax.experimental import pallas as pl
from jax.experimental.pallas import tpu as pltpu
from jax.sharding import PartitionSpec as P

HD = 256
FAR = -1e30
NEAR = -1e29
EPS = 1e-06
F32 = jnp.float32
BF16 = jnp.bfloat16
PAD = 16
LANES = 128
VMEM = pl.BlockSpec(memory_space=pltpu.VMEM)


def call(body, outs, args, scratch=(), flops=1_000_000, name=None):
    moved = sum(math.prod(a.shape) * a.dtype.itemsize for a in (*args, *outs))
    single = len(outs) == 1
    return pl.pallas_call(
        body,
        out_shape=outs[0] if single else tuple(outs),
        in_specs=[VMEM] * len(args),
        out_specs=VMEM if single else tuple(VMEM for _ in outs),
        scratch_shapes=scratch,
        compiler_params=pltpu.CompilerParams(vmem_limit_bytes=40 * 1024 * 1024),
        cost_estimate=pl.CostEstimate(flops=flops, bytes_accessed=moved, transcendentals=0),
        name=name,
    )(*args)


def shape(dims, dtype=BF16):
    return jax.ShapeDtypeStruct(dims, dtype)


def dot(a, b, contract, precision=None):
    return lax.dot_general(
        a, b, (contract, ((), ())), preferred_element_type=F32, precision=precision
    )


def thirds(value):
    high = value.astype(BF16).astype(F32)
    rest = value - high
    middle = rest.astype(BF16).astype(F32)
    return high, middle, rest - middle


def decay_sums(log_decay):
    rows = log_decay.shape[0]
    below = lax.broadcasted_iota(jnp.int32, (rows, rows), 0) >= lax.broadcasted_iota(
        jnp.int32, (rows, rows), 1
    )
    lower = jnp.where(below, 1.0, 0.0).astype(F32)
    return dot(lower, log_decay, ((1,), (0,)), lax.Precision.HIGHEST), below


def split_cache(n, k_ref, v_ref, *pieces):
    width = pieces[0].shape[2]
    here = lax.axis_index("head")
    for e, piece in enumerate(pieces):
        target = lax.rem(here + e, n)
        columns = pl.ds(pl.multiple_of(target * width, LANES), width)
        piece[0] = k_ref[:, columns]
        piece[1] = v_ref[:, columns]


def write_total(out, head, at, total):
    row = lax.broadcasted_iota(jnp.int32, (PAD, HD), 0)
    high, middle, low = thirds(total)
    tile = jnp.where(row == 0, high, jnp.where(row == 1, middle, jnp.where(row == 2, low, 0.0)))
    out[head, pl.ds(at, PAD), :] = tile.astype(BF16)


def read_total(ref, head, at):
    tile = ref[head, pl.ds(at, PAD), :].astype(F32)
    return tile[0:1, :] + tile[1:2, :] + tile[2:3, :]


def summarize(plane, k_ref, v_ref, d_ref, *rest):
    outs, (held,) = rest[:-1], rest[-1:]
    heads = d_ref.shape[1]
    part = HD // plane
    mine = lax.rem(lax.axis_index("ctx"), plane)
    sums, _ = decay_sums(d_ref[...])
    rows = sums.shape[0]
    for head in range(heads):
        columns = pl.ds(head * HD, HD)
        column = sums[:, head : head + 1]
        last = column[rows - 1 : rows, :]
        carried = (k_ref[:, columns].astype(F32) * jnp.exp(last - column)).astype(BF16)
        held[head] = dot(carried, v_ref[:, columns], ((0,), (0,)))
        total = jnp.broadcast_to(last, (1, HD))
        for s, out in enumerate(outs):
            slot = jnp.bitwise_xor(mine, s)
            piece = held[head, pl.ds(pl.multiple_of(slot * part, part), part), :]
            out[head, pl.ds(0, part), :] = piece.astype(BF16)
            write_total(out, head, part, total)


def plane_total(plane, *refs):
    ins, out = refs[:plane], refs[plane]
    heads, part = out.shape[0], out.shape[1] - PAD
    mine = lax.rem(lax.axis_index("ctx"), plane)
    place = [jnp.bitwise_xor(mine, s) for s in range(plane)]
    for head in range(heads):
        totals = [read_total(ref, head, part) for ref in ins]
        sum_now = jnp.zeros((part, HD), F32)
        for s in range(plane):
            later = jnp.zeros((1, HD), F32)
            for t in range(plane):
                later = later + jnp.where(place[t] > place[s], totals[t], 0.0)
            sum_now = sum_now + jnp.exp(later) * ins[s][head, pl.ds(0, part), :].astype(F32)
        out[head, pl.ds(0, part), :] = sum_now.astype(BF16)
        write_total(out, head, part, functools.reduce(jnp.add, totals))


def priors(plane, far, *refs):
    ins, planes, outs = refs[:plane], refs[plane : plane + far], refs[plane + far :]
    heads, part = outs[0].shape[0], outs[0].shape[1]
    mine = lax.rem(lax.axis_index("ctx"), plane)
    place = [jnp.bitwise_xor(mine, s) for s in range(plane)]
    for head in range(heads):
        totals = [read_total(ref, head, part) for ref in ins]
        entering = jnp.zeros((part, HD), F32)
        between = jnp.zeros((1, HD), F32)
        for ref in planes:
            entering = entering + jnp.exp(between) * ref[head, pl.ds(0, part), :].astype(F32)
            between = between + read_total(ref, head, part)
        blocks = [ref[head, pl.ds(0, part), :].astype(F32) for ref in ins]
        for r, out in enumerate(outs):
            before = jnp.zeros((1, HD), F32)
            for t in range(plane):
                before = before + jnp.where(place[t] < place[r], totals[t], 0.0)
            state = jnp.exp(before) * entering
            for s in range(plane):
                if s == r:
                    continue
                gap = jnp.zeros((1, HD), F32)
                for t in range(plane):
                    inside = jnp.logical_and(place[t] > place[s], place[t] < place[r])
                    gap = gap + jnp.where(inside, totals[t], 0.0)
                state = state + jnp.where(place[s] < place[r], jnp.exp(gap), 0.0) * blocks[s]
            out[head] = state.astype(BF16)


def retain_inside(q_ref, k_ref, v_ref, d_ref, inside_ref, factor_ref):
    heads = d_ref.shape[1]
    sums, below = decay_sums(d_ref[...])
    rows = sums.shape[0]
    same = lax.broadcasted_iota(jnp.int32, (rows, rows), 0) == lax.broadcasted_iota(
        jnp.int32, (rows, rows), 1
    )
    factor_ref[...] = jnp.exp(sums)
    for head in range(heads):
        columns = pl.ds(head * HD, HD)
        column = jnp.broadcast_to(sums[:, head : head + 1], (rows, rows))
        across = jnp.sum(jnp.where(same, column, 0.0), axis=0, keepdims=True)
        spread = jnp.exp(jnp.minimum(column - across, 0.0))
        scores = dot(q_ref[:, columns], k_ref[:, columns], ((1,), (1,)))
        weights = jnp.where(below, spread * scores, 0.0).astype(BF16)
        inside_ref[:, columns] = dot(weights, v_ref[:, columns], ((1,), (0,)))


def retain_finish(plane, q_ref, gate_ref, inside_ref, factor_ref, *refs):
    states, out, held = refs[:plane], refs[plane], refs[plane + 1]
    heads = factor_ref.shape[1]
    part = HD // plane
    mine = lax.rem(lax.axis_index("ctx"), plane)
    for head in range(heads):
        columns = pl.ds(head * HD, HD)
        for s, ref in enumerate(states):
            slot = jnp.bitwise_xor(mine, s)
            held[head, pl.ds(pl.multiple_of(slot * part, part), part), :] = ref[head]
        before = dot(q_ref[:, columns], held[head], ((1,), (0,)))
        retained = inside_ref[:, columns] + factor_ref[:, head : head + 1] * before
        scale = lax.rsqrt(jnp.mean(retained * retained, axis=1, keepdims=True) + EPS)
        gate = gate_ref[:, columns].astype(F32)
        silu = gate / (1.0 + jnp.exp(-gate))
        out[:, columns] = (retained * scale * silu).astype(BF16)


def attend(plane, far, n, *refs):
    queries = refs[:plane]
    pieces = refs[plane : plane + far * n]
    outs = refs[plane + far * n : 2 * plane + far * n]
    keys, values = refs[2 * plane + far * n :]
    rows = queries[0].shape[0]
    heads = queries[0].shape[1] // HD
    length, width = pieces[0].shape[1:]
    group = heads * HD // width
    total = far * n * length
    index = lax.axis_index("ctx")
    mine, depth = lax.rem(index, plane), lax.div(index, plane)
    here = lax.axis_index("head")
    for i, piece in enumerate(pieces):
        keys[pl.ds(i * length, length), :] = piece[0]
        values[pl.ds(i * length, length), :] = piece[1]
    column = lax.broadcasted_iota(jnp.int32, (1, total), 1)
    limit = jnp.zeros((1, total), jnp.int32)
    for i in range(far * n):
        s, e = divmod(i, n)
        inside = jnp.logical_and(column >= i * length, column < (i + 1) * length)
        if s == 0:
            first = mine * rows + lax.rem(here + n - e, n) * length - i * length
            at = column + first
        else:
            at = jnp.where(depth >= s, -1, plane * rows)
        limit = jnp.where(inside, at, limit)
    scale = 1.0 / (math.sqrt(HD) * math.log(2.0))
    row = lax.broadcasted_iota(jnp.int32, (rows, total), 0)
    lane = lax.broadcasted_iota(jnp.int32, (rows, LANES), 1)
    for r in range(plane):
        position = row + jnp.bitwise_xor(mine, r) * rows
        allowed = position >= limit
        stats = jnp.zeros((rows, LANES), F32)
        for head in range(heads):
            columns = pl.ds(head * HD, HD)
            shared = pl.ds((head // group) * HD, HD)
            scores = dot(queries[r][:, columns], keys[:, shared], ((1,), (1,))) * scale
            masked = jnp.where(allowed, scores, FAR)
            top = jnp.maximum(jnp.max(masked, axis=1, keepdims=True), NEAR)
            weights = jnp.exp2(masked - top)
            summed = jnp.sum(weights, axis=1, keepdims=True)
            mixed = dot(weights.astype(BF16), values[:, shared], ((1,), (0,)))
            some = summed > 0.0
            safe = jnp.where(some, summed, 1.0)
            outs[r][:, columns] = (mixed / safe).astype(BF16)
            level = jnp.where(some, top + jnp.log2(safe), FAR)
            for i, third in enumerate(thirds(level)):
                stats = jnp.where(lane == 3 * head + i, third, stats)
        outs[r][:, pl.ds(heads * HD, LANES)] = stats.astype(BF16)


def merge(plane, *refs):
    ins, out = refs[:plane], refs[plane]
    heads = out.shape[1] // HD
    stats = [ref[:, pl.ds(heads * HD, LANES)].astype(F32) for ref in ins]
    for head in range(heads):
        columns = pl.ds(head * HD, HD)
        levels = [
            tile[:, 3 * head : 3 * head + 1]
            + tile[:, 3 * head + 1 : 3 * head + 2]
            + tile[:, 3 * head + 2 : 3 * head + 3]
            for tile in stats
        ]
        top = functools.reduce(jnp.maximum, levels)
        weights = [jnp.exp2(level - top) for level in levels]
        summed = functools.reduce(jnp.add, weights)
        mixed = functools.reduce(
            jnp.add, [w * ref[:, columns].astype(F32) for w, ref in zip(weights, ins)]
        )
        out[:, columns] = (mixed / summed).astype(BF16)


def per_device(count, n, q_ret, k_ret, v_ret, gate_ret, log_decay, q_cross, cache_k, cache_v):
    plane = math.gcd(count, 4)
    far = count // plane
    rows, wide = q_cross.shape
    heads = wide // HD
    length, width = cache_k.shape[0], cache_k.shape[1] // n
    part = HD // plane

    def in_plane(value, s):
        return lax.ppermute(value, "ctx", [(b, b ^ s) for b in range(count)])

    def onward(value, s):
        return lax.ppermute(value, "ctx", [(b, b + s * plane) for b in range(count - s * plane)])

    def to_head(value, s, e):
        table = [
            (b * n + y, (b + s * plane) * n + (y + e) % n)
            for b in range(count - s * plane)
            for y in range(n)
        ]
        return lax.ppermute(value, ("ctx", "head"), table)

    pieces = call(
        functools.partial(split_cache, n),
        [shape((2, length, width))] * n,
        (cache_k, cache_v),
        name="split_cache",
    )
    if n == 1:
        pieces = (pieces,)
    arrived = []
    for s in range(far):
        for e in range(n):
            arrived.append(pieces[e] if s == 0 and e == 0 else to_head(pieces[e], s, e))
    queries = [q_cross] + [in_plane(q_cross, s) for s in range(1, plane)]

    message = shape((heads, part + PAD, HD))
    sent = call(
        functools.partial(summarize, plane),
        [message] * plane,
        (k_ret, v_ret, log_decay),
        scratch=[pltpu.VMEM((heads, HD, HD), F32)],
        flops=2 * rows * HD * HD * heads,
        name="summarize",
    )
    slices = [sent[0]] + [in_plane(sent[s], s) for s in range(1, plane)]

    inside, factor = call(
        retain_inside,
        [shape((rows, wide), F32), shape((rows, heads), F32)],
        (q_ret, k_ret, v_ret, log_decay),
        flops=4 * rows * rows * HD * heads,
        name="retain_inside",
    )
    whole = call(functools.partial(plane_total, plane), [message], slices, name="plane_total")
    planes = [onward(whole, s) for s in range(1, far)]
    given = call(
        functools.partial(priors, plane, len(planes)),
        [shape((heads, part, HD))] * plane,
        (*slices, *planes),
        name="priors",
    )
    states = [given[0]] + [in_plane(given[s], s) for s in range(1, plane)]

    partial_outs = call(
        functools.partial(attend, plane, far, n),
        [shape((rows, wide + LANES))] * plane,
        (*queries, *arrived),
        scratch=[pltpu.VMEM((far * n * length, width), BF16) for _ in range(2)],
        flops=4 * rows * plane * heads * far * n * length * HD,
        name="attend",
    )
    returned = [partial_outs[0]] + [in_plane(partial_outs[s], s) for s in range(1, plane)]

    o_ret = call(
        functools.partial(retain_finish, plane),
        [shape((rows, wide))],
        (q_ret, gate_ret, inside, factor, *states),
        scratch=[pltpu.VMEM((heads, HD, HD), BF16)],
        flops=2 * rows * HD * HD * heads,
        name="retain_finish",
    )
    o_cross = call(functools.partial(merge, plane), [shape((rows, wide))], returned, name="merge")
    return o_ret, o_cross


def solution(mesh):
    split = P("ctx", "head")
    rows = P(("ctx", "head"), None)
    return jax.shard_map(
        functools.partial(per_device, mesh.shape["ctx"], mesh.shape["head"]),
        mesh=mesh,
        in_specs=(split,) * 6 + (rows,) * 2,
        out_specs=(split, split),
        check_vma=False,
    )
```

```python
import functools
import math

import jax
import jax.numpy as jnp
from jax import lax
from jax.experimental import pallas as pl
from jax.experimental.pallas import tpu as pltpu
from jax.sharding import PartitionSpec as P

HD = 256
FAR = -1e30
NEAR = -1e29
EPS = 1e-06
F32 = jnp.float32
BF16 = jnp.bfloat16
PAD = 16
LANES = 128
VMEM = pl.BlockSpec(memory_space=pltpu.VMEM)


def call(body, outs, args, scratch=(), flops=1_000_000, name=None):
    moved = sum(math.prod(a.shape) * a.dtype.itemsize for a in (*args, *outs))
    single = len(outs) == 1
    return pl.pallas_call(
        body,
        out_shape=outs[0] if single else tuple(outs),
        in_specs=[VMEM] * len(args),
        out_specs=VMEM if single else tuple(VMEM for _ in outs),
        scratch_shapes=scratch,
        compiler_params=pltpu.CompilerParams(vmem_limit_bytes=40 * 1024 * 1024),
        cost_estimate=pl.CostEstimate(flops=flops, bytes_accessed=moved, transcendentals=0),
        name=name,
    )(*args)


def shape(dims, dtype=BF16):
    return jax.ShapeDtypeStruct(dims, dtype)


def dot(a, b, contract, precision=None):
    return lax.dot_general(
        a, b, (contract, ((), ())), preferred_element_type=F32, precision=precision
    )


def thirds(value):
    high = value.astype(BF16).astype(F32)
    rest = value - high
    middle = rest.astype(BF16).astype(F32)
    return high, middle, rest - middle


def decay_sums(log_decay):
    rows = log_decay.shape[0]
    below = lax.broadcasted_iota(jnp.int32, (rows, rows), 0) >= lax.broadcasted_iota(
        jnp.int32, (rows, rows), 1
    )
    lower = jnp.where(below, 1.0, 0.0).astype(F32)
    return dot(lower, log_decay, ((1,), (0,)), lax.Precision.HIGHEST), below


def split_cache(n, k_ref, v_ref, *pieces):
    width = k_ref.shape[1] // n
    here = lax.axis_index("head")
    for e, piece in enumerate(pieces):
        target = lax.rem(here + e, n)
        columns = pl.ds(pl.multiple_of(target * width, LANES), width)
        piece[:, pl.ds(0, width)] = k_ref[:, columns]
        piece[:, pl.ds(width, width)] = v_ref[:, columns]


def join_rows(n, *refs):
    pieces, out = refs[:n], refs[n]
    length = pieces[0].shape[0]
    here = lax.axis_index("head")
    for e, piece in enumerate(pieces):
        place = lax.rem(here + n - e, n)
        out[pl.ds(pl.multiple_of(place * length, PAD), length), :] = piece[...]


def bits():
    index = lax.axis_index("ctx")
    low = lax.rem(index, 2)
    return low, lax.rem(lax.div(index, 2), 2), lax.div(index, 4)


def put_total(out, at, total):
    wide = out.shape[1]
    if out.dtype == F32:
        out[pl.ds(at, PAD), :] = jnp.broadcast_to(total, (PAD, wide))
        return
    row = lax.broadcasted_iota(jnp.int32, (PAD, wide), 0)
    high, middle, low = thirds(total)
    tile = jnp.where(row == 0, high, jnp.where(row == 1, middle, jnp.where(row == 2, low, 0.0)))
    out[pl.ds(at, PAD), :] = tile.astype(out.dtype)


def total_of(ref):
    tile = ref[pl.ds(ref.shape[0] - PAD, PAD), :].astype(F32)
    if ref.dtype == F32:
        return tile[0:1, :]
    return tile[0:1, :] + tile[1:2, :] + tile[2:3, :]


def state_of(ref):
    return ref[pl.ds(0, ref.shape[0] - PAD), :].astype(F32)


def part_of(held, which, rows):
    return held[pl.ds(pl.multiple_of(which * rows, rows), rows), :]


def summarize(k_ref, v_ref, d_ref, send, keep, held):
    low, _, _ = bits()
    half = HD // 2
    sums, _ = decay_sums(d_ref[...])
    rows = sums.shape[0]
    totals = []
    for head in range(d_ref.shape[1]):
        columns = pl.ds(head * HD, HD)
        column = sums[:, head : head + 1]
        last = column[rows - 1 : rows, :]
        carried = (k_ref[:, columns].astype(F32) * jnp.exp(last - column)).astype(BF16)
        held[:, columns] = dot(carried, v_ref[:, columns], ((0,), (0,)))
        totals.append(jnp.broadcast_to(last, (1, HD)))
    total = jnp.concatenate(totals, axis=1)
    for out, which in ((send, 1 - low), (keep, low)):
        out[pl.ds(0, half), :] = part_of(held, which, half).astype(out.dtype)
        put_total(out, half, total)


def pair_total(first, keep_ref, other_ref):
    kept, other = state_of(keep_ref), state_of(other_ref)
    kept_total, other_total = total_of(keep_ref), total_of(other_ref)
    late = jnp.where(first, other_total, kept_total)
    earlier, later = jnp.where(first, kept, other), jnp.where(first, other, kept)
    return jnp.exp(late) * earlier + later, kept_total + other_total


def chip_total(keep_ref, other_ref, send, keep, held):
    low, high, _ = bits()
    quarter = HD // 4
    held[...], total = pair_total(low == 0, keep_ref, other_ref)
    for out, which in ((send, 1 - high), (keep, high)):
        out[pl.ds(0, quarter), :] = part_of(held, which, quarter).astype(out.dtype)
        put_total(out, quarter, total)


def plane_total(keep_ref, other_ref, out):
    _, high, _ = bits()
    state, total = pair_total(high == 0, keep_ref, other_ref)
    out[pl.ds(0, state.shape[0]), :] = state.astype(out.dtype)
    put_total(out, state.shape[0], total)


def chip_priors(keep_ref, other_ref, *refs):
    planes, send, keep = refs[:-2], refs[-2], refs[-1]
    _, high, _ = bits()
    entering = jnp.zeros(send.shape, F32)
    between = jnp.zeros((1, send.shape[1]), F32)
    for ref in planes:
        entering = entering + jnp.exp(between) * state_of(ref)
        between = between + total_of(ref)
    first = high == 0
    early = jnp.where(first, state_of(keep_ref), state_of(other_ref))
    early_total = jnp.where(first, total_of(keep_ref), total_of(other_ref))
    second = jnp.exp(early_total) * entering + early
    send[...] = jnp.where(first, second, entering).astype(send.dtype)
    keep[...] = jnp.where(first, entering, second).astype(keep.dtype)


def block_priors(keep_ref, other_ref, prior_ref, prior_other_ref, send, keep, held):
    low, high, _ = bits()
    quarter = prior_ref.shape[0]
    for ref, which in ((prior_ref, high), (prior_other_ref, 1 - high)):
        held[pl.ds(pl.multiple_of(which * quarter, quarter), quarter), :] = ref[...].astype(F32)
    first = low == 0
    early = jnp.where(first, state_of(keep_ref), state_of(other_ref))
    early_total = jnp.where(first, total_of(keep_ref), total_of(other_ref))
    entering = held[...]
    second = jnp.exp(early_total) * entering + early
    send[...] = jnp.where(first, second, entering).astype(send.dtype)
    keep[...] = jnp.where(first, entering, second).astype(keep.dtype)


def retain_inside(q_ref, k_ref, v_ref, d_ref, inside_ref, factor_ref):
    heads = d_ref.shape[1]
    sums, below = decay_sums(d_ref[...])
    rows = sums.shape[0]
    same = lax.broadcasted_iota(jnp.int32, (rows, rows), 0) == lax.broadcasted_iota(
        jnp.int32, (rows, rows), 1
    )
    factor_ref[...] = jnp.exp(sums)
    for head in range(heads):
        columns = pl.ds(head * HD, HD)
        column = jnp.broadcast_to(sums[:, head : head + 1], (rows, rows))
        across = jnp.sum(jnp.where(same, column, 0.0), axis=0, keepdims=True)
        spread = jnp.exp(jnp.minimum(column - across, 0.0))
        scores = dot(q_ref[:, columns], k_ref[:, columns], ((1,), (1,)))
        weights = jnp.where(below, spread * scores, 0.0).astype(BF16)
        inside_ref[:, columns] = dot(weights, v_ref[:, columns], ((1,), (0,)))


def retain_finish(q_ref, gate_ref, inside_ref, factor_ref, keep_ref, other_ref, out, held):
    low, _, _ = bits()
    half = keep_ref.shape[0]
    for ref, which in ((keep_ref, low), (other_ref, 1 - low)):
        held[pl.ds(pl.multiple_of(which * half, half), half), :] = ref[...]
    for head in range(factor_ref.shape[1]):
        columns = pl.ds(head * HD, HD)
        before = dot(q_ref[:, columns], held[:, columns], ((1,), (0,)))
        retained = inside_ref[:, columns] + factor_ref[:, head : head + 1] * before
        scale = lax.rsqrt(jnp.mean(retained * retained, axis=1, keepdims=True) + EPS)
        gate = gate_ref[:, columns].astype(F32)
        silu = gate / (1.0 + jnp.exp(-gate))
        out[:, columns] = (retained * scale * silu).astype(BF16)


def attend(far, q_ref, q_other_ref, *refs):
    blocks, (send, keep, keys, values) = refs[: 2 * far], refs[2 * far :]
    rows, wide = q_ref.shape
    heads = wide // HD
    length, width = blocks[0].shape[0], blocks[0].shape[1] // 2
    group = wide // width
    total = 2 * far * length
    low, high, depth = bits()
    for i, block in enumerate(blocks):
        keys[pl.ds(i * length, length), :] = block[:, pl.ds(0, width)]
        values[pl.ds(i * length, length), :] = block[:, pl.ds(width, width)]
    column = lax.broadcasted_iota(jnp.int32, (1, total), 1)
    limit = jnp.zeros((1, total), jnp.int32)
    for i in range(2 * far):
        s, t = divmod(i, 2)
        if s == 0:
            core = low if t == 0 else 1 - low
            at = column + ((2 * high + core) * length - i * length)
        else:
            at = jnp.where(depth >= s, -1, 4 * rows)
        limit = jnp.where(column >= i * length, at, limit)
    scale = 1.0 / (math.sqrt(HD) * math.log(2.0))
    row = lax.broadcasted_iota(jnp.int32, (rows, total), 0)
    lane = lax.broadcasted_iota(jnp.int32, (rows, LANES), 1)
    for query, out, place in ((q_other_ref, send, 1 - high), (q_ref, keep, high)):
        allowed = row + (2 * place + low) * rows >= limit
        stats = jnp.zeros((rows, LANES), F32)
        for head in range(heads):
            columns = pl.ds(head * HD, HD)
            shared = pl.ds((head // group) * HD, HD)
            scores = dot(query[:, columns], keys[:, shared], ((1,), (1,))) * scale
            masked = jnp.where(allowed, scores, FAR)
            top = jnp.maximum(jnp.max(masked, axis=1, keepdims=True), NEAR)
            weights = jnp.exp2(masked - top)
            summed = jnp.sum(weights, axis=1, keepdims=True)
            mixed = dot(weights.astype(BF16), values[:, shared], ((1,), (0,)))
            some = summed > 0.0
            safe = jnp.where(some, summed, 1.0)
            out[:, columns] = (mixed / safe).astype(out.dtype)
            level = jnp.where(some, top + jnp.log2(safe), FAR)
            for i, third in enumerate(thirds(level)):
                stats = jnp.where(lane == 3 * head + i, third, stats)
        out[:, pl.ds(wide, LANES)] = stats.astype(out.dtype)


def merge(keep_ref, other_ref, out):
    wide = out.shape[1]
    ins = (keep_ref, other_ref)
    stats = [ref[:, pl.ds(wide, LANES)].astype(F32) for ref in ins]
    for head in range(wide // HD):
        columns = pl.ds(head * HD, HD)
        levels = [
            tile[:, 3 * head : 3 * head + 1]
            + tile[:, 3 * head + 1 : 3 * head + 2]
            + tile[:, 3 * head + 2 : 3 * head + 3]
            for tile in stats
        ]
        top = functools.reduce(jnp.maximum, levels)
        weights = [jnp.exp2(level - top) for level in levels]
        share = 1.0 / functools.reduce(jnp.add, weights)
        mixed = functools.reduce(
            jnp.add, [(w * share) * ref[:, columns].astype(F32) for w, ref in zip(weights, ins)]
        )
        out[:, columns] = mixed.astype(BF16)


def per_device(count, n, q_ret, k_ret, v_ret, gate_ret, log_decay, q_cross, cache_k, cache_v):
    far = count // 4
    rows, wide = q_cross.shape
    heads = wide // HD
    length, width = cache_k.shape[0], cache_k.shape[1] // n
    half, quarter = HD // 2, HD // 4

    def swap(value, bit):
        return lax.ppermute(value, "ctx", [(b, b ^ bit) for b in range(count)])

    def onward(value, s):
        return lax.ppermute(value, "ctx", [(b, b + s * 4) for b in range(count - s * 4)])

    def to_head(value, e):
        return lax.ppermute(value, "head", [(y, (y + e) % n) for y in range(n)])

    pieces = call(
        functools.partial(split_cache, n),
        [shape((length, 2 * width))] * n,
        (cache_k, cache_v),
        name="split_cache",
    )
    arrived = [pieces[0]] + [to_head(pieces[e], e) for e in range(1, n)]
    sum_send, sum_keep = call(
        summarize,
        [shape((half + PAD, wide)), shape((half + PAD, wide), F32)],
        (k_ret, v_ret, log_decay),
        scratch=[pltpu.VMEM((HD, wide), F32)],
        flops=2 * rows * HD * HD * heads,
        name="summarize",
    )
    sum_other = swap(sum_send, 1)
    block = call(
        functools.partial(join_rows, n), [shape((n * length, 2 * width))], arrived, name="join_rows"
    )
    blocks = [block] + [onward(block, s) for s in range(1, far)]
    chip_send, chip_keep = call(
        chip_total,
        [shape((quarter + PAD, wide)), shape((quarter + PAD, wide), F32)],
        (sum_keep, sum_other),
        scratch=[pltpu.VMEM((half, wide), F32)],
        name="chip_total",
    )
    chip_other = swap(chip_send, 2)
    q_other = swap(q_cross, 2)
    whole = call(plane_total, [shape((quarter + PAD, wide))], (chip_keep, chip_other), name="plane_total")
    planes = [onward(whole, s) for s in range(1, far)]
    inside, factor = call(
        retain_inside,
        [shape((rows, wide), F32), shape((rows, heads), F32)],
        (q_ret, k_ret, v_ret, log_decay),
        flops=4 * rows * rows * HD * heads,
        name="retain_inside",
    )
    both = []
    for one in blocks:
        both += [one, swap(one, 1)]
    part_send, part_keep = call(
        functools.partial(attend, far),
        [shape((rows, wide + LANES)), shape((rows, wide + LANES), F32)],
        (q_cross, q_other, *both),
        scratch=[pltpu.VMEM((2 * far * n * length, width), BF16) for _ in range(2)],
        flops=8 * rows * heads * 2 * far * n * length * HD,
        name="attend",
    )
    part_other = swap(part_send, 2)
    prior_send, prior_keep = call(
        chip_priors,
        [shape((quarter, wide)), shape((quarter, wide), F32)],
        (chip_keep, chip_other, *planes),
        name="chip_priors",
    )
    prior_other = swap(prior_send, 2)
    state_send, state_keep = call(
        block_priors,
        [shape((half, wide)), shape((half, wide))],
        (sum_keep, sum_other, prior_keep, prior_other),
        scratch=[pltpu.VMEM((half, wide), F32)],
        name="block_priors",
    )
    state_other = swap(state_send, 1)
    o_ret = call(
        retain_finish,
        [shape((rows, wide))],
        (q_ret, gate_ret, inside, factor, state_keep, state_other),
        scratch=[pltpu.VMEM((HD, wide), BF16)],
        flops=2 * rows * HD * HD * heads,
        name="retain_finish",
    )
    o_cross = call(merge, [shape((rows, wide))], (part_keep, part_other), name="merge")
    return o_ret, o_cross


def solution(mesh):
    split = P("ctx", "head")
    rows = P(("ctx", "head"), None)
    return jax.shard_map(
        functools.partial(per_device, mesh.shape["ctx"], mesh.shape["head"]),
        mesh=mesh,
        in_specs=(split,) * 6 + (rows,) * 2,
        out_specs=(split, split),
        check_vma=False,
    )
```

```python
import functools
import math

import jax
import jax.numpy as jnp
from jax import lax
from jax.experimental import pallas as pl
from jax.experimental.pallas import tpu as pltpu
from jax.sharding import PartitionSpec as P

HD = 256
FAR = -1e30
NEAR = -1e29
EPS = 1e-06
F32 = jnp.float32
BF16 = jnp.bfloat16
PAD = 16
LANES = 128
VMEM = pl.BlockSpec(memory_space=pltpu.VMEM)
ANY = pl.BlockSpec(memory_space=pl.ANY)
HBM = pl.BlockSpec(memory_space=pltpu.HBM)


def call(
    body, outs, args, scratch=(), name=None, takes=VMEM, gives=VMEM, after=(),
    aliases=None,
):
    single = len(outs) == 1
    used, total = len(args), len(args) + len(after)

    def kernel(*refs):
        body(*refs[:used], *refs[total:])

    return pl.pallas_call(
        kernel,
        out_shape=outs[0] if single else tuple(outs),
        in_specs=(takes if isinstance(takes, list) else [takes] * used) + [ANY] * len(after),
        out_specs=gives if single or isinstance(gives, tuple) else tuple(gives for _ in outs),
        scratch_shapes=scratch,
        input_output_aliases=aliases or {},
        compiler_params=pltpu.CompilerParams(vmem_limit_bytes=40 * 1024 * 1024),
        cost_estimate=pl.CostEstimate(flops=1000, bytes_accessed=1000, transcendentals=0),
        name=name,
    )(*args, *after)


def shape(dims, dtype=BF16):
    return jax.ShapeDtypeStruct(dims, dtype)


def dot(a, b, contract, precision=None):
    return lax.dot_general(
        a, b, (contract, ((), ())), preferred_element_type=F32, precision=precision
    )


def thirds(value):
    high = value.astype(BF16).astype(F32)
    rest = value - high
    middle = rest.astype(BF16).astype(F32)
    return high, middle, rest - middle


def lower_ones(rows):
    below = lax.broadcasted_iota(jnp.int32, (rows, rows), 0) >= lax.broadcasted_iota(
        jnp.int32, (rows, rows), 1
    )
    return below, jnp.where(below, 1.0, 0.0).astype(F32)


def load_all(n, count, *refs):
    k_ref, v_ref, *plain = refs[:count]
    outs, sems = refs[count:-1], refs[-1]
    pieces, copies = outs[:n], outs[n:]
    width = k_ref.shape[1] // n
    here = lax.axis_index("head")
    moves = []
    for e, piece in enumerate(pieces):
        target = lax.rem(here + e, n)
        columns = pl.ds(pl.multiple_of(target * width, LANES), width)
        moves.append((k_ref.at[:, columns], piece.at[:, pl.ds(0, width)]))
        moves.append((v_ref.at[:, columns], piece.at[:, pl.ds(width, width)]))
    moves += list(zip(plain, copies))
    running = [pltpu.make_async_copy(a, b, sems.at[i]) for i, (a, b) in enumerate(moves)]
    for one in running:
        one.start()
    for one in running:
        one.wait()


def join_rows(n, *refs):
    pieces, out = refs[:n], refs[n]
    length = pieces[0].shape[0]
    here = lax.axis_index("head")
    for e, piece in enumerate(pieces):
        place = lax.rem(here + n - e, n)
        out[pl.ds(pl.multiple_of(place * length, PAD), length), :] = piece[...]


def bits():
    index = lax.axis_index("ctx")
    low = lax.rem(index, 2)
    return low, lax.rem(lax.div(index, 2), 2), lax.div(index, 4)


def put_total(out, at, total):
    wide = out.shape[1]
    if out.dtype == F32:
        out[pl.ds(at, PAD), :] = jnp.broadcast_to(total, (PAD, wide))
        return
    row = lax.broadcasted_iota(jnp.int32, (PAD, wide), 0)
    high, middle, low = thirds(total)
    tile = jnp.where(row == 0, high, jnp.where(row == 1, middle, jnp.where(row == 2, low, 0.0)))
    out[pl.ds(at, PAD), :] = tile.astype(out.dtype)


def total_of(ref):
    tile = ref[pl.ds(ref.shape[0] - PAD, PAD), :].astype(F32)
    if ref.dtype == F32:
        return tile[0:1, :]
    return tile[0:1, :] + tile[1:2, :] + tile[2:3, :]


def state_of(ref):
    return ref[pl.ds(0, ref.shape[0] - PAD), :].astype(F32)


def part_of(held, which, rows):
    return held[pl.ds(pl.multiple_of(which * rows, rows), rows), :]


def summarize(k_ref, v_ref, d_ref, send, keep, held):
    low, _, _ = bits()
    half = HD // 2
    rows = d_ref.shape[1]
    sums = dot(lower_ones(rows)[1], d_ref[...], ((1,), (1,)), lax.Precision.HIGHEST)
    totals = []
    for head in range(d_ref.shape[0]):
        columns = pl.ds(head * HD, HD)
        column = sums[:, head : head + 1]
        last = column[rows - 1 : rows, :]
        carried = (k_ref[:, columns].astype(F32) * jnp.exp(last - column)).astype(BF16)
        held[:, columns] = dot(carried, v_ref[:, columns], ((0,), (0,)))
        totals.append(jnp.broadcast_to(last, (1, HD)))
    total = jnp.concatenate(totals, axis=1)
    for out, which in ((send, 1 - low), (keep, low)):
        out[pl.ds(0, half), :] = part_of(held, which, half).astype(out.dtype)
        put_total(out, half, total)


def pair_total(first, keep_ref, other_ref):
    kept, other = state_of(keep_ref), state_of(other_ref)
    kept_total, other_total = total_of(keep_ref), total_of(other_ref)
    late = jnp.where(first, other_total, kept_total)
    earlier, later = jnp.where(first, kept, other), jnp.where(first, other, kept)
    return jnp.exp(late) * earlier + later, kept_total + other_total


def chip_total(keep_ref, other_ref, send, keep, held):
    low, high, _ = bits()
    quarter = HD // 4
    held[...], total = pair_total(low == 0, keep_ref, other_ref)
    for out, which in ((send, 1 - high), (keep, high)):
        out[pl.ds(0, quarter), :] = part_of(held, which, quarter).astype(out.dtype)
        put_total(out, quarter, total)


def plane_total(keep_ref, other_ref, out):
    _, high, _ = bits()
    state, total = pair_total(high == 0, keep_ref, other_ref)
    out[pl.ds(0, state.shape[0]), :] = state.astype(out.dtype)
    put_total(out, state.shape[0], total)


def chip_priors(keep_ref, other_ref, *refs):
    planes, send, keep = refs[:-2], refs[-2], refs[-1]
    _, high, _ = bits()
    entering = jnp.zeros(send.shape, F32)
    between = jnp.zeros((1, send.shape[1]), F32)
    for ref in planes:
        entering = entering + jnp.exp(between) * state_of(ref)
        between = between + total_of(ref)
    first = high == 0
    early = jnp.where(first, state_of(keep_ref), state_of(other_ref))
    early_total = jnp.where(first, total_of(keep_ref), total_of(other_ref))
    second = jnp.exp(early_total) * entering + early
    send[...] = jnp.where(first, second, entering).astype(send.dtype)
    keep[...] = jnp.where(first, entering, second).astype(keep.dtype)


def block_priors(keep_ref, other_ref, prior_ref, prior_other_ref, send, keep, held):
    low, high, _ = bits()
    quarter = prior_ref.shape[0]
    for ref, which in ((prior_ref, high), (prior_other_ref, 1 - high)):
        held[pl.ds(pl.multiple_of(which * quarter, quarter), quarter), :] = ref[...].astype(F32)
    first = low == 0
    early = jnp.where(first, state_of(keep_ref), state_of(other_ref))
    early_total = jnp.where(first, total_of(keep_ref), total_of(other_ref))
    entering = held[...]
    second = jnp.exp(early_total) * entering + early
    send[...] = jnp.where(first, second, entering).astype(send.dtype)
    keep[...] = jnp.where(first, entering, second).astype(keep.dtype)


def grow(own_ref, earlier_ref, _, out, __):
    rows = out.shape[0] - PAD
    own, earlier = total_of(own_ref), total_of(earlier_ref)
    state = jnp.exp(own) * state_of(earlier_ref) + state_of(own_ref)
    out[pl.ds(0, rows), :] = state.astype(out.dtype)
    put_total(out, rows, own + earlier)


def retain_inside(q_ref, k_ref, v_ref, d_ref, inside_ref, factor_ref):
    heads, rows = d_ref.shape
    below, ones = lower_ones(rows)
    sums = dot(ones, d_ref[...], ((1,), (1,)), lax.Precision.HIGHEST)
    same = lax.broadcasted_iota(jnp.int32, (rows, rows), 0) == lax.broadcasted_iota(
        jnp.int32, (rows, rows), 1
    )
    factor_ref[...] = jnp.exp(sums)
    for head in range(heads):
        columns = pl.ds(head * HD, HD)
        column = jnp.broadcast_to(sums[:, head : head + 1], (rows, rows))
        across = jnp.sum(jnp.where(same, column, 0.0), axis=0, keepdims=True)
        spread = jnp.exp(jnp.minimum(column - across, 0.0))
        scores = dot(q_ref[:, columns], k_ref[:, columns], ((1,), (1,)))
        weights = jnp.where(below, spread * scores, 0.0).astype(BF16)
        inside_ref[:, columns] = dot(weights, v_ref[:, columns], ((1,), (0,)))


def finish(
    part_ref, part_other_ref, q_ref, gate_ref, inside_ref, factor_ref, keep_ref, other_ref,
    o_ret, o_cross, held, ret_held, cross_held, sems,
):
    merge(part_ref, part_other_ref, cross_held)
    cross_out = pltpu.make_async_copy(cross_held, o_cross, sems.at[0])
    cross_out.start()
    low, _, _ = bits()
    half = keep_ref.shape[0]
    for ref, which in ((keep_ref, low), (other_ref, 1 - low)):
        held[pl.ds(pl.multiple_of(which * half, half), half), :] = ref[...]
    for head in range(factor_ref.shape[1]):
        columns = pl.ds(head * HD, HD)
        before = dot(q_ref[:, columns], held[:, columns], ((1,), (0,)))
        retained = inside_ref[:, columns] + factor_ref[:, head : head + 1] * before
        scale = lax.rsqrt(jnp.mean(retained * retained, axis=1, keepdims=True) + EPS)
        gate = gate_ref[:, columns].astype(F32)
        silu = gate / (1.0 + jnp.exp(-gate))
        ret_held[:, columns] = (retained * scale * silu).astype(BF16)
    ret_out = pltpu.make_async_copy(ret_held, o_ret, sems.at[1])
    ret_out.start()
    cross_out.wait()
    ret_out.wait()


def attend(first, count, q_ref, q_other_ref, *refs):
    blocks, refs = refs[: 2 * count], refs[2 * count :]
    last = first > 0
    carried, refs = (refs[:4], refs[4:]) if last else ((), refs)
    outs, (keys, values) = refs[:-2], refs[-2:]
    rows, wide = q_ref.shape
    heads = wide // HD
    length, width = blocks[0].shape[0], blocks[0].shape[1] // 2
    group = wide // width
    total = 2 * count * length
    low, high, depth = bits()
    for i, block in enumerate(blocks):
        keys[pl.ds(i * length, length), :] = block[:, pl.ds(0, width)]
        values[pl.ds(i * length, length), :] = block[:, pl.ds(width, width)]
    column = lax.broadcasted_iota(jnp.int32, (1, total), 1)
    limit = jnp.zeros((1, total), jnp.int32)
    for i in range(2 * count):
        s, t = divmod(i, 2)
        s = s + first
        if s == 0:
            core = low if t == 0 else 1 - low
            at = column + ((2 * high + core) * length - i * length)
        else:
            at = jnp.where(depth >= s, -1, 4 * rows)
        limit = jnp.where(column >= i * length, at, limit)
    scale = 1.0 / (math.sqrt(HD) * math.log(2.0))
    row = lax.broadcasted_iota(jnp.int32, (rows, total), 0)
    lane = lax.broadcasted_iota(jnp.int32, (rows, LANES), 1)
    for which, (query, place) in enumerate(((q_other_ref, 1 - high), (q_ref, high))):
        allowed = row + (2 * place + low) * rows >= limit
        stats = jnp.zeros((rows, LANES), F32)
        if last:
            mixed_ref, stats_ref = carried[2 * which : 2 * which + 2]
            out = outs[which]
        else:
            out, stats_out = outs[2 * which : 2 * which + 2]
        for head in range(heads):
            columns = pl.ds(head * HD, HD)
            shared = pl.ds((head // group) * HD, HD)
            scores = dot(query[:, columns], keys[:, shared], ((1,), (1,))) * scale
            masked = jnp.where(allowed, scores, FAR)
            top = jnp.maximum(jnp.max(masked, axis=1, keepdims=True), NEAR)
            if last:
                old = stats_ref[:, 2 * head : 2 * head + 1]
                top = jnp.maximum(top, old)
            weights = jnp.exp2(masked - top)
            summed = jnp.sum(weights, axis=1, keepdims=True)
            mixed = dot(weights.astype(BF16), values[:, shared], ((1,), (0,)))
            if not last:
                out[:, columns] = mixed
                stats = jnp.where(lane == 2 * head, top, stats)
                stats = jnp.where(lane == 2 * head + 1, summed, stats)
                continue
            shrink = jnp.exp2(old - top)
            summed = summed + shrink * stats_ref[:, 2 * head + 1 : 2 * head + 2]
            mixed = mixed + shrink * mixed_ref[:, columns]
            some = summed > 0.0
            safe = jnp.where(some, summed, 1.0)
            out[:, columns] = (mixed / safe).astype(out.dtype)
            level = jnp.where(some, top + jnp.log2(safe), FAR)
            for i, third in enumerate(thirds(level)):
                stats = jnp.where(lane == 3 * head + i, third, stats)
        if last:
            out[:, pl.ds(wide, LANES)] = stats.astype(out.dtype)
        else:
            stats_out[...] = stats


def merge(keep_ref, other_ref, out):
    wide = out.shape[1]
    ins = (keep_ref, other_ref)
    stats = [ref[:, pl.ds(wide, LANES)].astype(F32) for ref in ins]
    for head in range(wide // HD):
        columns = pl.ds(head * HD, HD)
        levels = [
            tile[:, 3 * head : 3 * head + 1]
            + tile[:, 3 * head + 1 : 3 * head + 2]
            + tile[:, 3 * head + 2 : 3 * head + 3]
            for tile in stats
        ]
        top = functools.reduce(jnp.maximum, levels)
        weights = [jnp.exp2(level - top) for level in levels]
        share = 1.0 / functools.reduce(jnp.add, weights)
        mixed = functools.reduce(
            jnp.add, [(w * share) * ref[:, columns].astype(F32) for w, ref in zip(weights, ins)]
        )
        out[:, columns] = mixed.astype(BF16)


def per_device(count, n, q_ret, k_ret, v_ret, gate_ret, log_decay, q_cross, cache_k, cache_v):
    far = count // 4
    rows, wide = q_cross.shape
    heads = wide // HD
    length, width = cache_k.shape[0], cache_k.shape[1] // n
    half, quarter = HD // 2, HD // 4

    def swap(value, bit):
        return lax.ppermute(value, "ctx", [(b, b ^ bit) for b in range(count)])

    def along(value, step, least):
        pairs = [(b, b + step * 4) for b in range(least * 4, count - step * 4)]
        return lax.ppermute(value, "ctx", pairs)

    def to_head(value, e):
        return lax.ppermute(value, "head", [(y, (y + e) % n) for y in range(n)])

    plain = (k_ret, v_ret, log_decay.T, q_ret, q_cross, gate_ret)
    loaded = call(
        functools.partial(load_all, n, 2 + len(plain)),
        [pltpu.VMEM((length, 2 * width), BF16)] * n + [pltpu.VMEM(a.shape, a.dtype) for a in plain],
        [pltpu.with_memory_space_constraint(a, pltpu.HBM) for a in (cache_k, cache_v, *plain)],
        scratch=[pltpu.SemaphoreType.DMA((2 * n + len(plain),))],
        name="load_all",
        takes=HBM,
    )
    pieces = loaded[:n]
    k_ret, v_ret, decays, q_ret, q_cross, gate_ret = loaded[n:]
    arrived = [pieces[0]] + [to_head(pieces[e], e) for e in range(1, n)]
    sum_send, sum_keep = call(
        summarize,
        [shape((half + PAD, wide)), shape((half + PAD, wide), F32)],
        (k_ret, v_ret, decays),
        scratch=[pltpu.VMEM((HD, wide), F32)],
        name="summarize",
    )
    sum_other = swap(sum_send, 1)
    chip_send, chip_keep = call(
        chip_total,
        [shape((quarter + PAD, wide)), shape((quarter + PAD, wide), F32)],
        (sum_keep, sum_other),
        scratch=[pltpu.VMEM((half, wide), F32)],
        name="chip_total",
        after=arrived[-1:],
    )
    inside, factor = call(
        retain_inside,
        [shape((rows, wide), F32), shape((rows, heads), F32)],
        (q_ret, k_ret, v_ret, decays),
        name="retain_inside",
        after=(chip_send,),
    )
    blocks = [
        call(
            functools.partial(join_rows, n),
            [shape((n * length, 2 * width))],
            arrived,
            name="join_rows",
        )
    ]
    for s in range(1, far - 1):
        blocks.append(along(blocks[-1], 1, s - 1))
    chip_other = swap(chip_send, 2)
    q_other = swap(q_cross, 2)
    window = call(
        plane_total,
        [shape((quarter + PAD, wide))],
        (chip_keep, chip_other),
        name="plane_total",
        after=(factor,),
    )
    def look(first, count, outs, carried, name):
        keys = 2 * count * n * length
        both = []
        for one in blocks[first : first + count]:
            both += [one, swap(one, 1)]
        return call(
            functools.partial(attend, first, count),
            outs,
            (q_cross, q_other, *both, *carried),
            scratch=[pltpu.VMEM((keys, width), BF16) for _ in range(2)],
            name=name,
        )

    near = max(far // 2, 1)
    so_far = look(
        0, near, [shape((rows, wide), F32), shape((rows, LANES), F32)] * 2, (), "attend_near"
    )
    planes, step = [], 1
    while step < far:
        planes.append(along(window, step, 0))
        step *= 2
        if step < far:
            window, blocks[-1] = call(
                grow,
                [shape(window.shape), shape(blocks[-1].shape)],
                (window, planes[-1], blocks[-1]),
                name="grow",
                takes=[VMEM, VMEM, ANY],
                gives=(VMEM, ANY),
                after=so_far[1:2],
                aliases={2: 1},
            )
    prior_send, prior_keep = call(
        chip_priors,
        [shape((quarter, wide)), shape((quarter, wide), F32)],
        (chip_keep, chip_other, *planes),
        name="chip_priors",
    )
    if far > 1:
        arriving = along(blocks[-1], 1, far - 2)
        blocks.append(
            call(
                lambda *refs: None,
                [shape(arriving.shape)],
                (arriving,),
                name="hold",
                takes=ANY,
                gives=ANY,
                after=(prior_send,),
                aliases={0: 0},
            )
        )
    part_send, part_keep = look(
        near,
        far - near,
        [shape((rows, wide + LANES)), shape((rows, wide + LANES), F32)],
        so_far,
        "attend_far",
    )
    part_other = swap(part_send, 2)
    prior_other = swap(prior_send, 2)
    state_send, state_keep = call(
        block_priors,
        [shape((half, wide)), shape((half, wide))],
        (sum_keep, sum_other, prior_keep, prior_other),
        scratch=[pltpu.VMEM((half, wide), F32)],
        name="block_priors",
    )
    state_other = swap(state_send, 1)
    held = pltpu.VMEM((rows, wide), BF16)
    return call(
        finish,
        [shape((rows, wide))] * 2,
        (part_keep, part_other, q_ret, gate_ret, inside, factor, state_keep, state_other),
        scratch=[pltpu.VMEM((HD, wide), BF16), held, held, pltpu.SemaphoreType.DMA((2,))],
        name="finish",
        gives=HBM,
    )


def solution(mesh):
    split = P("ctx", "head")
    rows = P(("ctx", "head"), None)
    return jax.shard_map(
        functools.partial(per_device, mesh.shape["ctx"], mesh.shape["head"]),
        mesh=mesh,
        in_specs=(split,) * 6 + (rows,) * 2,
        out_specs=(split, split),
        check_vma=False,
    )
```

```python
import functools
import math

import jax
import jax.numpy as jnp
from jax import lax
from jax.experimental import pallas as pl
from jax.experimental.pallas import tpu as pltpu
from jax.sharding import PartitionSpec as P

HD = 256
FAR = -1e30
NEAR = -1e29
EPS = 1e-06
F32 = jnp.float32
BF16 = jnp.bfloat16
PAD = 16
LANES = 128
VMEM = pl.BlockSpec(memory_space=pltpu.VMEM)
ANY = pl.BlockSpec(memory_space=pl.ANY)
HBM = pl.BlockSpec(memory_space=pltpu.HBM)


def call(
    body, outs, args, scratch=(), name=None, takes=VMEM, gives=VMEM, after=(),
    aliases=None,
):
    single = len(outs) == 1
    used, total = len(args), len(args) + len(after)

    def kernel(*refs):
        body(*refs[:used], *refs[total:])

    return pl.pallas_call(
        kernel,
        out_shape=outs[0] if single else tuple(outs),
        in_specs=(takes if isinstance(takes, list) else [takes] * used) + [ANY] * len(after),
        out_specs=gives if single or isinstance(gives, tuple) else tuple(gives for _ in outs),
        scratch_shapes=scratch,
        input_output_aliases=aliases or {},
        compiler_params=pltpu.CompilerParams(vmem_limit_bytes=40 * 1024 * 1024),
        cost_estimate=pl.CostEstimate(flops=1000, bytes_accessed=1000, transcendentals=0),
        name=name,
    )(*args, *after)


def pass_on(value, *after):
    return call(
        lambda *refs: None,
        [shape(value.shape, value.dtype)],
        (value,),
        name="pass_on",
        takes=ANY,
        gives=ANY,
        after=after,
        aliases={0: 0},
    )


def shape(dims, dtype=BF16):
    return jax.ShapeDtypeStruct(dims, dtype)


def dot(a, b, contract, precision=None):
    return lax.dot_general(
        a, b, (contract, ((), ())), preferred_element_type=F32, precision=precision
    )


def thirds(value):
    high = value.astype(BF16).astype(F32)
    rest = value - high
    middle = rest.astype(BF16).astype(F32)
    return high, middle, rest - middle


def lower_ones(rows):
    below = lax.broadcasted_iota(jnp.int32, (rows, rows), 0) >= lax.broadcasted_iota(
        jnp.int32, (rows, rows), 1
    )
    return below, jnp.where(below, 1.0, 0.0).astype(F32)


def load_all(n, count, *refs):
    k_ref, v_ref, *plain = refs[:count]
    outs, sems = refs[count:-1], refs[-1]
    pieces, copies = outs[:n], outs[n:]
    width = k_ref.shape[1] // n
    here = lax.axis_index("head")
    moves = []
    for e, piece in enumerate(pieces):
        target = lax.rem(here + e, n)
        columns = pl.ds(pl.multiple_of(target * width, LANES), width)
        moves.append((k_ref.at[:, columns], piece.at[:, pl.ds(0, width)]))
        moves.append((v_ref.at[:, columns], piece.at[:, pl.ds(width, width)]))
    moves += list(zip(plain, copies))
    running = [pltpu.make_async_copy(a, b, sems.at[i]) for i, (a, b) in enumerate(moves)]
    for one in running:
        one.start()
    for one in running:
        one.wait()


def join_rows(n, *refs):
    pieces, out = refs[:n], refs[n]
    length = pieces[0].shape[0]
    here = lax.axis_index("head")
    for e, piece in enumerate(pieces):
        place = lax.rem(here + n - e, n)
        out[pl.ds(pl.multiple_of(place * length, PAD), length), :] = piece[...]


def bits():
    index = lax.axis_index("ctx")
    low = lax.rem(index, 2)
    return low, lax.rem(lax.div(index, 2), 2), lax.div(index, 4)


def put_total(out, at, total):
    wide = out.shape[1]
    if out.dtype == F32:
        out[pl.ds(at, PAD), :] = jnp.broadcast_to(total, (PAD, wide))
        return
    row = lax.broadcasted_iota(jnp.int32, (PAD, wide), 0)
    high, middle, low = thirds(total)
    tile = jnp.where(row == 0, high, jnp.where(row == 1, middle, jnp.where(row == 2, low, 0.0)))
    out[pl.ds(at, PAD), :] = tile.astype(out.dtype)


def total_of(ref):
    tile = ref[pl.ds(ref.shape[0] - PAD, PAD), :].astype(F32)
    if ref.dtype == F32:
        return tile[0:1, :]
    return tile[0:1, :] + tile[1:2, :] + tile[2:3, :]


def state_of(ref):
    return ref[pl.ds(0, ref.shape[0] - PAD), :].astype(F32)


def part_of(held, which, rows):
    return held[pl.ds(pl.multiple_of(which * rows, rows), rows), :]


def summarize(k_ref, v_ref, d_ref, send, keep, held):
    low, _, _ = bits()
    half = HD // 2
    rows = d_ref.shape[1]
    sums = dot(lower_ones(rows)[1], d_ref[...], ((1,), (1,)), lax.Precision.HIGHEST)
    totals = []
    for head in range(d_ref.shape[0]):
        columns = pl.ds(head * HD, HD)
        column = sums[:, head : head + 1]
        last = column[rows - 1 : rows, :]
        carried = (k_ref[:, columns].astype(F32) * jnp.exp(last - column)).astype(BF16)
        held[:, columns] = dot(carried, v_ref[:, columns], ((0,), (0,)))
        totals.append(jnp.broadcast_to(last, (1, HD)))
    total = jnp.concatenate(totals, axis=1)
    for out, which in ((send, 1 - low), (keep, low)):
        out[pl.ds(0, half), :] = part_of(held, which, half).astype(out.dtype)
        put_total(out, half, total)


def pair_total(first, keep_ref, other_ref):
    kept, other = state_of(keep_ref), state_of(other_ref)
    kept_total, other_total = total_of(keep_ref), total_of(other_ref)
    late = jnp.where(first, other_total, kept_total)
    earlier, later = jnp.where(first, kept, other), jnp.where(first, other, kept)
    return jnp.exp(late) * earlier + later, kept_total + other_total


def chip_total(keep_ref, other_ref, send, keep, held):
    low, high, _ = bits()
    quarter = HD // 4
    held[...], total = pair_total(low == 0, keep_ref, other_ref)
    for out, which in ((send, 1 - high), (keep, high)):
        out[pl.ds(0, quarter), :] = part_of(held, which, quarter).astype(out.dtype)
        put_total(out, quarter, total)


def plane_total(keep_ref, other_ref, out):
    _, high, _ = bits()
    state, total = pair_total(high == 0, keep_ref, other_ref)
    out[pl.ds(0, state.shape[0]), :] = state.astype(out.dtype)
    put_total(out, state.shape[0], total)


def chip_priors(keep_ref, other_ref, *refs):
    planes, send, keep = refs[:-2], refs[-2], refs[-1]
    _, high, depth = bits()
    entering = jnp.zeros(send.shape, F32)
    between = jnp.zeros((1, send.shape[1]), F32)
    for i, ref in enumerate(planes):
        earlier = lax.rem(lax.div(depth, 2**i), 2) == 1
        entering = entering + jnp.where(earlier, jnp.exp(between) * state_of(ref), 0.0)
        between = between + jnp.where(earlier, total_of(ref), 0.0)
    first = high == 0
    early = jnp.where(first, state_of(keep_ref), state_of(other_ref))
    early_total = jnp.where(first, total_of(keep_ref), total_of(other_ref))
    second = jnp.exp(early_total) * entering + early
    send[...] = jnp.where(first, second, entering).astype(send.dtype)
    keep[...] = jnp.where(first, entering, second).astype(keep.dtype)


def block_priors(keep_ref, other_ref, prior_ref, prior_other_ref, send, keep, held):
    low, high, _ = bits()
    quarter = prior_ref.shape[0]
    for ref, which in ((prior_ref, high), (prior_other_ref, 1 - high)):
        held[pl.ds(pl.multiple_of(which * quarter, quarter), quarter), :] = ref[...].astype(F32)
    first = low == 0
    early = jnp.where(first, state_of(keep_ref), state_of(other_ref))
    early_total = jnp.where(first, total_of(keep_ref), total_of(other_ref))
    entering = held[...]
    second = jnp.exp(early_total) * entering + early
    send[...] = jnp.where(first, second, entering).astype(send.dtype)
    keep[...] = jnp.where(first, entering, second).astype(keep.dtype)


def grow(bit, own_ref, other_ref, out):
    rows = out.shape[0] - PAD
    first = lax.rem(lax.div(bits()[2], bit), 2) == 0
    state, total = pair_total(first, own_ref, other_ref)
    out[pl.ds(0, rows), :] = state.astype(out.dtype)
    put_total(out, rows, total)


def retain_inside(q_ref, k_ref, v_ref, d_ref, inside_ref, factor_ref):
    heads, rows = d_ref.shape
    below, ones = lower_ones(rows)
    sums = dot(ones, d_ref[...], ((1,), (1,)), lax.Precision.HIGHEST)
    same = lax.broadcasted_iota(jnp.int32, (rows, rows), 0) == lax.broadcasted_iota(
        jnp.int32, (rows, rows), 1
    )
    factor_ref[...] = jnp.exp(sums)
    for head in range(heads):
        columns = pl.ds(head * HD, HD)
        column = jnp.broadcast_to(sums[:, head : head + 1], (rows, rows))
        across = jnp.sum(jnp.where(same, column, 0.0), axis=0, keepdims=True)
        spread = jnp.exp(jnp.minimum(column - across, 0.0))
        scores = dot(q_ref[:, columns], k_ref[:, columns], ((1,), (1,)))
        weights = jnp.where(below, spread * scores, 0.0).astype(BF16)
        inside_ref[:, columns] = dot(weights, v_ref[:, columns], ((1,), (0,)))


def finish(
    part_ref, part_other_ref, q_ref, gate_ref, inside_ref, factor_ref, keep_ref, other_ref,
    o_ret, o_cross, held, ret_held, cross_held, sems,
):
    merge(part_ref, part_other_ref, cross_held)
    cross_out = pltpu.make_async_copy(cross_held, o_cross, sems.at[0])
    cross_out.start()
    low, _, _ = bits()
    half = keep_ref.shape[0]
    for ref, which in ((keep_ref, low), (other_ref, 1 - low)):
        held[pl.ds(pl.multiple_of(which * half, half), half), :] = ref[...]
    for head in range(factor_ref.shape[1]):
        columns = pl.ds(head * HD, HD)
        before = dot(q_ref[:, columns], held[:, columns], ((1,), (0,)))
        retained = inside_ref[:, columns] + factor_ref[:, head : head + 1] * before
        scale = lax.rsqrt(jnp.mean(retained * retained, axis=1, keepdims=True) + EPS)
        gate = gate_ref[:, columns].astype(F32)
        silu = gate / (1.0 + jnp.exp(-gate))
        ret_held[:, columns] = (retained * scale * silu).astype(BF16)
    ret_out = pltpu.make_async_copy(ret_held, o_ret, sems.at[1])
    ret_out.start()
    cross_out.wait()
    ret_out.wait()


def attend(hops, last, q_ref, q_other_ref, *refs):
    count = len(hops)
    blocks, refs = refs[: 2 * count], refs[2 * count :]
    carried, refs = (refs[:4], refs[4:]) if last else ((), refs)
    outs, (keys, values) = refs[:-2], refs[-2:]
    rows, wide = q_ref.shape
    heads = wide // HD
    length, width = blocks[0].shape[0], blocks[0].shape[1] // 2
    group = wide // width
    total = 2 * count * length
    low, high, depth = bits()
    for i, block in enumerate(blocks):
        keys[pl.ds(i * length, length), :] = block[:, pl.ds(0, width)]
        values[pl.ds(i * length, length), :] = block[:, pl.ds(width, width)]
    column = lax.broadcasted_iota(jnp.int32, (1, total), 1)
    limit = jnp.zeros((1, total), jnp.int32)
    for i in range(2 * count):
        s, t = hops[i // 2], i % 2
        if s == 0:
            core = low if t == 0 else 1 - low
            at = column + ((2 * high + core) * length - i * length)
        else:
            at = jnp.where(jnp.bitwise_xor(depth, s) < depth, -1, 4 * rows)
        limit = jnp.where(column >= i * length, at, limit)
    scale = 1.0 / (math.sqrt(HD) * math.log(2.0))
    row = lax.broadcasted_iota(jnp.int32, (rows, total), 0)
    lane = lax.broadcasted_iota(jnp.int32, (rows, LANES), 1)
    for which, (query, place) in enumerate(((q_other_ref, 1 - high), (q_ref, high))):
        allowed = row + (2 * place + low) * rows >= limit
        stats = jnp.zeros((rows, LANES), F32)
        if last:
            mixed_ref, stats_ref = carried[2 * which : 2 * which + 2]
            out = outs[which]
        else:
            out, stats_out = outs[2 * which : 2 * which + 2]
        for head in range(heads):
            columns = pl.ds(head * HD, HD)
            shared = pl.ds((head // group) * HD, HD)
            scores = dot(query[:, columns], keys[:, shared], ((1,), (1,))) * scale
            masked = jnp.where(allowed, scores, FAR)
            top = jnp.maximum(jnp.max(masked, axis=1, keepdims=True), NEAR)
            if last:
                old = stats_ref[:, 2 * head : 2 * head + 1]
                top = jnp.maximum(top, old)
            weights = jnp.exp2(masked - top)
            summed = jnp.sum(weights, axis=1, keepdims=True)
            mixed = dot(weights.astype(BF16), values[:, shared], ((1,), (0,)))
            if not last:
                out[:, columns] = mixed
                stats = jnp.where(lane == 2 * head, top, stats)
                stats = jnp.where(lane == 2 * head + 1, summed, stats)
                continue
            shrink = jnp.exp2(old - top)
            summed = summed + shrink * stats_ref[:, 2 * head + 1 : 2 * head + 2]
            mixed = mixed + shrink * mixed_ref[:, columns]
            some = summed > 0.0
            safe = jnp.where(some, summed, 1.0)
            out[:, columns] = (mixed / safe).astype(out.dtype)
            level = jnp.where(some, top + jnp.log2(safe), FAR)
            for i, third in enumerate(thirds(level)):
                stats = jnp.where(lane == 3 * head + i, third, stats)
        if last:
            out[:, pl.ds(wide, LANES)] = stats.astype(out.dtype)
        else:
            stats_out[...] = stats


def merge(keep_ref, other_ref, out):
    wide = out.shape[1]
    ins = (keep_ref, other_ref)
    stats = [ref[:, pl.ds(wide, LANES)].astype(F32) for ref in ins]
    for head in range(wide // HD):
        columns = pl.ds(head * HD, HD)
        levels = [
            tile[:, 3 * head : 3 * head + 1]
            + tile[:, 3 * head + 1 : 3 * head + 2]
            + tile[:, 3 * head + 2 : 3 * head + 3]
            for tile in stats
        ]
        top = functools.reduce(jnp.maximum, levels)
        weights = [jnp.exp2(level - top) for level in levels]
        share = 1.0 / functools.reduce(jnp.add, weights)
        mixed = functools.reduce(
            jnp.add, [(w * share) * ref[:, columns].astype(F32) for w, ref in zip(weights, ins)]
        )
        out[:, columns] = mixed.astype(BF16)


def per_device(count, n, q_ret, k_ret, v_ret, gate_ret, log_decay, q_cross, cache_k, cache_v):
    far = count // 4
    rows, wide = q_cross.shape
    heads = wide // HD
    length, width = cache_k.shape[0], cache_k.shape[1] // n
    half, quarter = HD // 2, HD // 4

    def swap(value, bit):
        return lax.ppermute(value, "ctx", [(b, b ^ bit) for b in range(count)])

    def to_head(value, e):
        return lax.ppermute(value, "head", [(y, (y + e) % n) for y in range(n)])

    plain = (k_ret, v_ret, log_decay.T, q_ret, q_cross, gate_ret)
    loaded = call(
        functools.partial(load_all, n, 2 + len(plain)),
        [pltpu.VMEM((length, 2 * width), BF16)] * n + [pltpu.VMEM(a.shape, a.dtype) for a in plain],
        [pltpu.with_memory_space_constraint(a, pltpu.HBM) for a in (cache_k, cache_v, *plain)],
        scratch=[pltpu.SemaphoreType.DMA((2 * n + len(plain),))],
        name="load_all",
        takes=HBM,
    )
    pieces = loaded[:n]
    k_ret, v_ret, decays, q_ret, q_cross, gate_ret = loaded[n:]
    arrived = [pieces[0]] + [to_head(pieces[e], e) for e in range(1, n)]
    sum_send, sum_keep = call(
        summarize,
        [shape((half + PAD, wide)), shape((half + PAD, wide), F32)],
        (k_ret, v_ret, decays),
        scratch=[pltpu.VMEM((HD, wide), F32)],
        name="summarize",
    )
    sum_other = swap(sum_send, 1)
    chip_send, chip_keep = call(
        chip_total,
        [shape((quarter + PAD, wide)), shape((quarter + PAD, wide), F32)],
        (sum_keep, sum_other),
        scratch=[pltpu.VMEM((half, wide), F32)],
        name="chip_total",
        after=arrived[-1:],
    )
    inside, factor = call(
        retain_inside,
        [shape((rows, wide), F32), shape((rows, heads), F32)],
        (q_ret, k_ret, v_ret, decays),
        name="retain_inside",
        after=(chip_send,),
    )
    blocks = {
        0: call(
            functools.partial(join_rows, n),
            [shape((n * length, 2 * width))],
            arrived,
            name="join_rows",
        )
    }
    chip_other = swap(chip_send, 2)
    q_cross = pass_on(q_cross, chip_send)
    q_other = swap(q_cross, 2)
    window = call(
        plane_total,
        [shape((quarter + PAD, wide))],
        (chip_keep, chip_other),
        name="plane_total",
        after=(factor,),
    )
    bit = far // 2
    while bit:
        for s in list(blocks):
            if s and bit == 1:
                blocks[s] = pass_on(blocks[s], window)
            blocks[s ^ bit] = swap(blocks[s], 4 * bit)
        bit //= 2
    planes, bit = [], 1
    while bit < far:
        planes.append(swap(window, 4 * bit))
        if 2 * bit < far:
            window = call(
                functools.partial(grow, bit),
                [shape(window.shape)],
                (window, planes[-1]),
                name="grow",
                after=(q_other,),
            )
        bit *= 2

    for s in blocks:
        if s % 2 and s > 1:
            blocks[s] = pass_on(blocks[s], window)
    def look(hops, last, outs, carried, name):
        keys = 2 * len(hops) * n * length
        both = []
        for s in hops:
            both += [blocks[s], swap(blocks[s], 1)]
        return call(
            functools.partial(attend, hops, last),
            outs,
            (q_cross, q_other, *both, *carried),
            scratch=[pltpu.VMEM((keys, width), BF16) for _ in range(2)],
            name=name,
        )

    hops = list(blocks)
    near = far // 2
    so_far = look(
        hops[:near],
        False,
        [shape((rows, wide), F32), shape((rows, LANES), F32)] * 2,
        (),
        "attend_near",
    )
    part_send, part_keep = look(
        hops[near:],
        True,
        [shape((rows, wide + LANES)), shape((rows, wide + LANES), F32)],
        so_far,
        "attend_far",
    )
    part_other = swap(part_send, 2)
    prior_send, prior_keep = call(
        chip_priors,
        [shape((quarter, wide)), shape((quarter, wide), F32)],
        (chip_keep, chip_other, *planes),
        name="chip_priors",
        after=so_far[1:2],
    )
    prior_other = swap(prior_send, 2)
    state_send, state_keep = call(
        block_priors,
        [shape((half, wide)), shape((half, wide))],
        (sum_keep, sum_other, prior_keep, prior_other),
        scratch=[pltpu.VMEM((half, wide), F32)],
        name="block_priors",
    )
    state_other = swap(state_send, 1)
    held = pltpu.VMEM((rows, wide), BF16)
    return call(
        finish,
        [shape((rows, wide))] * 2,
        (part_keep, part_other, q_ret, gate_ret, inside, factor, state_keep, state_other),
        scratch=[pltpu.VMEM((HD, wide), BF16), held, held, pltpu.SemaphoreType.DMA((2,))],
        name="finish",
        gives=HBM,
    )


def solution(mesh):
    split = P("ctx", "head")
    rows = P(("ctx", "head"), None)
    return jax.shard_map(
        functools.partial(per_device, mesh.shape["ctx"], mesh.shape["head"]),
        mesh=mesh,
        in_specs=(split,) * 6 + (rows,) * 2,
        out_specs=(split, split),
        check_vma=False,
    )
```

```python
import functools
import math

import jax
import jax.numpy as jnp
from jax import lax
from jax.experimental import pallas as pl
from jax.experimental.pallas import tpu as pltpu
from jax.sharding import PartitionSpec as P

HD = 256
FAR = -1e30
NEAR = -1e29
EPS = 1e-06
F32 = jnp.float32
BF16 = jnp.bfloat16
PAD = 16
LANES = 128
VMEM = pl.BlockSpec(memory_space=pltpu.VMEM)
ANY = pl.BlockSpec(memory_space=pl.ANY)
HBM = pl.BlockSpec(memory_space=pltpu.HBM)


def call(
    body, outs, args, scratch=(), name=None, takes=VMEM, gives=VMEM, after=(),
    aliases=None,
):
    single = len(outs) == 1
    used, total = len(args), len(args) + len(after)

    def kernel(*refs):
        body(*refs[:used], *refs[total:])

    return pl.pallas_call(
        kernel,
        out_shape=outs[0] if single else tuple(outs),
        in_specs=(takes if isinstance(takes, list) else [takes] * used) + [ANY] * len(after),
        out_specs=gives if single or isinstance(gives, tuple) else tuple(gives for _ in outs),
        scratch_shapes=scratch,
        input_output_aliases=aliases or {},
        compiler_params=pltpu.CompilerParams(vmem_limit_bytes=40 * 1024 * 1024),
        cost_estimate=pl.CostEstimate(flops=1000, bytes_accessed=1000, transcendentals=0),
        name=name,
    )(*args, *after)


def pass_on(value, *after):
    return call(
        lambda *refs: None,
        [shape(value.shape, value.dtype)],
        (value,),
        name="pass_on",
        takes=ANY,
        gives=ANY,
        after=after,
        aliases={0: 0},
    )


def shape(dims, dtype=BF16):
    return jax.ShapeDtypeStruct(dims, dtype)


def dot(a, b, contract, precision=None):
    return lax.dot_general(
        a, b, (contract, ((), ())), preferred_element_type=F32, precision=precision
    )


def thirds(value):
    high = value.astype(BF16).astype(F32)
    rest = value - high
    middle = rest.astype(BF16).astype(F32)
    return high, middle, rest - middle


def lower_ones(rows):
    below = lax.broadcasted_iota(jnp.int32, (rows, rows), 0) >= lax.broadcasted_iota(
        jnp.int32, (rows, rows), 1
    )
    return below, jnp.where(below, 1.0, 0.0).astype(F32)


def load_all(n, count, *refs):
    k_ref, v_ref, *plain = refs[:count]
    outs, sems = refs[count:-1], refs[-1]
    pieces, copies = outs[:n], outs[n:]
    width = k_ref.shape[1] // n
    here = lax.axis_index("head")
    moves = []
    for e, piece in enumerate(pieces):
        target = lax.rem(here + e, n)
        columns = pl.ds(pl.multiple_of(target * width, LANES), width)
        moves.append((k_ref.at[:, columns], piece.at[:, pl.ds(0, width)]))
        moves.append((v_ref.at[:, columns], piece.at[:, pl.ds(width, width)]))
    moves += list(zip(plain, copies))
    running = [pltpu.make_async_copy(a, b, sems.at[i]) for i, (a, b) in enumerate(moves)]
    for one in running:
        one.start()
    for one in running:
        one.wait()


def join_rows(n, *refs):
    pieces, out = refs[:n], refs[n]
    length = pieces[0].shape[0]
    here = lax.axis_index("head")
    for e, piece in enumerate(pieces):
        place = lax.rem(here + n - e, n)
        out[pl.ds(pl.multiple_of(place * length, PAD), length), :] = piece[...]


def bits():
    index = lax.axis_index("ctx")
    low = lax.rem(index, 2)
    return low, lax.rem(lax.div(index, 2), 2), lax.div(index, 4)


def put_total(out, at, total):
    wide = out.shape[1]
    if out.dtype == F32:
        out[pl.ds(at, PAD), :] = jnp.broadcast_to(total, (PAD, wide))
        return
    row = lax.broadcasted_iota(jnp.int32, (PAD, wide), 0)
    high, middle, low = thirds(total)
    tile = jnp.where(row == 0, high, jnp.where(row == 1, middle, jnp.where(row == 2, low, 0.0)))
    out[pl.ds(at, PAD), :] = tile.astype(out.dtype)


def total_of(ref):
    tile = ref[pl.ds(ref.shape[0] - PAD, PAD), :].astype(F32)
    if ref.dtype == F32:
        return tile[0:1, :]
    return tile[0:1, :] + tile[1:2, :] + tile[2:3, :]


def state_of(ref):
    return ref[pl.ds(0, ref.shape[0] - PAD), :].astype(F32)


def part_of(held, which, rows):
    return held[pl.ds(pl.multiple_of(which * rows, rows), rows), :]


def summarize(k_ref, v_ref, d_ref, send, keep, held):
    low, _, _ = bits()
    half = HD // 2
    rows = d_ref.shape[1]
    sums = dot(lower_ones(rows)[1], d_ref[...], ((1,), (1,)), lax.Precision.HIGHEST)
    totals = []
    for head in range(d_ref.shape[0]):
        columns = pl.ds(head * HD, HD)
        column = sums[:, head : head + 1]
        last = column[rows - 1 : rows, :]
        carried = (k_ref[:, columns].astype(F32) * jnp.exp(last - column)).astype(BF16)
        held[:, columns] = dot(carried, v_ref[:, columns], ((0,), (0,)))
        totals.append(jnp.broadcast_to(last, (1, HD)))
    total = jnp.concatenate(totals, axis=1)
    for out, which in ((send, 1 - low), (keep, low)):
        out[pl.ds(0, half), :] = part_of(held, which, half).astype(out.dtype)
        put_total(out, half, total)


def pair_total(first, keep_ref, other_ref):
    kept, other = state_of(keep_ref), state_of(other_ref)
    kept_total, other_total = total_of(keep_ref), total_of(other_ref)
    late = jnp.where(first, other_total, kept_total)
    earlier, later = jnp.where(first, kept, other), jnp.where(first, other, kept)
    return jnp.exp(late) * earlier + later, kept_total + other_total


def chip_total(keep_ref, other_ref, send, keep, held):
    low, high, _ = bits()
    quarter = HD // 4
    held[...], total = pair_total(low == 0, keep_ref, other_ref)
    for out, which in ((send, 1 - high), (keep, high)):
        out[pl.ds(0, quarter), :] = part_of(held, which, quarter).astype(out.dtype)
        put_total(out, quarter, total)


def plane_total(keep_ref, other_ref, out):
    _, high, _ = bits()
    state, total = pair_total(high == 0, keep_ref, other_ref)
    out[pl.ds(0, state.shape[0]), :] = state.astype(out.dtype)
    put_total(out, state.shape[0], total)


def chip_priors(keep_ref, other_ref, *refs):
    planes, send, keep = refs[:-2], refs[-2], refs[-1]
    _, high, depth = bits()
    entering = jnp.zeros(send.shape, F32)
    between = jnp.zeros((1, send.shape[1]), F32)
    for i, ref in enumerate(planes):
        earlier = lax.rem(lax.div(depth, 2**i), 2) == 1
        entering = entering + jnp.where(earlier, jnp.exp(between) * state_of(ref), 0.0)
        between = between + jnp.where(earlier, total_of(ref), 0.0)
    first = high == 0
    early = jnp.where(first, state_of(keep_ref), state_of(other_ref))
    early_total = jnp.where(first, total_of(keep_ref), total_of(other_ref))
    second = jnp.exp(early_total) * entering + early
    send[...] = jnp.where(first, second, entering).astype(send.dtype)
    keep[...] = jnp.where(first, entering, second).astype(keep.dtype)


def block_priors(keep_ref, other_ref, prior_ref, prior_other_ref, send, keep, held):
    low, high, _ = bits()
    quarter = prior_ref.shape[0]
    for ref, which in ((prior_ref, high), (prior_other_ref, 1 - high)):
        held[pl.ds(pl.multiple_of(which * quarter, quarter), quarter), :] = ref[...].astype(F32)
    first = low == 0
    early = jnp.where(first, state_of(keep_ref), state_of(other_ref))
    early_total = jnp.where(first, total_of(keep_ref), total_of(other_ref))
    entering = held[...]
    second = jnp.exp(early_total) * entering + early
    send[...] = jnp.where(first, second, entering).astype(send.dtype)
    keep[...] = jnp.where(first, entering, second).astype(keep.dtype)


def grow(bit, own_ref, other_ref, out):
    rows = out.shape[0] - PAD
    first = lax.rem(lax.div(bits()[2], bit), 2) == 0
    state, total = pair_total(first, own_ref, other_ref)
    out[pl.ds(0, rows), :] = state.astype(out.dtype)
    put_total(out, rows, total)


def retain_inside(q_ref, k_ref, v_ref, d_ref, inside_ref, factor_ref):
    heads, rows = d_ref.shape
    below, ones = lower_ones(rows)
    sums = dot(ones, d_ref[...], ((1,), (1,)), lax.Precision.HIGHEST)
    same = lax.broadcasted_iota(jnp.int32, (rows, rows), 0) == lax.broadcasted_iota(
        jnp.int32, (rows, rows), 1
    )
    factor_ref[...] = jnp.exp(sums)
    for head in range(heads):
        columns = pl.ds(head * HD, HD)
        column = jnp.broadcast_to(sums[:, head : head + 1], (rows, rows))
        across = jnp.sum(jnp.where(same, column, 0.0), axis=0, keepdims=True)
        spread = jnp.exp(jnp.minimum(column - across, 0.0))
        scores = dot(q_ref[:, columns], k_ref[:, columns], ((1,), (1,)))
        weights = jnp.where(below, spread * scores, 0.0).astype(BF16)
        inside_ref[:, columns] = dot(weights, v_ref[:, columns], ((1,), (0,)))


def finish(
    part_ref, part_other_ref, q_ref, gate_ref, inside_ref, factor_ref, keep_ref, other_ref,
    o_ret, o_cross, held, ret_held, cross_held, sems,
):
    merge(part_ref, part_other_ref, cross_held)
    cross_out = pltpu.make_async_copy(cross_held, o_cross, sems.at[0])
    cross_out.start()
    low, _, _ = bits()
    half = keep_ref.shape[0]
    for ref, which in ((keep_ref, low), (other_ref, 1 - low)):
        held[pl.ds(pl.multiple_of(which * half, half), half), :] = ref[...]
    for head in range(factor_ref.shape[1]):
        columns = pl.ds(head * HD, HD)
        before = dot(q_ref[:, columns], held[:, columns], ((1,), (0,)))
        retained = inside_ref[:, columns] + factor_ref[:, head : head + 1] * before
        scale = lax.rsqrt(jnp.mean(retained * retained, axis=1, keepdims=True) + EPS)
        gate = gate_ref[:, columns].astype(F32)
        silu = gate / (1.0 + jnp.exp(-gate))
        ret_held[:, columns] = (retained * scale * silu).astype(BF16)
    ret_out = pltpu.make_async_copy(ret_held, o_ret, sems.at[1])
    ret_out.start()
    cross_out.wait()
    ret_out.wait()


def copy_after(source, out):
    out[...] = source[...]


def attend(hops, last, sides, *refs):
    count = len(hops)
    queries, refs = refs[: len(sides)], refs[len(sides) :]
    blocks, refs = refs[: 2 * count], refs[2 * count :]
    taken = 2 * len(sides) if last else 0
    carried, refs = refs[:taken], refs[taken:]
    outs, (keys, values) = refs[:-2], refs[-2:]
    rows, wide = queries[0].shape
    heads = wide // HD
    length, width = blocks[0].shape[0], blocks[0].shape[1] // 2
    group = wide // width
    total = 2 * count * length
    low, high, depth = bits()
    for i, block in enumerate(blocks):
        keys[pl.ds(i * length, length), :] = block[:, pl.ds(0, width)]
        values[pl.ds(i * length, length), :] = block[:, pl.ds(width, width)]
    column = lax.broadcasted_iota(jnp.int32, (1, total), 1)
    limit = jnp.zeros((1, total), jnp.int32)
    for i in range(2 * count):
        s, t = hops[i // 2], i % 2
        if s == 0:
            core = low if t == 0 else 1 - low
            at = column + ((2 * high + core) * length - i * length)
        else:
            at = jnp.where(jnp.bitwise_xor(depth, s) < depth, -1, 4 * rows)
        limit = jnp.where(column >= i * length, at, limit)
    scale = 1.0 / (math.sqrt(HD) * math.log(2.0))
    row = lax.broadcasted_iota(jnp.int32, (rows, total), 0)
    lane = lax.broadcasted_iota(jnp.int32, (rows, LANES), 1)
    for which, (query, side) in enumerate(zip(queries, sides)):
        place = jnp.bitwise_xor(high, side)
        allowed = row + (2 * place + low) * rows >= limit
        stats = jnp.zeros((rows, LANES), F32)
        if last:
            mixed_ref, stats_ref = carried[2 * which : 2 * which + 2]
            out = outs[which]
        else:
            out, stats_out = outs[2 * which : 2 * which + 2]
        for head in range(heads):
            columns = pl.ds(head * HD, HD)
            shared = pl.ds((head // group) * HD, HD)
            scores = dot(query[:, columns], keys[:, shared], ((1,), (1,))) * scale
            masked = jnp.where(allowed, scores, FAR)
            top = jnp.maximum(jnp.max(masked, axis=1, keepdims=True), NEAR)
            if last:
                old = stats_ref[:, 2 * head : 2 * head + 1]
                top = jnp.maximum(top, old)
            weights = jnp.exp2(masked - top)
            summed = jnp.sum(weights, axis=1, keepdims=True)
            mixed = dot(weights.astype(BF16), values[:, shared], ((1,), (0,)))
            if not last:
                out[:, columns] = mixed
                stats = jnp.where(lane == 2 * head, top, stats)
                stats = jnp.where(lane == 2 * head + 1, summed, stats)
                continue
            shrink = jnp.exp2(old - top)
            summed = summed + shrink * stats_ref[:, 2 * head + 1 : 2 * head + 2]
            mixed = mixed + shrink * mixed_ref[:, columns]
            some = summed > 0.0
            safe = jnp.where(some, summed, 1.0)
            out[:, columns] = (mixed / safe).astype(out.dtype)
            level = jnp.where(some, top + jnp.log2(safe), FAR)
            for i, third in enumerate(thirds(level)):
                stats = jnp.where(lane == 3 * head + i, third, stats)
        if last:
            out[:, pl.ds(wide, LANES)] = stats.astype(out.dtype)
        else:
            stats_out[...] = stats


def merge(keep_ref, other_ref, out):
    wide = out.shape[1]
    ins = (keep_ref, other_ref)
    stats = [ref[:, pl.ds(wide, LANES)].astype(F32) for ref in ins]
    for head in range(wide // HD):
        columns = pl.ds(head * HD, HD)
        levels = [
            tile[:, 3 * head : 3 * head + 1]
            + tile[:, 3 * head + 1 : 3 * head + 2]
            + tile[:, 3 * head + 2 : 3 * head + 3]
            for tile in stats
        ]
        top = functools.reduce(jnp.maximum, levels)
        weights = [jnp.exp2(level - top) for level in levels]
        share = 1.0 / functools.reduce(jnp.add, weights)
        mixed = functools.reduce(
            jnp.add, [(w * share) * ref[:, columns].astype(F32) for w, ref in zip(weights, ins)]
        )
        out[:, columns] = mixed.astype(BF16)


def per_device(count, n, q_ret, k_ret, v_ret, gate_ret, log_decay, q_cross, cache_k, cache_v):
    far = count // 4
    rows, wide = q_cross.shape
    heads = wide // HD
    length, width = cache_k.shape[0], cache_k.shape[1] // n
    half, quarter = HD // 2, HD // 4

    def swap(value, bit):
        return lax.ppermute(value, "ctx", [(b, b ^ bit) for b in range(count)])

    def to_head(value, e):
        return lax.ppermute(value, "head", [(y, (y + e) % n) for y in range(n)])

    plain = (k_ret, v_ret, log_decay.T, q_ret, q_cross, gate_ret)
    loaded = call(
        functools.partial(load_all, n, 2 + len(plain)),
        [pltpu.VMEM((length, 2 * width), BF16)] * n + [pltpu.VMEM(a.shape, a.dtype) for a in plain],
        [pltpu.with_memory_space_constraint(a, pltpu.HBM) for a in (cache_k, cache_v, *plain)],
        scratch=[pltpu.SemaphoreType.DMA((2 * n + len(plain),))],
        name="load_all",
        takes=HBM,
    )
    pieces = loaded[:n]
    k_ret, v_ret, decays, q_ret, q_cross, gate_ret = loaded[n:]
    arrived = [pieces[0]] + [to_head(pieces[e], e) for e in range(1, n)]
    sum_send, sum_keep = call(
        summarize,
        [shape((half + PAD, wide)), shape((half + PAD, wide), F32)],
        (k_ret, v_ret, decays),
        scratch=[pltpu.VMEM((HD, wide), F32)],
        name="summarize",
    )
    sum_other = swap(sum_send, 1)
    chip_send, chip_keep = call(
        chip_total,
        [shape((quarter + PAD, wide)), shape((quarter + PAD, wide), F32)],
        (sum_keep, sum_other),
        scratch=[pltpu.VMEM((half, wide), F32)],
        name="chip_total",
        after=arrived[-1:],
    )
    inside, factor = call(
        retain_inside,
        [shape((rows, wide), F32), shape((rows, heads), F32)],
        (q_ret, k_ret, v_ret, decays),
        name="retain_inside",
        after=(chip_send,),
    )
    blocks = {
        0: call(
            functools.partial(join_rows, n),
            [shape((n * length, 2 * width))],
            arrived,
            name="join_rows",
        )
    }
    chip_other = swap(chip_send, 2)
    q_other = swap(q_cross, 2)
    bit = far // 2
    while bit > 1:
        for s in list(blocks):
            blocks[s ^ bit] = swap(blocks[s], 4 * bit)
        bit //= 2
    blocks[1] = swap(blocks[0], 4)
    window = call(
        plane_total,
        [shape((quarter + PAD, wide))],
        (chip_keep, chip_other),
        name="plane_total",
        after=(factor,),
    )
    planes, bit = [], 1
    while bit < far:
        planes.append(swap(window, 4 * bit))
        if 2 * bit < far:
            window = call(
                functools.partial(grow, bit),
                [shape(window.shape)],
                (window, planes[-1]),
                name="grow",
                after=(q_other, *[blocks[s] for s in blocks if s]),
            )
        bit *= 2

    def look(hops, last, outs, queries, carried, name):
        keys = 2 * len(hops) * n * length
        both = []
        for s in hops:
            if s not in swapped:
                swapped[s] = swap(blocks[s], 1)
            both += [blocks[s], swapped[s]]
        return call(
            functools.partial(attend, hops, last, [side for _, side in queries]),
            outs,
            (*[query for query, _ in queries], *both, *carried),
            scratch=[pltpu.VMEM((keys, width), BF16) for _ in range(2)],
            name=name,
        )

    swapped = {}
    near = list(blocks)
    so_far = look(
        near,
        False,
        [shape((rows, wide), F32), shape((rows, LANES), F32)] * 2,
        ((q_other, 1), (q_cross, 0)),
        (),
        "attend_near",
    )
    prior_send, prior_keep = call(
        chip_priors,
        [shape((quarter, wide)), shape((quarter, wide), F32)],
        (chip_keep, chip_other, *planes),
        name="chip_priors",
        after=so_far[1:2],
    )
    for s in near:
        if s > 1:
            ready = call(copy_after, [shape(blocks[s].shape)], (blocks[s],), after=(window,))
            blocks[s ^ 1] = pass_on(swap(ready, 4), prior_send)
    hops = [s for s in blocks if s not in near]
    packed = (rows, wide + LANES)
    part_send = look(hops, True, [shape(packed)], ((q_other, 1),), so_far[:2], "attend_far")
    part_keep = look(hops, True, [shape(packed, F32)], ((q_cross, 0),), so_far[2:], "attend_own")
    part_other = swap(part_send, 2)
    prior_other = swap(prior_send, 2)
    state_send, state_keep = call(
        block_priors,
        [shape((half, wide)), shape((half, wide))],
        (sum_keep, sum_other, prior_keep, prior_other),
        scratch=[pltpu.VMEM((half, wide), F32)],
        name="block_priors",
    )
    state_other = swap(state_send, 1)
    held = pltpu.VMEM((rows, wide), BF16)
    return call(
        finish,
        [shape((rows, wide))] * 2,
        (part_keep, part_other, q_ret, gate_ret, inside, factor, state_keep, state_other),
        scratch=[pltpu.VMEM((HD, wide), BF16), held, held, pltpu.SemaphoreType.DMA((2,))],
        name="finish",
        gives=HBM,
    )


def solution(mesh):
    split = P("ctx", "head")
    rows = P(("ctx", "head"), None)
    return jax.shard_map(
        functools.partial(per_device, mesh.shape["ctx"], mesh.shape["head"]),
        mesh=mesh,
        in_specs=(split,) * 6 + (rows,) * 2,
        out_specs=(split, split),
        check_vma=False,
    )
```

```python
import functools
import math

import jax
import jax.numpy as jnp
from jax import lax
from jax.experimental import pallas as pl
from jax.experimental.pallas import tpu as pltpu
from jax.sharding import PartitionSpec as P

HD = 256
FAR = -1e30
NEAR = -1e29
EPS = 1e-06
F32 = jnp.float32
BF16 = jnp.bfloat16
PAD = 16
LANES = 128
VMEM = pl.BlockSpec(memory_space=pltpu.VMEM)
ANY = pl.BlockSpec(memory_space=pl.ANY)
HBM = pl.BlockSpec(memory_space=pltpu.HBM)


def call(
    body, outs, args, scratch=(), name=None, takes=VMEM, gives=VMEM, after=(),
    aliases=None,
):
    single = len(outs) == 1
    used, total = len(args), len(args) + len(after)

    def kernel(*refs):
        body(*refs[:used], *refs[total:])

    return pl.pallas_call(
        kernel,
        out_shape=outs[0] if single else tuple(outs),
        in_specs=(takes if isinstance(takes, list) else [takes] * used) + [ANY] * len(after),
        out_specs=gives if single or isinstance(gives, tuple) else tuple(gives for _ in outs),
        scratch_shapes=scratch,
        input_output_aliases=aliases or {},
        compiler_params=pltpu.CompilerParams(vmem_limit_bytes=40 * 1024 * 1024),
        cost_estimate=pl.CostEstimate(flops=1000, bytes_accessed=1000, transcendentals=0),
        name=name,
    )(*args, *after)


def pass_on(value, *after):
    return call(
        lambda *refs: None,
        [shape(value.shape, value.dtype)],
        (value,),
        name="pass_on",
        takes=ANY,
        gives=ANY,
        after=after,
        aliases={0: 0},
    )


def shape(dims, dtype=BF16):
    return jax.ShapeDtypeStruct(dims, dtype)


def dot(a, b, contract, precision=None):
    return lax.dot_general(
        a, b, (contract, ((), ())), preferred_element_type=F32, precision=precision
    )


def thirds(value):
    high = value.astype(BF16).astype(F32)
    rest = value - high
    middle = rest.astype(BF16).astype(F32)
    return high, middle, rest - middle


def lower_ones(rows):
    below = lax.broadcasted_iota(jnp.int32, (rows, rows), 0) >= lax.broadcasted_iota(
        jnp.int32, (rows, rows), 1
    )
    return below, jnp.where(below, 1.0, 0.0).astype(F32)


def load_all(n, count, *refs):
    k_ref, v_ref, *plain = refs[:count]
    outs, sems = refs[count:-1], refs[-1]
    pieces, copies = outs[:n], outs[n:]
    width = k_ref.shape[1] // n
    here = lax.axis_index("head")
    moves = []
    for e, piece in enumerate(pieces):
        target = lax.rem(here + e, n)
        columns = pl.ds(pl.multiple_of(target * width, LANES), width)
        moves.append((k_ref.at[:, columns], piece.at[:, pl.ds(0, width)]))
        moves.append((v_ref.at[:, columns], piece.at[:, pl.ds(width, width)]))
    moves += list(zip(plain, copies))
    running = [pltpu.make_async_copy(a, b, sems.at[i]) for i, (a, b) in enumerate(moves)]
    for one in running:
        one.start()
    for one in running:
        one.wait()


def join_rows(n, *refs):
    pieces, out = refs[:n], refs[n]
    length = pieces[0].shape[0]
    here = lax.axis_index("head")
    for e, piece in enumerate(pieces):
        place = lax.rem(here + n - e, n)
        out[pl.ds(pl.multiple_of(place * length, PAD), length), :] = piece[...]


def bits():
    index = lax.axis_index("ctx")
    low = lax.rem(index, 2)
    return low, lax.rem(lax.div(index, 2), 2), lax.div(index, 4)


def put_total(out, at, total):
    wide = out.shape[1]
    if out.dtype == F32:
        out[pl.ds(at, PAD), :] = jnp.broadcast_to(total, (PAD, wide))
        return
    row = lax.broadcasted_iota(jnp.int32, (PAD, wide), 0)
    high, middle, low = thirds(total)
    tile = jnp.where(row == 0, high, jnp.where(row == 1, middle, jnp.where(row == 2, low, 0.0)))
    out[pl.ds(at, PAD), :] = tile.astype(out.dtype)


def total_of(ref):
    tile = ref[pl.ds(ref.shape[0] - PAD, PAD), :].astype(F32)
    if ref.dtype == F32:
        return tile[0:1, :]
    return tile[0:1, :] + tile[1:2, :] + tile[2:3, :]


def state_of(ref):
    return ref[pl.ds(0, ref.shape[0] - PAD), :].astype(F32)


def part_of(held, which, rows):
    return held[pl.ds(pl.multiple_of(which * rows, rows), rows), :]


def summarize(k_ref, v_ref, d_ref, send, keep, held):
    low, _, _ = bits()
    half = HD // 2
    rows = d_ref.shape[1]
    sums = dot(lower_ones(rows)[1], d_ref[...], ((1,), (1,)), lax.Precision.HIGHEST)
    totals = []
    for head in range(d_ref.shape[0]):
        columns = pl.ds(head * HD, HD)
        column = sums[:, head : head + 1]
        last = column[rows - 1 : rows, :]
        carried = (k_ref[:, columns].astype(F32) * jnp.exp(last - column)).astype(BF16)
        held[:, columns] = dot(carried, v_ref[:, columns], ((0,), (0,)))
        totals.append(jnp.broadcast_to(last, (1, HD)))
    total = jnp.concatenate(totals, axis=1)
    for out, which in ((send, 1 - low), (keep, low)):
        out[pl.ds(0, half), :] = part_of(held, which, half).astype(out.dtype)
        put_total(out, half, total)


def pair_total(first, keep_ref, other_ref):
    kept, other = state_of(keep_ref), state_of(other_ref)
    kept_total, other_total = total_of(keep_ref), total_of(other_ref)
    late = jnp.where(first, other_total, kept_total)
    earlier, later = jnp.where(first, kept, other), jnp.where(first, other, kept)
    return jnp.exp(late) * earlier + later, kept_total + other_total


def chip_total(keep_ref, other_ref, send, keep, held):
    low, high, _ = bits()
    quarter = HD // 4
    held[...], total = pair_total(low == 0, keep_ref, other_ref)
    for out, which in ((send, 1 - high), (keep, high)):
        out[pl.ds(0, quarter), :] = part_of(held, which, quarter).astype(out.dtype)
        put_total(out, quarter, total)


def plane_total(keep_ref, other_ref, out):
    _, high, _ = bits()
    state, total = pair_total(high == 0, keep_ref, other_ref)
    out[pl.ds(0, state.shape[0]), :] = state.astype(out.dtype)
    put_total(out, state.shape[0], total)


def chip_priors(keep_ref, other_ref, *refs):
    planes, send, keep = refs[:-2], refs[-2], refs[-1]
    _, high, depth = bits()
    entering = jnp.zeros(send.shape, F32)
    between = jnp.zeros((1, send.shape[1]), F32)
    for i, ref in enumerate(planes):
        earlier = lax.rem(lax.div(depth, 2**i), 2) == 1
        entering = entering + jnp.where(earlier, jnp.exp(between) * state_of(ref), 0.0)
        between = between + jnp.where(earlier, total_of(ref), 0.0)
    first = high == 0
    early = jnp.where(first, state_of(keep_ref), state_of(other_ref))
    early_total = jnp.where(first, total_of(keep_ref), total_of(other_ref))
    second = jnp.exp(early_total) * entering + early
    send[...] = jnp.where(first, second, entering).astype(send.dtype)
    keep[...] = jnp.where(first, entering, second).astype(keep.dtype)


def block_priors(keep_ref, other_ref, prior_ref, prior_other_ref, send, keep, held):
    low, high, _ = bits()
    quarter = prior_ref.shape[0]
    for ref, which in ((prior_ref, high), (prior_other_ref, 1 - high)):
        held[pl.ds(pl.multiple_of(which * quarter, quarter), quarter), :] = ref[...].astype(F32)
    first = low == 0
    early = jnp.where(first, state_of(keep_ref), state_of(other_ref))
    early_total = jnp.where(first, total_of(keep_ref), total_of(other_ref))
    entering = held[...]
    second = jnp.exp(early_total) * entering + early
    send[...] = jnp.where(first, second, entering).astype(send.dtype)
    keep[...] = jnp.where(first, entering, second).astype(keep.dtype)


def grow(bit, own_ref, other_ref, out):
    rows = out.shape[0] - PAD
    first = lax.rem(lax.div(bits()[2], bit), 2) == 0
    state, total = pair_total(first, own_ref, other_ref)
    out[pl.ds(0, rows), :] = state.astype(out.dtype)
    put_total(out, rows, total)


def retain_inside(q_ref, k_ref, v_ref, d_ref, inside_ref, factor_ref):
    heads, rows = d_ref.shape
    below, ones = lower_ones(rows)
    sums = dot(ones, d_ref[...], ((1,), (1,)), lax.Precision.HIGHEST)
    same = lax.broadcasted_iota(jnp.int32, (rows, rows), 0) == lax.broadcasted_iota(
        jnp.int32, (rows, rows), 1
    )
    factor_ref[...] = jnp.exp(sums)
    for head in range(heads):
        columns = pl.ds(head * HD, HD)
        column = jnp.broadcast_to(sums[:, head : head + 1], (rows, rows))
        across = jnp.sum(jnp.where(same, column, 0.0), axis=0, keepdims=True)
        spread = jnp.exp(jnp.minimum(column - across, 0.0))
        scores = dot(q_ref[:, columns], k_ref[:, columns], ((1,), (1,)))
        weights = jnp.where(below, spread * scores, 0.0).astype(BF16)
        inside_ref[:, columns] = dot(weights, v_ref[:, columns], ((1,), (0,)))


def finish(
    part_ref, part_other_ref, q_ref, gate_ref, inside_ref, factor_ref, keep_ref, other_ref,
    o_ret, o_cross, held, ret_held, cross_held, sems,
):
    merge(part_ref, part_other_ref, cross_held)
    cross_out = pltpu.make_async_copy(cross_held, o_cross, sems.at[0])
    cross_out.start()
    low, _, _ = bits()
    half = keep_ref.shape[0]
    for ref, which in ((keep_ref, low), (other_ref, 1 - low)):
        held[pl.ds(pl.multiple_of(which * half, half), half), :] = ref[...]
    for head in range(factor_ref.shape[1]):
        columns = pl.ds(head * HD, HD)
        before = dot(q_ref[:, columns], held[:, columns], ((1,), (0,)))
        retained = inside_ref[:, columns] + factor_ref[:, head : head + 1] * before
        scale = lax.rsqrt(jnp.mean(retained * retained, axis=1, keepdims=True) + EPS)
        gate = gate_ref[:, columns].astype(F32)
        silu = gate / (1.0 + jnp.exp(-gate))
        ret_held[:, columns] = (retained * scale * silu).astype(BF16)
    ret_out = pltpu.make_async_copy(ret_held, o_ret, sems.at[1])
    ret_out.start()
    cross_out.wait()
    ret_out.wait()


def copy_after(source, out):
    out[...] = source[...]


def attend(hops, last, sides, *refs):
    count = len(hops)
    queries, refs = refs[: len(sides)], refs[len(sides) :]
    blocks, refs = refs[: 2 * count], refs[2 * count :]
    taken = 2 * len(sides) if last else 0
    carried, refs = refs[:taken], refs[taken:]
    outs, (keys, values) = refs[:-2], refs[-2:]
    rows, wide = queries[0].shape
    heads = wide // HD
    length, width = blocks[0].shape[0], blocks[0].shape[1] // 2
    group = wide // width
    total = 2 * count * length
    low, high, depth = bits()
    for i, block in enumerate(blocks):
        keys[pl.ds(i * length, length), :] = block[:, pl.ds(0, width)]
        values[pl.ds(i * length, length), :] = block[:, pl.ds(width, width)]
    column = lax.broadcasted_iota(jnp.int32, (1, total), 1)
    limit = jnp.zeros((1, total), jnp.int32)
    for i in range(2 * count):
        s, t = hops[i // 2], i % 2
        if s == 0:
            core = low if t == 0 else 1 - low
            at = column + ((2 * high + core) * length - i * length)
        else:
            at = jnp.where(jnp.bitwise_xor(depth, s) < depth, -1, 4 * rows)
        limit = jnp.where(column >= i * length, at, limit)
    scale = 1.0 / (math.sqrt(HD) * math.log(2.0))
    row = lax.broadcasted_iota(jnp.int32, (rows, total), 0)
    lane = lax.broadcasted_iota(jnp.int32, (rows, LANES), 1)
    for which, (query, side) in enumerate(zip(queries, sides)):
        place = jnp.bitwise_xor(high, side)
        allowed = row + (2 * place + low) * rows >= limit
        stats = jnp.zeros((rows, LANES), F32)
        if last:
            mixed_ref, stats_ref = carried[2 * which : 2 * which + 2]
            out = outs[which]
        else:
            out, stats_out = outs[2 * which : 2 * which + 2]
        for head in range(heads):
            columns = pl.ds(head * HD, HD)
            shared = pl.ds((head // group) * HD, HD)
            scores = dot(query[:, columns], keys[:, shared], ((1,), (1,))) * scale
            masked = jnp.where(allowed, scores, FAR)
            top = jnp.maximum(jnp.max(masked, axis=1, keepdims=True), NEAR)
            if last:
                old = stats_ref[:, 2 * head : 2 * head + 1]
                top = jnp.maximum(top, old)
            weights = jnp.exp2(masked - top)
            summed = jnp.sum(weights, axis=1, keepdims=True)
            mixed = dot(weights.astype(BF16), values[:, shared], ((1,), (0,)))
            if not last:
                out[:, columns] = mixed
                stats = jnp.where(lane == 2 * head, top, stats)
                stats = jnp.where(lane == 2 * head + 1, summed, stats)
                continue
            shrink = jnp.exp2(old - top)
            summed = summed + shrink * stats_ref[:, 2 * head + 1 : 2 * head + 2]
            mixed = mixed + shrink * mixed_ref[:, columns]
            some = summed > 0.0
            safe = jnp.where(some, summed, 1.0)
            out[:, columns] = (mixed / safe).astype(out.dtype)
            level = jnp.where(some, top + jnp.log2(safe), FAR)
            for i, third in enumerate(thirds(level)):
                stats = jnp.where(lane == 3 * head + i, third, stats)
        if last:
            out[:, pl.ds(wide, LANES)] = stats.astype(out.dtype)
        else:
            stats_out[...] = stats


def merge(keep_ref, other_ref, out):
    wide = out.shape[1]
    ins = (keep_ref, other_ref)
    stats = [ref[:, pl.ds(wide, LANES)].astype(F32) for ref in ins]
    for head in range(wide // HD):
        columns = pl.ds(head * HD, HD)
        levels = [
            tile[:, 3 * head : 3 * head + 1]
            + tile[:, 3 * head + 1 : 3 * head + 2]
            + tile[:, 3 * head + 2 : 3 * head + 3]
            for tile in stats
        ]
        top = functools.reduce(jnp.maximum, levels)
        weights = [jnp.exp2(level - top) for level in levels]
        share = 1.0 / functools.reduce(jnp.add, weights)
        mixed = functools.reduce(
            jnp.add, [(w * share) * ref[:, columns].astype(F32) for w, ref in zip(weights, ins)]
        )
        out[:, columns] = mixed.astype(BF16)


def per_device(count, n, q_ret, k_ret, v_ret, gate_ret, log_decay, q_cross, cache_k, cache_v):
    far = count // 4
    rows, wide = q_cross.shape
    heads = wide // HD
    length, width = cache_k.shape[0], cache_k.shape[1] // n
    half, quarter = HD // 2, HD // 4

    def swap(value, bit):
        return lax.ppermute(value, "ctx", [(b, b ^ bit) for b in range(count)])

    def to_head(value, e, bit):
        pairs = [
            (b * n + y, (b ^ (4 * bit)) * n + (y + e) % n) for b in range(count) for y in range(n)
        ]
        return lax.ppermute(value, ("ctx", "head"), pairs)

    def joined(bit):
        parts = [pieces[e] if e + bit == 0 else to_head(pieces[e], e, bit) for e in range(n)]
        return call(
            functools.partial(join_rows, n),
            [shape((n * length, 2 * width))],
            parts,
            name="join_rows",
        )

    plain = (k_ret, v_ret, log_decay.T, q_ret, q_cross, gate_ret)
    loaded = call(
        functools.partial(load_all, n, 2 + len(plain)),
        [pltpu.VMEM((length, 2 * width), BF16)] * n + [pltpu.VMEM(a.shape, a.dtype) for a in plain],
        [pltpu.with_memory_space_constraint(a, pltpu.HBM) for a in (cache_k, cache_v, *plain)],
        scratch=[pltpu.SemaphoreType.DMA((2 * n + len(plain),))],
        name="load_all",
        takes=HBM,
    )
    pieces = loaded[:n]
    k_ret, v_ret, decays, q_ret, q_cross, gate_ret = loaded[n:]
    sum_send, sum_keep = call(
        summarize,
        [shape((half + PAD, wide)), shape((half + PAD, wide), F32)],
        (k_ret, v_ret, decays),
        scratch=[pltpu.VMEM((HD, wide), F32)],
        name="summarize",
    )
    sum_other = swap(sum_send, 1)
    chip_send, chip_keep = call(
        chip_total,
        [shape((quarter + PAD, wide)), shape((quarter + PAD, wide), F32)],
        (sum_keep, sum_other),
        scratch=[pltpu.VMEM((half, wide), F32)],
        name="chip_total",
    )
    inside, factor = call(
        retain_inside,
        [shape((rows, wide), F32), shape((rows, heads), F32)],
        (q_ret, k_ret, v_ret, decays),
        name="retain_inside",
        after=(chip_send,),
    )
    chip_other = swap(chip_send, 2)
    q_other = swap(q_cross, 2)
    blocks = {0: joined(0)}
    bit = far // 2
    while bit > 1:
        for s in list(blocks):
            blocks[s ^ bit] = joined(bit) if s == 0 else swap(blocks[s], 4 * bit)
        bit //= 2
    blocks[1] = joined(1)
    window = call(
        plane_total,
        [shape((quarter + PAD, wide))],
        (chip_keep, chip_other),
        name="plane_total",
        after=(factor,),
    )
    planes, bit = [], 1
    while bit < far:
        planes.append(swap(window, 4 * bit))
        if 2 * bit < far:
            window = call(
                functools.partial(grow, bit),
                [shape(window.shape)],
                (window, planes[-1]),
                name="grow",
                after=(q_other, *[blocks[s] for s in blocks if s]),
            )
        bit *= 2

    def look(hops, last, outs, queries, carried, name):
        keys = 2 * len(hops) * n * length
        both = []
        for s in hops:
            if s not in swapped:
                swapped[s] = swap(blocks[s], 1)
            both += [blocks[s], swapped[s]]
        return call(
            functools.partial(attend, hops, last, [side for _, side in queries]),
            outs,
            (*[query for query, _ in queries], *both, *carried),
            scratch=[pltpu.VMEM((keys, width), BF16) for _ in range(2)],
            name=name,
        )

    swapped = {}
    near = list(blocks)
    so_far = look(
        near,
        False,
        [shape((rows, wide), F32), shape((rows, LANES), F32)] * 2,
        ((q_other, 1), (q_cross, 0)),
        (),
        "attend_near",
    )
    prior_send, prior_keep = call(
        chip_priors,
        [shape((quarter, wide)), shape((quarter, wide), F32)],
        (chip_keep, chip_other, *planes),
        name="chip_priors",
        after=so_far[1:2],
    )
    for s in near:
        if s > 1:
            ready = call(copy_after, [shape(blocks[s].shape)], (blocks[s],), after=(window,))
            blocks[s ^ 1] = pass_on(swap(ready, 4), prior_send)
    hops = [s for s in blocks if s not in near]
    packed = (rows, wide + LANES)
    part_send = look(hops, True, [shape(packed)], ((q_other, 1),), so_far[:2], "attend_far")
    part_keep = look(hops, True, [shape(packed, F32)], ((q_cross, 0),), so_far[2:], "attend_own")
    part_other = swap(part_send, 2)
    prior_other = swap(prior_send, 2)
    state_send, state_keep = call(
        block_priors,
        [shape((half, wide)), shape((half, wide))],
        (sum_keep, sum_other, prior_keep, prior_other),
        scratch=[pltpu.VMEM((half, wide), F32)],
        name="block_priors",
    )
    state_other = swap(state_send, 1)
    held = pltpu.VMEM((rows, wide), BF16)
    return call(
        finish,
        [shape((rows, wide))] * 2,
        (part_keep, part_other, q_ret, gate_ret, inside, factor, state_keep, state_other),
        scratch=[pltpu.VMEM((HD, wide), BF16), held, held, pltpu.SemaphoreType.DMA((2,))],
        name="finish",
        gives=HBM,
    )


def solution(mesh):
    split = P("ctx", "head")
    rows = P(("ctx", "head"), None)
    return jax.shard_map(
        functools.partial(per_device, mesh.shape["ctx"], mesh.shape["head"]),
        mesh=mesh,
        in_specs=(split,) * 6 + (rows,) * 2,
        out_specs=(split, split),
        check_vma=False,
    )
```

```python
import functools
import math

import jax
import jax.numpy as jnp
from jax import lax
from jax.experimental import pallas as pl
from jax.experimental.pallas import tpu as pltpu
from jax.sharding import PartitionSpec as P

HD = 256
FAR = -1e30
NEAR = -1e29
EPS = 1e-06
F32 = jnp.float32
BF16 = jnp.bfloat16
PAD = 16
LANES = 128
VMEM = pl.BlockSpec(memory_space=pltpu.VMEM)
ANY = pl.BlockSpec(memory_space=pl.ANY)
HBM = pl.BlockSpec(memory_space=pltpu.HBM)


def call(
    body, outs, args, scratch=(), name=None, flops=1000, takes=VMEM, gives=VMEM, after=(),
    aliases=None,
):
    single = len(outs) == 1
    used, total = len(args), len(args) + len(after)

    def kernel(*refs):
        body(*refs[:used], *refs[total:])

    return pl.pallas_call(
        kernel,
        out_shape=outs[0] if single else tuple(outs),
        in_specs=(takes if isinstance(takes, list) else [takes] * used) + [ANY] * len(after),
        out_specs=gives if single or isinstance(gives, tuple) else tuple(gives for _ in outs),
        scratch_shapes=scratch,
        input_output_aliases=aliases or {},
        compiler_params=pltpu.CompilerParams(vmem_limit_bytes=40 * 1024 * 1024),
        cost_estimate=pl.CostEstimate(flops=flops, bytes_accessed=1000, transcendentals=0),
        name=name,
    )(*args, *after)


def pass_on(value, *after):
    return call(
        lambda *refs: None,
        [shape(value.shape, value.dtype)],
        (value,),
        name="pass_on",
        takes=ANY,
        gives=ANY,
        after=after,
        aliases={0: 0},
    )


def shape(dims, dtype=BF16):
    return jax.ShapeDtypeStruct(dims, dtype)


def dot(a, b, contract, precision=None):
    return lax.dot_general(
        a, b, (contract, ((), ())), preferred_element_type=F32, precision=precision
    )


def thirds(value):
    high = value.astype(BF16).astype(F32)
    rest = value - high
    middle = rest.astype(BF16).astype(F32)
    return high, middle, rest - middle


def lower_ones(rows):
    below = lax.broadcasted_iota(jnp.int32, (rows, rows), 0) >= lax.broadcasted_iota(
        jnp.int32, (rows, rows), 1
    )
    return below, jnp.where(below, 1.0, 0.0).astype(F32)


def load_all(n, count, *refs):
    k_ref, v_ref, *plain = refs[:count]
    outs, sems = refs[count:-1], refs[-1]
    pieces, copies = outs[:n], outs[n:]
    width = k_ref.shape[1] // n
    here = lax.axis_index("head")
    moves = []
    for e, piece in enumerate(pieces):
        target = lax.rem(here + e, n)
        columns = pl.ds(pl.multiple_of(target * width, LANES), width)
        moves.append((k_ref.at[:, columns], piece.at[:, pl.ds(0, width)]))
        moves.append((v_ref.at[:, columns], piece.at[:, pl.ds(width, width)]))
    moves += list(zip(plain, copies))
    running = [pltpu.make_async_copy(a, b, sems.at[i]) for i, (a, b) in enumerate(moves)]
    for one in running:
        one.start()
    for one in running:
        one.wait()


def join_rows(n, *refs):
    pieces, out = refs[:n], refs[n]
    length = pieces[0].shape[0]
    here = lax.axis_index("head")
    for e, piece in enumerate(pieces):
        place = lax.rem(here + n - e, n)
        out[pl.ds(pl.multiple_of(place * length, PAD), length), :] = piece[...]


def bits():
    index = lax.axis_index("ctx")
    low = lax.rem(index, 2)
    return low, lax.rem(lax.div(index, 2), 2), lax.div(index, 4)


def put_total(out, at, total):
    wide = out.shape[1]
    if out.dtype == F32:
        out[pl.ds(at, PAD), :] = jnp.broadcast_to(total, (PAD, wide))
        return
    row = lax.broadcasted_iota(jnp.int32, (PAD, wide), 0)
    high, middle, low = thirds(total)
    tile = jnp.where(row == 0, high, jnp.where(row == 1, middle, jnp.where(row == 2, low, 0.0)))
    out[pl.ds(at, PAD), :] = tile.astype(out.dtype)


def total_of(ref):
    tile = ref[pl.ds(ref.shape[0] - PAD, PAD), :].astype(F32)
    if ref.dtype == F32:
        return tile[0:1, :]
    return tile[0:1, :] + tile[1:2, :] + tile[2:3, :]


def state_of(ref):
    return ref[pl.ds(0, ref.shape[0] - PAD), :].astype(F32)


def part_of(held, which, rows):
    return held[pl.ds(pl.multiple_of(which * rows, rows), rows), :]


def summarize(k_ref, v_ref, d_ref, send, keep, held):
    low, _, _ = bits()
    half = HD // 2
    rows = d_ref.shape[1]
    sums = dot(lower_ones(rows)[1], d_ref[...], ((1,), (1,)), lax.Precision.HIGHEST)
    totals = []
    for head in range(d_ref.shape[0]):
        columns = pl.ds(head * HD, HD)
        column = sums[:, head : head + 1]
        last = column[rows - 1 : rows, :]
        carried = (k_ref[:, columns].astype(F32) * jnp.exp(last - column)).astype(BF16)
        held[:, columns] = dot(carried, v_ref[:, columns], ((0,), (0,)))
        totals.append(jnp.broadcast_to(last, (1, HD)))
    total = jnp.concatenate(totals, axis=1)
    for out, which in ((send, 1 - low), (keep, low)):
        out[pl.ds(0, half), :] = part_of(held, which, half).astype(out.dtype)
        put_total(out, half, total)


def pair_total(first, keep_ref, other_ref):
    kept, other = state_of(keep_ref), state_of(other_ref)
    kept_total, other_total = total_of(keep_ref), total_of(other_ref)
    late = jnp.where(first, other_total, kept_total)
    earlier, later = jnp.where(first, kept, other), jnp.where(first, other, kept)
    return jnp.exp(late) * earlier + later, kept_total + other_total


def chip_total(keep_ref, other_ref, send, keep, held):
    low, high, _ = bits()
    quarter = HD // 4
    held[...], total = pair_total(low == 0, keep_ref, other_ref)
    for out, which in ((send, 1 - high), (keep, high)):
        out[pl.ds(0, quarter), :] = part_of(held, which, quarter).astype(out.dtype)
        put_total(out, quarter, total)


def plane_total(keep_ref, other_ref, block_ref, out, block_out):
    block_out[...] = block_ref[...]
    _, high, _ = bits()
    state, total = pair_total(high == 0, keep_ref, other_ref)
    out[pl.ds(0, state.shape[0]), :] = state.astype(out.dtype)
    put_total(out, state.shape[0], total)


def chip_priors(keep_ref, other_ref, *refs):
    planes, send, keep = refs[:-2], refs[-2], refs[-1]
    _, high, depth = bits()
    entering = jnp.zeros(send.shape, F32)
    between = jnp.zeros((1, send.shape[1]), F32)
    for i, ref in enumerate(planes):
        earlier = lax.rem(lax.div(depth, 2**i), 2) == 1
        entering = entering + jnp.where(earlier, jnp.exp(between) * state_of(ref), 0.0)
        between = between + jnp.where(earlier, total_of(ref), 0.0)
    first = high == 0
    early = jnp.where(first, state_of(keep_ref), state_of(other_ref))
    early_total = jnp.where(first, total_of(keep_ref), total_of(other_ref))
    second = jnp.exp(early_total) * entering + early
    send[...] = jnp.where(first, second, entering).astype(send.dtype)
    keep[...] = jnp.where(first, entering, second).astype(keep.dtype)


def block_priors(keep_ref, other_ref, prior_ref, prior_other_ref, send, keep, held):
    low, high, _ = bits()
    quarter = prior_ref.shape[0]
    for ref, which in ((prior_ref, high), (prior_other_ref, 1 - high)):
        held[pl.ds(pl.multiple_of(which * quarter, quarter), quarter), :] = ref[...].astype(F32)
    first = low == 0
    early = jnp.where(first, state_of(keep_ref), state_of(other_ref))
    early_total = jnp.where(first, total_of(keep_ref), total_of(other_ref))
    entering = held[...]
    second = jnp.exp(early_total) * entering + early
    send[...] = jnp.where(first, second, entering).astype(send.dtype)
    keep[...] = jnp.where(first, entering, second).astype(keep.dtype)


def grow(bit, own_ref, other_ref, out):
    rows = out.shape[0] - PAD
    first = lax.rem(lax.div(bits()[2], bit), 2) == 0
    state, total = pair_total(first, own_ref, other_ref)
    out[pl.ds(0, rows), :] = state.astype(out.dtype)
    put_total(out, rows, total)


def retain_inside(q_ref, k_ref, v_ref, d_ref, inside_ref, factor_ref):
    heads, rows = d_ref.shape
    below, ones = lower_ones(rows)
    sums = dot(ones, d_ref[...], ((1,), (1,)), lax.Precision.HIGHEST)
    same = lax.broadcasted_iota(jnp.int32, (rows, rows), 0) == lax.broadcasted_iota(
        jnp.int32, (rows, rows), 1
    )
    factor_ref[...] = jnp.exp(sums)
    for head in range(heads):
        columns = pl.ds(head * HD, HD)
        column = jnp.broadcast_to(sums[:, head : head + 1], (rows, rows))
        across = jnp.sum(jnp.where(same, column, 0.0), axis=0, keepdims=True)
        spread = jnp.exp(jnp.minimum(column - across, 0.0))
        scores = dot(q_ref[:, columns], k_ref[:, columns], ((1,), (1,)))
        weights = jnp.where(below, spread * scores, 0.0).astype(BF16)
        inside_ref[:, columns] = dot(weights, v_ref[:, columns], ((1,), (0,)))


def finish(
    part_ref, part_other_ref, q_ref, gate_ref, inside_ref, factor_ref, keep_ref, other_ref,
    o_ret, o_cross, held, ret_held, cross_held, sems,
):
    merge(part_ref, part_other_ref, cross_held)
    cross_out = pltpu.make_async_copy(cross_held, o_cross, sems.at[0])
    cross_out.start()
    low, _, _ = bits()
    half = keep_ref.shape[0]
    for ref, which in ((keep_ref, low), (other_ref, 1 - low)):
        held[pl.ds(pl.multiple_of(which * half, half), half), :] = ref[...]
    for head in range(factor_ref.shape[1]):
        columns = pl.ds(head * HD, HD)
        before = dot(q_ref[:, columns], held[:, columns], ((1,), (0,)))
        retained = inside_ref[:, columns] + factor_ref[:, head : head + 1] * before
        scale = lax.rsqrt(jnp.mean(retained * retained, axis=1, keepdims=True) + EPS)
        gate = gate_ref[:, columns].astype(F32)
        silu = gate / (1.0 + jnp.exp(-gate))
        ret_held[:, columns] = (retained * scale * silu).astype(BF16)
    ret_out = pltpu.make_async_copy(ret_held, o_ret, sems.at[1])
    ret_out.start()
    cross_out.wait()
    ret_out.wait()


def copy_after(source, out):
    out[...] = source[...]


def attend(hops, last, sides, *refs):
    count = len(hops)
    queries, refs = refs[: len(sides)], refs[len(sides) :]
    blocks, refs = refs[: 2 * count], refs[2 * count :]
    taken = 2 * len(sides) if last else 0
    carried, refs = refs[:taken], refs[taken:]
    outs, (keys, values) = refs[:-2], refs[-2:]
    rows, wide = queries[0].shape
    heads = wide // HD
    length, width = blocks[0].shape[0], blocks[0].shape[1] // 2
    group = wide // width
    total = 2 * count * length
    low, high, depth = bits()
    for i, block in enumerate(blocks):
        keys[pl.ds(i * length, length), :] = block[:, pl.ds(0, width)]
        values[pl.ds(i * length, length), :] = block[:, pl.ds(width, width)]
    column = lax.broadcasted_iota(jnp.int32, (1, total), 1)
    limit = jnp.zeros((1, total), jnp.int32)
    for i in range(2 * count):
        s, t = hops[i // 2], i % 2
        if s == 0:
            core = low if t == 0 else 1 - low
            at = column + ((2 * high + core) * length - i * length)
        else:
            at = jnp.where(jnp.bitwise_xor(depth, s) < depth, -1, 4 * rows)
        limit = jnp.where(column >= i * length, at, limit)
    scale = 1.0 / (math.sqrt(HD) * math.log(2.0))
    row = lax.broadcasted_iota(jnp.int32, (rows, total), 0)
    lane = lax.broadcasted_iota(jnp.int32, (rows, LANES), 1)
    for which, (query, side) in enumerate(zip(queries, sides)):
        place = jnp.bitwise_xor(high, side)
        allowed = row + (2 * place + low) * rows >= limit
        stats = jnp.zeros((rows, LANES), F32)
        if last:
            mixed_ref, stats_ref = carried[2 * which : 2 * which + 2]
            out = outs[which]
        else:
            out, stats_out = outs[2 * which : 2 * which + 2]
        for head in range(heads):
            columns = pl.ds(head * HD, HD)
            shared = pl.ds((head // group) * HD, HD)
            scores = dot(query[:, columns], keys[:, shared], ((1,), (1,))) * scale
            masked = jnp.where(allowed, scores, FAR)
            top = jnp.maximum(jnp.max(masked, axis=1, keepdims=True), NEAR)
            if last:
                old = stats_ref[:, 2 * head : 2 * head + 1]
                top = jnp.maximum(top, old)
            weights = jnp.exp2(masked - top)
            summed = jnp.sum(weights, axis=1, keepdims=True)
            mixed = dot(weights.astype(BF16), values[:, shared], ((1,), (0,)))
            if not last:
                out[:, columns] = mixed
                stats = jnp.where(lane == 2 * head, top, stats)
                stats = jnp.where(lane == 2 * head + 1, summed, stats)
                continue
            shrink = jnp.exp2(old - top)
            summed = summed + shrink * stats_ref[:, 2 * head + 1 : 2 * head + 2]
            mixed = mixed + shrink * mixed_ref[:, columns]
            some = summed > 0.0
            safe = jnp.where(some, summed, 1.0)
            out[:, columns] = (mixed / safe).astype(out.dtype)
            level = jnp.where(some, top + jnp.log2(safe), FAR)
            for i, third in enumerate(thirds(level)):
                stats = jnp.where(lane == 3 * head + i, third, stats)
        if last:
            out[:, pl.ds(wide, LANES)] = stats.astype(out.dtype)
        else:
            stats_out[...] = stats


def merge(keep_ref, other_ref, out):
    wide = out.shape[1]
    ins = (keep_ref, other_ref)
    stats = [ref[:, pl.ds(wide, LANES)].astype(F32) for ref in ins]
    for head in range(wide // HD):
        columns = pl.ds(head * HD, HD)
        levels = [
            tile[:, 3 * head : 3 * head + 1]
            + tile[:, 3 * head + 1 : 3 * head + 2]
            + tile[:, 3 * head + 2 : 3 * head + 3]
            for tile in stats
        ]
        top = functools.reduce(jnp.maximum, levels)
        weights = [jnp.exp2(level - top) for level in levels]
        share = 1.0 / functools.reduce(jnp.add, weights)
        mixed = functools.reduce(
            jnp.add, [(w * share) * ref[:, columns].astype(F32) for w, ref in zip(weights, ins)]
        )
        out[:, columns] = mixed.astype(BF16)


def per_device(count, n, q_ret, k_ret, v_ret, gate_ret, log_decay, q_cross, cache_k, cache_v):
    far = count // 4
    rows, wide = q_cross.shape
    heads = wide // HD
    length, width = cache_k.shape[0], cache_k.shape[1] // n
    half, quarter = HD // 2, HD // 4

    def swap(value, bit):
        return lax.ppermute(value, "ctx", [(b, b ^ bit) for b in range(count)])

    def to_head(value, e):
        return lax.ppermute(value, "head", [(y, (y + e) % n) for y in range(n)])

    plain = (k_ret, v_ret, log_decay.T, q_ret, q_cross, gate_ret)
    loaded = call(
        functools.partial(load_all, n, 2 + len(plain)),
        [pltpu.VMEM((length, 2 * width), BF16)] * n + [pltpu.VMEM(a.shape, a.dtype) for a in plain],
        [pltpu.with_memory_space_constraint(a, pltpu.HBM) for a in (cache_k, cache_v, *plain)],
        scratch=[pltpu.SemaphoreType.DMA((2 * n + len(plain),))],
        name="load_all",
        takes=HBM,
    )
    pieces = loaded[:n]
    k_ret, v_ret, decays, q_ret, q_cross, gate_ret = loaded[n:]
    arrived = [pieces[0]] + [to_head(pieces[e], e) for e in range(1, n)]
    sum_send, sum_keep = call(
        summarize,
        [shape((half + PAD, wide)), shape((half + PAD, wide), F32)],
        (k_ret, v_ret, decays),
        scratch=[pltpu.VMEM((HD, wide), F32)],
        name="summarize",
        flops=3000000000,
    )
    sum_other = swap(sum_send, 1)
    chip_send, chip_keep = call(
        chip_total,
        [shape((quarter + PAD, wide)), shape((quarter + PAD, wide), F32)],
        (sum_keep, sum_other),
        scratch=[pltpu.VMEM((half, wide), F32)],
        name="chip_total",
    )
    inside, factor = call(
        retain_inside,
        [shape((rows, wide), F32), shape((rows, heads), F32)],
        (q_ret, k_ret, v_ret, decays),
        name="retain_inside",
        after=(chip_send,),
    )
    blocks = {
        0: call(
            functools.partial(join_rows, n),
            [shape((n * length, 2 * width))],
            arrived,
            name="join_rows",
            flops=3000000000,
        )
    }
    chip_other = swap(chip_send, 2)
    q_other = swap(q_cross, 2)
    bit = far // 2
    while bit > 1:
        for s in list(blocks):
            blocks[s ^ bit] = swap(blocks[s], 4 * bit)
        bit //= 2
    window, handed = call(
        plane_total,
        [shape((quarter + PAD, wide)), shape(blocks[0].shape)],
        (chip_keep, chip_other, blocks[0]),
        name="plane_total",
        after=(factor,),
    )
    blocks[1] = swap(handed, 4)
    planes, bit = [], 1
    while bit < far:
        planes.append(swap(window, 4 * bit))
        if 2 * bit < far:
            window = call(
                functools.partial(grow, bit),
                [shape(window.shape)],
                (window, planes[-1]),
                name="grow",
                flops=3000000000,
                after=(q_other, *[blocks[s] for s in blocks if s]),
            )
        bit *= 2

    def look(hops, last, outs, queries, carried, name):
        keys = 2 * len(hops) * n * length
        both = []
        for s in hops:
            if s not in swapped:
                swapped[s] = swap(blocks[s], 1)
            both += [blocks[s], swapped[s]]
        return call(
            functools.partial(attend, hops, last, [side for _, side in queries]),
            outs,
            (*[query for query, _ in queries], *both, *carried),
            scratch=[pltpu.VMEM((keys, width), BF16) for _ in range(2)],
            name=name,
        )

    swapped = {}
    near = list(blocks)
    so_far = look(
        near,
        False,
        [shape((rows, wide), F32), shape((rows, LANES), F32)] * 2,
        ((q_other, 1), (q_cross, 0)),
        (),
        "attend_near",
    )
    prior_send, prior_keep = call(
        chip_priors,
        [shape((quarter, wide)), shape((quarter, wide), F32)],
        (chip_keep, chip_other, *planes),
        name="chip_priors",
        after=so_far[1:2],
    )
    for s in near:
        if s > 1:
            ready = call(copy_after, [shape(blocks[s].shape)], (blocks[s],), after=(window,))
            blocks[s ^ 1] = pass_on(swap(ready, 4), prior_send)
    hops = [s for s in blocks if s not in near]
    packed = (rows, wide + LANES)
    part_send = look(hops, True, [shape(packed)], ((q_other, 1),), so_far[:2], "attend_far")
    part_keep = look(hops, True, [shape(packed, F32)], ((q_cross, 0),), so_far[2:], "attend_own")
    part_other = swap(part_send, 2)
    prior_other = swap(prior_send, 2)
    state_send, state_keep = call(
        block_priors,
        [shape((half, wide)), shape((half, wide))],
        (sum_keep, sum_other, prior_keep, prior_other),
        scratch=[pltpu.VMEM((half, wide), F32)],
        name="block_priors",
    )
    state_other = swap(state_send, 1)
    held = pltpu.VMEM((rows, wide), BF16)
    return call(
        finish,
        [shape((rows, wide))] * 2,
        (part_keep, part_other, q_ret, gate_ret, inside, factor, state_keep, state_other),
        scratch=[pltpu.VMEM((HD, wide), BF16), held, held, pltpu.SemaphoreType.DMA((2,))],
        name="finish",
        gives=HBM,
    )


def solution(mesh):
    split = P("ctx", "head")
    rows = P(("ctx", "head"), None)
    return jax.shard_map(
        functools.partial(per_device, mesh.shape["ctx"], mesh.shape["head"]),
        mesh=mesh,
        in_specs=(split,) * 6 + (rows,) * 2,
        out_specs=(split, split),
        check_vma=False,
    )
```

```python
import functools
import math

import jax
import jax.numpy as jnp
from jax import lax
from jax.experimental import pallas as pl
from jax.experimental.pallas import tpu as pltpu
from jax.sharding import PartitionSpec as P

HD = 256
FAR = -1e30
NEAR = -1e29
EPS = 1e-06
F32 = jnp.float32
BF16 = jnp.bfloat16
PAD = 16
LANES = 128
VMEM = pl.BlockSpec(memory_space=pltpu.VMEM)
ANY = pl.BlockSpec(memory_space=pl.ANY)
HBM = pl.BlockSpec(memory_space=pltpu.HBM)


def call(
    body, outs, args, scratch=(), name=None, flops=1000, takes=VMEM, gives=VMEM, after=(),
    aliases=None,
):
    single = len(outs) == 1
    used, total = len(args), len(args) + len(after)

    def kernel(*refs):
        body(*refs[:used], *refs[total:])

    return pl.pallas_call(
        kernel,
        out_shape=outs[0] if single else tuple(outs),
        in_specs=(takes if isinstance(takes, list) else [takes] * used) + [ANY] * len(after),
        out_specs=gives if single or isinstance(gives, tuple) else tuple(gives for _ in outs),
        scratch_shapes=scratch,
        input_output_aliases=aliases or {},
        compiler_params=pltpu.CompilerParams(vmem_limit_bytes=40 * 1024 * 1024),
        cost_estimate=pl.CostEstimate(flops=flops, bytes_accessed=1000, transcendentals=0),
        name=name,
    )(*args, *after)


def pass_on(value, *after):
    return call(
        lambda *refs: None,
        [shape(value.shape, value.dtype)],
        (value,),
        name="pass_on",
        takes=ANY,
        gives=ANY,
        after=after,
        aliases={0: 0},
    )


def shape(dims, dtype=BF16):
    return jax.ShapeDtypeStruct(dims, dtype)


def dot(a, b, contract, precision=None):
    return lax.dot_general(
        a, b, (contract, ((), ())), preferred_element_type=F32, precision=precision
    )


def thirds(value):
    high = value.astype(BF16).astype(F32)
    rest = value - high
    middle = rest.astype(BF16).astype(F32)
    return high, middle, rest - middle


def lower_ones(rows):
    below = lax.broadcasted_iota(jnp.int32, (rows, rows), 0) >= lax.broadcasted_iota(
        jnp.int32, (rows, rows), 1
    )
    return below, jnp.where(below, 1.0, 0.0).astype(F32)


def join_rows(n, *refs):
    pieces, out = refs[:n], refs[n]
    length = pieces[0].shape[0]
    here = lax.axis_index("head")
    for e, piece in enumerate(pieces):
        place = lax.rem(here + n - e, n)
        out[pl.ds(pl.multiple_of(place * length, PAD), length), :] = piece[...]


def bits():
    index = lax.axis_index("ctx")
    low = lax.rem(index, 2)
    return low, lax.rem(lax.div(index, 2), 2), lax.div(index, 4)


def put_total(out, at, total):
    wide = out.shape[1]
    if out.dtype == F32:
        out[pl.ds(at, PAD), :] = jnp.broadcast_to(total, (PAD, wide))
        return
    row = lax.broadcasted_iota(jnp.int32, (PAD, wide), 0)
    high, middle, low = thirds(total)
    tile = jnp.where(row == 0, high, jnp.where(row == 1, middle, jnp.where(row == 2, low, 0.0)))
    out[pl.ds(at, PAD), :] = tile.astype(out.dtype)


def total_of(ref):
    tile = ref[pl.ds(ref.shape[0] - PAD, PAD), :].astype(F32)
    if ref.dtype == F32:
        return tile[0:1, :]
    return tile[0:1, :] + tile[1:2, :] + tile[2:3, :]


def state_of(ref):
    return ref[pl.ds(0, ref.shape[0] - PAD), :].astype(F32)


def part_of(held, which, rows):
    return held[pl.ds(pl.multiple_of(which * rows, rows), rows), :]


def summarize(k_ref, v_ref, d_ref, send, keep, held):
    low, _, _ = bits()
    half = HD // 2
    rows = d_ref.shape[1]
    sums = dot(lower_ones(rows)[1], d_ref[...], ((1,), (1,)), lax.Precision.HIGHEST)
    totals = []
    for head in range(d_ref.shape[0]):
        columns = pl.ds(head * HD, HD)
        column = sums[:, head : head + 1]
        last = column[rows - 1 : rows, :]
        carried = (k_ref[:, columns].astype(F32) * jnp.exp(last - column)).astype(BF16)
        held[:, columns] = dot(carried, v_ref[:, columns], ((0,), (0,)))
        totals.append(jnp.broadcast_to(last, (1, HD)))
    total = jnp.concatenate(totals, axis=1)
    for out, which in ((send, 1 - low), (keep, low)):
        out[pl.ds(0, half), :] = part_of(held, which, half).astype(out.dtype)
        put_total(out, half, total)


def load_all(n, count, *refs):
    k_ref, v_ref, *plain = refs[:count]
    outs, (held, sems) = refs[count:-2], refs[-2:]
    pieces, copies, (send, keep) = outs[:n], outs[n:-2], outs[-2:]
    width = k_ref.shape[1] // n
    here = lax.axis_index("head")
    moves = list(zip(plain, copies))
    for e, piece in enumerate(pieces):
        target = lax.rem(here + e, n)
        columns = pl.ds(pl.multiple_of(target * width, LANES), width)
        moves.append((k_ref.at[:, columns], piece.at[:, pl.ds(0, width)]))
        moves.append((v_ref.at[:, columns], piece.at[:, pl.ds(width, width)]))
    running = [pltpu.make_async_copy(a, b, sems.at[i]) for i, (a, b) in enumerate(moves)]
    for one in running:
        one.start()
    for one in running[:3]:
        one.wait()
    summarize(*copies[:3], send, keep, held)
    for one in running[3:]:
        one.wait()


def pair_total(first, keep_ref, other_ref):
    kept, other = state_of(keep_ref), state_of(other_ref)
    kept_total, other_total = total_of(keep_ref), total_of(other_ref)
    late = jnp.where(first, other_total, kept_total)
    earlier, later = jnp.where(first, kept, other), jnp.where(first, other, kept)
    return jnp.exp(late) * earlier + later, kept_total + other_total


def chip_total(keep_ref, other_ref, send, keep, held):
    low, high, _ = bits()
    quarter = HD // 4
    held[...], total = pair_total(low == 0, keep_ref, other_ref)
    for out, which in ((send, 1 - high), (keep, high)):
        out[pl.ds(0, quarter), :] = part_of(held, which, quarter).astype(out.dtype)
        put_total(out, quarter, total)


def plane_total(keep_ref, other_ref, block_ref, out, block_out):
    block_out[...] = block_ref[...]
    _, high, _ = bits()
    state, total = pair_total(high == 0, keep_ref, other_ref)
    out[pl.ds(0, state.shape[0]), :] = state.astype(out.dtype)
    put_total(out, state.shape[0], total)


def chip_priors(keep_ref, other_ref, *refs):
    planes, send, keep = refs[:-2], refs[-2], refs[-1]
    _, high, depth = bits()
    entering = jnp.zeros(send.shape, F32)
    between = jnp.zeros((1, send.shape[1]), F32)
    for i, ref in enumerate(planes):
        earlier = lax.rem(lax.div(depth, 2**i), 2) == 1
        entering = entering + jnp.where(earlier, jnp.exp(between) * state_of(ref), 0.0)
        between = between + jnp.where(earlier, total_of(ref), 0.0)
    first = high == 0
    early = jnp.where(first, state_of(keep_ref), state_of(other_ref))
    early_total = jnp.where(first, total_of(keep_ref), total_of(other_ref))
    second = jnp.exp(early_total) * entering + early
    send[...] = jnp.where(first, second, entering).astype(send.dtype)
    keep[...] = jnp.where(first, entering, second).astype(keep.dtype)


def block_priors(keep_ref, other_ref, prior_ref, prior_other_ref, send, keep, held):
    low, high, _ = bits()
    quarter = prior_ref.shape[0]
    for ref, which in ((prior_ref, high), (prior_other_ref, 1 - high)):
        held[pl.ds(pl.multiple_of(which * quarter, quarter), quarter), :] = ref[...].astype(F32)
    first = low == 0
    early = jnp.where(first, state_of(keep_ref), state_of(other_ref))
    early_total = jnp.where(first, total_of(keep_ref), total_of(other_ref))
    entering = held[...]
    second = jnp.exp(early_total) * entering + early
    send[...] = jnp.where(first, second, entering).astype(send.dtype)
    keep[...] = jnp.where(first, entering, second).astype(keep.dtype)


def grow(bit, own_ref, other_ref, out):
    rows = out.shape[0] - PAD
    first = lax.rem(lax.div(bits()[2], bit), 2) == 0
    state, total = pair_total(first, own_ref, other_ref)
    out[pl.ds(0, rows), :] = state.astype(out.dtype)
    put_total(out, rows, total)


def retain_inside(q_ref, k_ref, v_ref, d_ref, inside_ref, factor_ref):
    heads, rows = d_ref.shape
    below, ones = lower_ones(rows)
    sums = dot(ones, d_ref[...], ((1,), (1,)), lax.Precision.HIGHEST)
    same = lax.broadcasted_iota(jnp.int32, (rows, rows), 0) == lax.broadcasted_iota(
        jnp.int32, (rows, rows), 1
    )
    factor_ref[...] = jnp.exp(sums)
    for head in range(heads):
        columns = pl.ds(head * HD, HD)
        column = jnp.broadcast_to(sums[:, head : head + 1], (rows, rows))
        across = jnp.sum(jnp.where(same, column, 0.0), axis=0, keepdims=True)
        spread = jnp.exp(jnp.minimum(column - across, 0.0))
        scores = dot(q_ref[:, columns], k_ref[:, columns], ((1,), (1,)))
        weights = jnp.where(below, spread * scores, 0.0).astype(BF16)
        inside_ref[:, columns] = dot(weights, v_ref[:, columns], ((1,), (0,)))


def finish(
    part_ref, part_other_ref, q_ref, gate_ref, inside_ref, factor_ref, keep_ref, other_ref,
    o_ret, o_cross, held, ret_held, cross_held, sems,
):
    merge(part_ref, part_other_ref, cross_held)
    cross_out = pltpu.make_async_copy(cross_held, o_cross, sems.at[0])
    cross_out.start()
    low, _, _ = bits()
    half = keep_ref.shape[0]
    for ref, which in ((keep_ref, low), (other_ref, 1 - low)):
        held[pl.ds(pl.multiple_of(which * half, half), half), :] = ref[...]
    for head in range(factor_ref.shape[1]):
        columns = pl.ds(head * HD, HD)
        before = dot(q_ref[:, columns], held[:, columns], ((1,), (0,)))
        retained = inside_ref[:, columns] + factor_ref[:, head : head + 1] * before
        scale = lax.rsqrt(jnp.mean(retained * retained, axis=1, keepdims=True) + EPS)
        gate = gate_ref[:, columns].astype(F32)
        silu = gate / (1.0 + jnp.exp(-gate))
        ret_held[:, columns] = (retained * scale * silu).astype(BF16)
    ret_out = pltpu.make_async_copy(ret_held, o_ret, sems.at[1])
    ret_out.start()
    cross_out.wait()
    ret_out.wait()


def copy_after(source, out):
    out[...] = source[...]


def attend(hops, last, sides, *refs):
    count = len(hops)
    queries, refs = refs[: len(sides)], refs[len(sides) :]
    blocks, refs = refs[: 2 * count], refs[2 * count :]
    taken = 2 * len(sides) if last else 0
    carried, refs = refs[:taken], refs[taken:]
    outs, (keys, values) = refs[:-2], refs[-2:]
    rows, wide = queries[0].shape
    heads = wide // HD
    length, width = blocks[0].shape[0], blocks[0].shape[1] // 2
    group = wide // width
    total = 2 * count * length
    low, high, depth = bits()
    for i, block in enumerate(blocks):
        keys[pl.ds(i * length, length), :] = block[:, pl.ds(0, width)]
        values[pl.ds(i * length, length), :] = block[:, pl.ds(width, width)]
    column = lax.broadcasted_iota(jnp.int32, (1, total), 1)
    limit = jnp.zeros((1, total), jnp.int32)
    for i in range(2 * count):
        s, t = hops[i // 2], i % 2
        if s == 0:
            core = low if t == 0 else 1 - low
            at = column + ((2 * high + core) * length - i * length)
        else:
            at = jnp.where(jnp.bitwise_xor(depth, s) < depth, -1, 4 * rows)
        limit = jnp.where(column >= i * length, at, limit)
    scale = 1.0 / (math.sqrt(HD) * math.log(2.0))
    row = lax.broadcasted_iota(jnp.int32, (rows, total), 0)
    lane = lax.broadcasted_iota(jnp.int32, (rows, LANES), 1)
    for which, (query, side) in enumerate(zip(queries, sides)):
        place = jnp.bitwise_xor(high, side)
        allowed = row + (2 * place + low) * rows >= limit
        stats = jnp.zeros((rows, LANES), F32)
        if last:
            mixed_ref, stats_ref = carried[2 * which : 2 * which + 2]
            out = outs[which]
        else:
            out, stats_out = outs[2 * which : 2 * which + 2]
        for head in range(heads):
            columns = pl.ds(head * HD, HD)
            shared = pl.ds((head // group) * HD, HD)
            scores = dot(query[:, columns], keys[:, shared], ((1,), (1,))) * scale
            masked = jnp.where(allowed, scores, FAR)
            top = jnp.maximum(jnp.max(masked, axis=1, keepdims=True), NEAR)
            if last:
                old = stats_ref[:, 2 * head : 2 * head + 1]
                top = jnp.maximum(top, old)
            weights = jnp.exp2(masked - top)
            summed = jnp.sum(weights, axis=1, keepdims=True)
            mixed = dot(weights.astype(BF16), values[:, shared], ((1,), (0,)))
            if not last:
                out[:, columns] = mixed
                stats = jnp.where(lane == 2 * head, top, stats)
                stats = jnp.where(lane == 2 * head + 1, summed, stats)
                continue
            shrink = jnp.exp2(old - top)
            summed = summed + shrink * stats_ref[:, 2 * head + 1 : 2 * head + 2]
            mixed = mixed + shrink * mixed_ref[:, columns]
            some = summed > 0.0
            safe = jnp.where(some, summed, 1.0)
            out[:, columns] = (mixed / safe).astype(out.dtype)
            level = jnp.where(some, top + jnp.log2(safe), FAR)
            for i, third in enumerate(thirds(level)):
                stats = jnp.where(lane == 3 * head + i, third, stats)
        if last:
            out[:, pl.ds(wide, LANES)] = stats.astype(out.dtype)
        else:
            stats_out[...] = stats


def merge(keep_ref, other_ref, out):
    wide = out.shape[1]
    ins = (keep_ref, other_ref)
    stats = [ref[:, pl.ds(wide, LANES)].astype(F32) for ref in ins]
    for head in range(wide // HD):
        columns = pl.ds(head * HD, HD)
        levels = [
            tile[:, 3 * head : 3 * head + 1]
            + tile[:, 3 * head + 1 : 3 * head + 2]
            + tile[:, 3 * head + 2 : 3 * head + 3]
            for tile in stats
        ]
        top = functools.reduce(jnp.maximum, levels)
        weights = [jnp.exp2(level - top) for level in levels]
        share = 1.0 / functools.reduce(jnp.add, weights)
        mixed = functools.reduce(
            jnp.add, [(w * share) * ref[:, columns].astype(F32) for w, ref in zip(weights, ins)]
        )
        out[:, columns] = mixed.astype(BF16)


def per_device(count, n, q_ret, k_ret, v_ret, gate_ret, log_decay, q_cross, cache_k, cache_v):
    far = count // 4
    rows, wide = q_cross.shape
    heads = wide // HD
    length, width = cache_k.shape[0], cache_k.shape[1] // n
    half, quarter = HD // 2, HD // 4

    def swap(value, bit):
        return lax.ppermute(value, "ctx", [(b, b ^ bit) for b in range(count)])

    def to_head(value, e):
        return lax.ppermute(value, "head", [(y, (y + e) % n) for y in range(n)])

    plain = (k_ret, v_ret, log_decay.T, q_ret, q_cross, gate_ret)
    loaded = call(
        functools.partial(load_all, n, 2 + len(plain)),
        [pltpu.VMEM((length, 2 * width), BF16)] * n
        + [pltpu.VMEM(a.shape, a.dtype) for a in plain]
        + [pltpu.VMEM((half + PAD, wide), BF16), pltpu.VMEM((half + PAD, wide), F32)],
        [pltpu.with_memory_space_constraint(a, pltpu.HBM) for a in (cache_k, cache_v, *plain)],
        scratch=[pltpu.VMEM((HD, wide), F32), pltpu.SemaphoreType.DMA((2 * n + len(plain),))],
        name="load_all",
        takes=HBM,
    )
    pieces = loaded[:n]
    k_ret, v_ret, decays, q_ret, q_cross, gate_ret, sum_send, sum_keep = loaded[n:]
    arrived = [pieces[0]] + [to_head(pieces[e], e) for e in range(1, n)]
    sum_other = swap(sum_send, 1)
    chip_send, chip_keep = call(
        chip_total,
        [shape((quarter + PAD, wide)), shape((quarter + PAD, wide), F32)],
        (sum_keep, sum_other),
        scratch=[pltpu.VMEM((half, wide), F32)],
        name="chip_total",
    )
    inside, factor = call(
        retain_inside,
        [shape((rows, wide), F32), shape((rows, heads), F32)],
        (q_ret, k_ret, v_ret, decays),
        name="retain_inside",
        after=(chip_send,),
    )
    blocks = {
        0: call(
            functools.partial(join_rows, n),
            [shape((n * length, 2 * width))],
            arrived,
            name="join_rows",
            flops=3000000000,
        )
    }
    chip_other = swap(chip_send, 2)
    bit = far // 2
    while bit > 1:
        for s in list(blocks):
            blocks[s ^ bit] = swap(blocks[s], 4 * bit)
        bit //= 2
    window, handed = call(
        plane_total,
        [shape((quarter + PAD, wide)), shape(blocks[0].shape)],
        (chip_keep, chip_other, blocks[0]),
        name="plane_total",
        after=(factor,),
    )
    blocks[1] = swap(handed, 4)
    q_cross = pass_on(q_cross, blocks[far // 2])
    q_other = swap(q_cross, 2)
    planes, bit = [], 1
    while bit < far:
        planes.append(swap(window, 4 * bit))
        if 2 * bit < far:
            window = call(
                functools.partial(grow, bit),
                [shape(window.shape)],
                (window, planes[-1]),
                name="grow",
                flops=3000000000,
                after=tuple(blocks[s] for s in blocks if s),
            )
        bit *= 2

    def look(hops, last, outs, queries, carried, name):
        keys = 2 * len(hops) * n * length
        both = []
        for s in hops:
            if s not in swapped:
                swapped[s] = swap(blocks[s], 1)
            both += [blocks[s], swapped[s]]
        return call(
            functools.partial(attend, hops, last, [side for _, side in queries]),
            outs,
            (*[query for query, _ in queries], *both, *carried),
            scratch=[pltpu.VMEM((keys, width), BF16) for _ in range(2)],
            name=name,
        )

    swapped = {}
    near = list(blocks)
    so_far = look(
        near,
        False,
        [shape((rows, wide), F32), shape((rows, LANES), F32)] * 2,
        ((q_other, 1), (q_cross, 0)),
        (),
        "attend_near",
    )
    prior_send, prior_keep = call(
        chip_priors,
        [shape((quarter, wide)), shape((quarter, wide), F32)],
        (chip_keep, chip_other, *planes),
        name="chip_priors",
        after=so_far[1:2],
    )
    for s in near:
        if s > 1:
            ready = call(copy_after, [shape(blocks[s].shape)], (blocks[s],), after=(window,))
            blocks[s ^ 1] = pass_on(swap(ready, 4), prior_send)
    hops = [s for s in blocks if s not in near]
    packed = (rows, wide + LANES)
    part_send = look(hops, True, [shape(packed)], ((q_other, 1),), so_far[:2], "attend_far")
    part_keep = look(hops, True, [shape(packed, F32)], ((q_cross, 0),), so_far[2:], "attend_own")
    part_other = swap(part_send, 2)
    prior_other = swap(prior_send, 2)
    state_send, state_keep = call(
        block_priors,
        [shape((half, wide)), shape((half, wide))],
        (sum_keep, sum_other, prior_keep, prior_other),
        scratch=[pltpu.VMEM((half, wide), F32)],
        name="block_priors",
    )
    state_other = swap(state_send, 1)
    held = pltpu.VMEM((rows, wide), BF16)
    return call(
        finish,
        [shape((rows, wide))] * 2,
        (part_keep, part_other, q_ret, gate_ret, inside, factor, state_keep, state_other),
        scratch=[pltpu.VMEM((HD, wide), BF16), held, held, pltpu.SemaphoreType.DMA((2,))],
        name="finish",
        gives=HBM,
    )


def solution(mesh):
    split = P("ctx", "head")
    rows = P(("ctx", "head"), None)
    return jax.shard_map(
        functools.partial(per_device, mesh.shape["ctx"], mesh.shape["head"]),
        mesh=mesh,
        in_specs=(split,) * 6 + (rows,) * 2,
        out_specs=(split, split),
        check_vma=False,
    )
```

```python
import functools
import math

import jax
import jax.numpy as jnp
from jax import lax
from jax.experimental import pallas as pl
from jax.experimental.pallas import tpu as pltpu
from jax.sharding import PartitionSpec as P

HD = 256
FAR = -1e30
NEAR = -1e29
EPS = 1e-06
F32 = jnp.float32
BF16 = jnp.bfloat16
PAD = 16
LANES = 128
VMEM = pl.BlockSpec(memory_space=pltpu.VMEM)
ANY = pl.BlockSpec(memory_space=pl.ANY)
HBM = pl.BlockSpec(memory_space=pltpu.HBM)


def call(
    body, outs, args, scratch=(), name=None, flops=1000, takes=VMEM, gives=VMEM, after=(),
    aliases=None,
):
    single = len(outs) == 1
    used, total = len(args), len(args) + len(after)

    def kernel(*refs):
        body(*refs[:used], *refs[total:])

    return pl.pallas_call(
        kernel,
        out_shape=outs[0] if single else tuple(outs),
        in_specs=(takes if isinstance(takes, list) else [takes] * used) + [ANY] * len(after),
        out_specs=gives if single or isinstance(gives, tuple) else tuple(gives for _ in outs),
        scratch_shapes=scratch,
        input_output_aliases=aliases or {},
        compiler_params=pltpu.CompilerParams(vmem_limit_bytes=40 * 1024 * 1024),
        cost_estimate=pl.CostEstimate(flops=flops, bytes_accessed=1000, transcendentals=0),
        name=name,
    )(*args, *after)


def pass_on(value, *after):
    return call(
        lambda *refs: None,
        [shape(value.shape, value.dtype)],
        (value,),
        name="pass_on",
        takes=ANY,
        gives=ANY,
        after=after,
        aliases={0: 0},
    )


def shape(dims, dtype=BF16):
    return jax.ShapeDtypeStruct(dims, dtype)


def dot(a, b, contract, precision=None):
    return lax.dot_general(
        a, b, (contract, ((), ())), preferred_element_type=F32, precision=precision
    )


def thirds(value):
    high = value.astype(BF16).astype(F32)
    rest = value - high
    middle = rest.astype(BF16).astype(F32)
    return high, middle, rest - middle


def lower_ones(rows):
    below = lax.broadcasted_iota(jnp.int32, (rows, rows), 0) >= lax.broadcasted_iota(
        jnp.int32, (rows, rows), 1
    )
    return below, jnp.where(below, 1.0, 0.0).astype(F32)


def join_rows(n, *refs):
    pieces, out = refs[:n], refs[n]
    length = pieces[0].shape[0]
    here = lax.axis_index("head")
    for e, piece in enumerate(pieces):
        place = lax.rem(here + n - e, n)
        out[pl.ds(pl.multiple_of(place * length, PAD), length), :] = piece[...]


def bits():
    index = lax.axis_index("ctx")
    low = lax.rem(index, 2)
    return low, lax.rem(lax.div(index, 2), 2), lax.div(index, 4)


def put_total(out, at, total):
    wide = out.shape[1]
    if out.dtype == F32:
        out[pl.ds(at, PAD), :] = jnp.broadcast_to(total, (PAD, wide))
        return
    row = lax.broadcasted_iota(jnp.int32, (PAD, wide), 0)
    high, middle, low = thirds(total)
    tile = jnp.where(row == 0, high, jnp.where(row == 1, middle, jnp.where(row == 2, low, 0.0)))
    out[pl.ds(at, PAD), :] = tile.astype(out.dtype)


def total_of(ref):
    tile = ref[pl.ds(ref.shape[0] - PAD, PAD), :].astype(F32)
    if ref.dtype == F32:
        return tile[0:1, :]
    return tile[0:1, :] + tile[1:2, :] + tile[2:3, :]


def state_of(ref):
    return ref[pl.ds(0, ref.shape[0] - PAD), :].astype(F32)


def part_of(held, which, rows):
    return held[pl.ds(pl.multiple_of(which * rows, rows), rows), :]


def summarize(k_ref, v_ref, d_ref, send, keep, held):
    low, _, _ = bits()
    half = HD // 2
    rows = d_ref.shape[1]
    sums = dot(lower_ones(rows)[1], d_ref[...], ((1,), (1,)), lax.Precision.HIGHEST)
    totals = []
    for head in range(d_ref.shape[0]):
        columns = pl.ds(head * HD, HD)
        column = sums[:, head : head + 1]
        last = column[rows - 1 : rows, :]
        carried = (k_ref[:, columns].astype(F32) * jnp.exp(last - column)).astype(BF16)
        held[:, columns] = dot(carried, v_ref[:, columns], ((0,), (0,)))
        totals.append(jnp.broadcast_to(last, (1, HD)))
    total = jnp.concatenate(totals, axis=1)
    for out, which in ((send, 1 - low), (keep, low)):
        out[pl.ds(0, half), :] = part_of(held, which, half).astype(out.dtype)
        put_total(out, half, total)


def load_all(n, count, *refs):
    k_ref, v_ref, *plain = refs[:count]
    outs, (held, sems) = refs[count:-2], refs[-2:]
    pieces, copies, (send, keep) = outs[:n], outs[n:-2], outs[-2:]
    width = k_ref.shape[1] // n
    here = lax.axis_index("head")
    moves = list(zip(plain, copies))
    for e, piece in enumerate(pieces):
        target = lax.rem(here + e, n)
        columns = pl.ds(pl.multiple_of(target * width, LANES), width)
        moves.append((k_ref.at[:, columns], piece.at[:, pl.ds(0, width)]))
        moves.append((v_ref.at[:, columns], piece.at[:, pl.ds(width, width)]))
    running = [pltpu.make_async_copy(a, b, sems.at[i]) for i, (a, b) in enumerate(moves)]
    for one in running:
        one.start()
    for one in running[:3]:
        one.wait()
    summarize(*copies[:3], send, keep, held)
    for one in running[3:]:
        one.wait()


def pair_total(first, keep_ref, other_ref):
    kept, other = state_of(keep_ref), state_of(other_ref)
    kept_total, other_total = total_of(keep_ref), total_of(other_ref)
    late = jnp.where(first, other_total, kept_total)
    earlier, later = jnp.where(first, kept, other), jnp.where(first, other, kept)
    return jnp.exp(late) * earlier + later, kept_total + other_total


def chip_total(keep_ref, other_ref, send, keep, held):
    low, high, _ = bits()
    quarter = HD // 4
    held[...], total = pair_total(low == 0, keep_ref, other_ref)
    for out, which in ((send, 1 - high), (keep, high)):
        out[pl.ds(0, quarter), :] = part_of(held, which, quarter).astype(out.dtype)
        put_total(out, quarter, total)


def plane_total(keep_ref, other_ref, block_ref, out, block_out):
    block_out[...] = block_ref[...]
    _, high, _ = bits()
    state, total = pair_total(high == 0, keep_ref, other_ref)
    out[pl.ds(0, state.shape[0]), :] = state.astype(out.dtype)
    put_total(out, state.shape[0], total)


def chip_priors(keep_ref, other_ref, *refs):
    planes, send, keep = refs[:-2], refs[-2], refs[-1]
    _, high, depth = bits()
    entering = jnp.zeros(send.shape, F32)
    between = jnp.zeros((1, send.shape[1]), F32)
    for i, ref in enumerate(planes):
        earlier = lax.rem(lax.div(depth, 2**i), 2) == 1
        entering = entering + jnp.where(earlier, jnp.exp(between) * state_of(ref), 0.0)
        between = between + jnp.where(earlier, total_of(ref), 0.0)
    first = high == 0
    early = jnp.where(first, state_of(keep_ref), state_of(other_ref))
    early_total = jnp.where(first, total_of(keep_ref), total_of(other_ref))
    second = jnp.exp(early_total) * entering + early
    send[...] = jnp.where(first, second, entering).astype(send.dtype)
    keep[...] = jnp.where(first, entering, second).astype(keep.dtype)


def block_priors(keep_ref, other_ref, prior_ref, prior_other_ref, send, keep, held):
    low, high, _ = bits()
    quarter = prior_ref.shape[0]
    for ref, which in ((prior_ref, high), (prior_other_ref, 1 - high)):
        held[pl.ds(pl.multiple_of(which * quarter, quarter), quarter), :] = ref[...].astype(F32)
    first = low == 0
    early = jnp.where(first, state_of(keep_ref), state_of(other_ref))
    early_total = jnp.where(first, total_of(keep_ref), total_of(other_ref))
    entering = held[...]
    second = jnp.exp(early_total) * entering + early
    send[...] = jnp.where(first, second, entering).astype(send.dtype)
    keep[...] = jnp.where(first, entering, second).astype(keep.dtype)


def grow(bit, own_ref, other_ref, out):
    rows = out.shape[0] - PAD
    first = lax.rem(lax.div(bits()[2], bit), 2) == 0
    state, total = pair_total(first, own_ref, other_ref)
    out[pl.ds(0, rows), :] = state.astype(out.dtype)
    put_total(out, rows, total)


def retain_inside(q_ref, k_ref, v_ref, d_ref, inside_ref, factor_ref):
    heads, rows = d_ref.shape
    below, ones = lower_ones(rows)
    sums = dot(ones, d_ref[...], ((1,), (1,)), lax.Precision.HIGHEST)
    same = lax.broadcasted_iota(jnp.int32, (rows, rows), 0) == lax.broadcasted_iota(
        jnp.int32, (rows, rows), 1
    )
    factor_ref[...] = jnp.exp(sums)
    for head in range(heads):
        columns = pl.ds(head * HD, HD)
        column = jnp.broadcast_to(sums[:, head : head + 1], (rows, rows))
        across = jnp.sum(jnp.where(same, column, 0.0), axis=0, keepdims=True)
        spread = jnp.exp(jnp.minimum(column - across, 0.0))
        scores = dot(q_ref[:, columns], k_ref[:, columns], ((1,), (1,)))
        weights = jnp.where(below, spread * scores, 0.0).astype(BF16)
        inside_ref[:, columns] = dot(weights, v_ref[:, columns], ((1,), (0,)))


def retain_finish(q_ref, gate_ref, inside_ref, factor_ref, keep_ref, other_ref, o_ret, held, done, sem):
    low, _, _ = bits()
    half = keep_ref.shape[0]
    for ref, which in ((keep_ref, low), (other_ref, 1 - low)):
        held[pl.ds(pl.multiple_of(which * half, half), half), :] = ref[...]
    for head in range(factor_ref.shape[1]):
        columns = pl.ds(head * HD, HD)
        before = dot(q_ref[:, columns], held[:, columns], ((1,), (0,)))
        retained = inside_ref[:, columns] + factor_ref[:, head : head + 1] * before
        scale = lax.rsqrt(jnp.mean(retained * retained, axis=1, keepdims=True) + EPS)
        gate = gate_ref[:, columns].astype(F32)
        silu = gate / (1.0 + jnp.exp(-gate))
        done[:, columns] = (retained * scale * silu).astype(BF16)
    out = pltpu.make_async_copy(done, o_ret, sem)
    out.start()
    out.wait()


def finish(part_ref, part_other_ref, o_cross, done, sems):
    wide = done.shape[1]
    moves = []
    for head in range(wide // HD):
        merge(head, part_ref, part_other_ref, done)
        columns = pl.ds(head * HD, HD)
        moves.append(pltpu.make_async_copy(done.at[:, columns], o_cross.at[:, columns], sems.at[head]))
        moves[-1].start()
    for move in moves:
        move.wait()


def copy_after(source, out):
    out[...] = source[...]


def attend(hops, last, sides, *refs):
    count = len(hops)
    queries, refs = refs[: len(sides)], refs[len(sides) :]
    blocks, refs = refs[: 2 * count], refs[2 * count :]
    taken = 2 * len(sides) if last else 0
    carried, refs = refs[:taken], refs[taken:]
    outs, (keys, values) = refs[:-2], refs[-2:]
    rows, wide = queries[0].shape
    heads = wide // HD
    length, width = blocks[0].shape[0], blocks[0].shape[1] // 2
    group = wide // width
    total = 2 * count * length
    low, high, depth = bits()
    for i, block in enumerate(blocks):
        keys[pl.ds(i * length, length), :] = block[:, pl.ds(0, width)]
        values[pl.ds(i * length, length), :] = block[:, pl.ds(width, width)]
    column = lax.broadcasted_iota(jnp.int32, (1, total), 1)
    limit = jnp.zeros((1, total), jnp.int32)
    for i in range(2 * count):
        s, t = hops[i // 2], i % 2
        if s == 0:
            core = low if t == 0 else 1 - low
            at = column + ((2 * high + core) * length - i * length)
        else:
            at = jnp.where(jnp.bitwise_xor(depth, s) < depth, -1, 4 * rows)
        limit = jnp.where(column >= i * length, at, limit)
    scale = 1.0 / (math.sqrt(HD) * math.log(2.0))
    row = lax.broadcasted_iota(jnp.int32, (rows, total), 0)
    lane = lax.broadcasted_iota(jnp.int32, (rows, LANES), 1)
    for which, (query, side) in enumerate(zip(queries, sides)):
        place = jnp.bitwise_xor(high, side)
        allowed = row + (2 * place + low) * rows >= limit
        stats = jnp.zeros((rows, LANES), F32)
        if last:
            mixed_ref, stats_ref = carried[2 * which : 2 * which + 2]
            out = outs[which]
        else:
            out, stats_out = outs[2 * which : 2 * which + 2]
        for head in range(heads):
            columns = pl.ds(head * HD, HD)
            shared = pl.ds((head // group) * HD, HD)
            scores = dot(query[:, columns], keys[:, shared], ((1,), (1,))) * scale
            masked = jnp.where(allowed, scores, FAR)
            top = jnp.maximum(jnp.max(masked, axis=1, keepdims=True), NEAR)
            if last:
                old = stats_ref[:, 2 * head : 2 * head + 1]
                top = jnp.maximum(top, old)
            weights = jnp.exp2(masked - top)
            summed = jnp.sum(weights, axis=1, keepdims=True)
            mixed = dot(weights.astype(BF16), values[:, shared], ((1,), (0,)))
            if not last:
                out[:, columns] = mixed
                stats = jnp.where(lane == 2 * head, top, stats)
                stats = jnp.where(lane == 2 * head + 1, summed, stats)
                continue
            shrink = jnp.exp2(old - top)
            summed = summed + shrink * stats_ref[:, 2 * head + 1 : 2 * head + 2]
            mixed = mixed + shrink * mixed_ref[:, columns]
            some = summed > 0.0
            safe = jnp.where(some, summed, 1.0)
            out[:, columns] = (mixed / safe).astype(out.dtype)
            level = jnp.where(some, top + jnp.log2(safe), FAR)
            for i, third in enumerate(thirds(level)):
                stats = jnp.where(lane == 3 * head + i, third, stats)
        if last:
            out[:, pl.ds(wide, LANES)] = stats.astype(out.dtype)
        else:
            stats_out[...] = stats


def merge(head, keep_ref, other_ref, out):
    wide = out.shape[1]
    ins = (keep_ref, other_ref)
    columns = pl.ds(head * HD, HD)
    tiles = [ref[:, pl.ds(wide, LANES)].astype(F32) for ref in ins]
    levels = [
        tile[:, 3 * head : 3 * head + 1]
        + tile[:, 3 * head + 1 : 3 * head + 2]
        + tile[:, 3 * head + 2 : 3 * head + 3]
        for tile in tiles
    ]
    top = functools.reduce(jnp.maximum, levels)
    weights = [jnp.exp2(level - top) for level in levels]
    share = 1.0 / functools.reduce(jnp.add, weights)
    mixed = functools.reduce(
        jnp.add, [(w * share) * ref[:, columns].astype(F32) for w, ref in zip(weights, ins)]
    )
    out[:, columns] = mixed.astype(BF16)


def per_device(count, n, q_ret, k_ret, v_ret, gate_ret, log_decay, q_cross, cache_k, cache_v):
    far = count // 4
    rows, wide = q_cross.shape
    heads = wide // HD
    length, width = cache_k.shape[0], cache_k.shape[1] // n
    half, quarter = HD // 2, HD // 4

    def swap(value, bit):
        return lax.ppermute(value, "ctx", [(b, b ^ bit) for b in range(count)])

    def to_head(value, e):
        return lax.ppermute(value, "head", [(y, (y + e) % n) for y in range(n)])

    plain = (k_ret, v_ret, log_decay.T, q_ret, q_cross, gate_ret)
    loaded = call(
        functools.partial(load_all, n, 2 + len(plain)),
        [pltpu.VMEM((length, 2 * width), BF16)] * n
        + [pltpu.VMEM(a.shape, a.dtype) for a in plain]
        + [pltpu.VMEM((half + PAD, wide), BF16), pltpu.VMEM((half + PAD, wide), F32)],
        [pltpu.with_memory_space_constraint(a, pltpu.HBM) for a in (cache_k, cache_v, *plain)],
        scratch=[pltpu.VMEM((HD, wide), F32), pltpu.SemaphoreType.DMA((2 * n + len(plain),))],
        name="load_all",
        takes=HBM,
    )
    pieces = loaded[:n]
    k_ret, v_ret, decays, q_ret, q_cross, gate_ret, sum_send, sum_keep = loaded[n:]
    arrived = [pieces[0]] + [to_head(pieces[e], e) for e in range(1, n)]
    sum_other = swap(sum_send, 1)
    chip_send, chip_keep = call(
        chip_total,
        [shape((quarter + PAD, wide)), shape((quarter + PAD, wide), F32)],
        (sum_keep, sum_other),
        scratch=[pltpu.VMEM((half, wide), F32)],
        name="chip_total",
    )
    inside, factor = call(
        retain_inside,
        [shape((rows, wide), F32), shape((rows, heads), F32)],
        (q_ret, k_ret, v_ret, decays),
        name="retain_inside",
        after=(chip_send,),
    )
    blocks = {
        0: call(
            functools.partial(join_rows, n),
            [shape((n * length, 2 * width))],
            arrived,
            name="join_rows",
            flops=3000000000,
        )
    }
    chip_other = swap(chip_send, 2)
    bit = far // 2
    while bit > 1:
        for s in list(blocks):
            blocks[s ^ bit] = swap(blocks[s], 4 * bit)
        bit //= 2
    window, handed = call(
        plane_total,
        [shape((quarter + PAD, wide)), shape(blocks[0].shape)],
        (chip_keep, chip_other, blocks[0]),
        name="plane_total",
        after=(factor,),
    )
    blocks[1] = swap(handed, 4)
    q_cross = pass_on(q_cross, blocks[far // 2])
    q_other = swap(q_cross, 2)
    planes, bit = [], 1
    while bit < far:
        planes.append(swap(window, 4 * bit))
        if 2 * bit < far:
            window = call(
                functools.partial(grow, bit),
                [shape(window.shape)],
                (window, planes[-1]),
                name="grow",
                flops=3000000000,
                after=tuple(blocks[s] for s in blocks if s),
            )
        bit *= 2

    def look(hops, last, outs, queries, carried, name):
        keys = 2 * len(hops) * n * length
        both = []
        for s in hops:
            if s not in swapped:
                swapped[s] = swap(blocks[s], 1)
            both += [blocks[s], swapped[s]]
        return call(
            functools.partial(attend, hops, last, [side for _, side in queries]),
            outs,
            (*[query for query, _ in queries], *both, *carried),
            scratch=[pltpu.VMEM((keys, width), BF16) for _ in range(2)],
            name=name,
        )

    swapped = {}
    near = list(blocks)
    so_far = look(
        near,
        False,
        [shape((rows, wide), F32), shape((rows, LANES), F32)] * 2,
        ((q_other, 1), (q_cross, 0)),
        (),
        "attend_near",
    )
    prior_send, prior_keep = call(
        chip_priors,
        [shape((quarter, wide)), shape((quarter, wide), F32)],
        (chip_keep, chip_other, *planes),
        name="chip_priors",
        flops=3000000000,
        after=so_far[1:2],
    )
    for s in near:
        if s > 1:
            ready = call(copy_after, [shape(blocks[s].shape)], (blocks[s],), after=(window,))
            blocks[s ^ 1] = pass_on(swap(ready, 4), prior_send)
    hops = [s for s in blocks if s not in near]
    packed = (rows, wide + LANES)
    part_send = look(hops, True, [shape(packed)], ((q_other, 1),), so_far[:2], "attend_far")
    part_keep = look(hops, True, [shape(packed, F32)], ((q_cross, 0),), so_far[2:], "attend_own")
    part_other = swap(part_send, 2)
    prior_other = swap(prior_send, 2)
    state_send, state_keep = call(
        block_priors,
        [shape((half, wide)), shape((half, wide))],
        (sum_keep, sum_other, prior_keep, prior_other),
        scratch=[pltpu.VMEM((half, wide), F32)],
        name="block_priors",
    )
    state_other = swap(state_send, 1)
    done = pltpu.VMEM((rows, wide), BF16)
    o_ret = call(
        retain_finish,
        [shape((rows, wide))],
        (q_ret, gate_ret, inside, factor, state_keep, state_other),
        scratch=[pltpu.VMEM((HD, wide), BF16), done, pltpu.SemaphoreType.DMA],
        name="retain_finish",
        gives=HBM,
    )
    o_cross = call(
        finish,
        [shape((rows, wide))],
        (part_keep, part_other),
        scratch=[done, pltpu.SemaphoreType.DMA((heads,))],
        name="finish",
        gives=HBM,
    )
    return o_ret, o_cross


def solution(mesh):
    split = P("ctx", "head")
    rows = P(("ctx", "head"), None)
    return jax.shard_map(
        functools.partial(per_device, mesh.shape["ctx"], mesh.shape["head"]),
        mesh=mesh,
        in_specs=(split,) * 6 + (rows,) * 2,
        out_specs=(split, split),
        check_vma=False,
    )
```

```python
import functools
import math

import jax
import jax.numpy as jnp
from jax import lax
from jax.experimental import pallas as pl
from jax.experimental.pallas import tpu as pltpu
from jax.sharding import PartitionSpec as P

HD = 256
FAR = -1e30
NEAR = -1e29
EPS = 1e-06
F32 = jnp.float32
BF16 = jnp.bfloat16
PAD = 16
LANES = 128
VMEM = pl.BlockSpec(memory_space=pltpu.VMEM)
ANY = pl.BlockSpec(memory_space=pl.ANY)
HBM = pl.BlockSpec(memory_space=pltpu.HBM)


def call(
    body, outs, args, scratch=(), name=None, flops=1000, takes=VMEM, gives=VMEM, after=(),
    aliases=None,
):
    single = len(outs) == 1
    used, total = len(args), len(args) + len(after)

    def kernel(*refs):
        body(*refs[:used], *refs[total:])

    return pl.pallas_call(
        kernel,
        out_shape=outs[0] if single else tuple(outs),
        in_specs=(takes if isinstance(takes, list) else [takes] * used) + [ANY] * len(after),
        out_specs=gives if single or isinstance(gives, tuple) else tuple(gives for _ in outs),
        scratch_shapes=scratch,
        input_output_aliases=aliases or {},
        compiler_params=pltpu.CompilerParams(vmem_limit_bytes=40 * 1024 * 1024),
        cost_estimate=pl.CostEstimate(flops=flops, bytes_accessed=1000, transcendentals=0),
        name=name,
    )(*args, *after)


def pass_on(value, *after):
    return call(
        lambda *refs: None,
        [shape(value.shape, value.dtype)],
        (value,),
        name="pass_on",
        takes=ANY,
        gives=ANY,
        after=after,
        aliases={0: 0},
    )


def shape(dims, dtype=BF16):
    return jax.ShapeDtypeStruct(dims, dtype)


def dot(a, b, contract, precision=None):
    return lax.dot_general(
        a, b, (contract, ((), ())), preferred_element_type=F32, precision=precision
    )


def thirds(value):
    high = value.astype(BF16).astype(F32)
    rest = value - high
    middle = rest.astype(BF16).astype(F32)
    return high, middle, rest - middle


def lower_ones(rows):
    below = lax.broadcasted_iota(jnp.int32, (rows, rows), 0) >= lax.broadcasted_iota(
        jnp.int32, (rows, rows), 1
    )
    return below, jnp.where(below, 1.0, 0.0).astype(F32)


def join_rows(n, *refs):
    pieces, out = refs[:n], refs[n]
    length = pieces[0].shape[0]
    here = lax.axis_index("head")
    for e, piece in enumerate(pieces):
        place = lax.rem(here + n - e, n)
        out[pl.ds(pl.multiple_of(place * length, PAD), length), :] = piece[...]


def bits():
    index = lax.axis_index("ctx")
    low = lax.rem(index, 2)
    return low, lax.rem(lax.div(index, 2), 2), lax.div(index, 4)


def put_total(out, at, total):
    wide = out.shape[1]
    if out.dtype == F32:
        out[pl.ds(at, PAD), :] = jnp.broadcast_to(total, (PAD, wide))
        return
    row = lax.broadcasted_iota(jnp.int32, (PAD, wide), 0)
    high, middle, low = thirds(total)
    tile = jnp.where(row == 0, high, jnp.where(row == 1, middle, jnp.where(row == 2, low, 0.0)))
    out[pl.ds(at, PAD), :] = tile.astype(out.dtype)


def total_of(ref):
    tile = ref[pl.ds(ref.shape[0] - PAD, PAD), :].astype(F32)
    if ref.dtype == F32:
        return tile[0:1, :]
    return tile[0:1, :] + tile[1:2, :] + tile[2:3, :]


def state_of(ref):
    return ref[pl.ds(0, ref.shape[0] - PAD), :].astype(F32)


def part_of(held, which, rows):
    return held[pl.ds(pl.multiple_of(which * rows, rows), rows), :]


def summarize(k_ref, v_ref, d_ref, send, keep, held):
    low, _, _ = bits()
    half = HD // 2
    rows = d_ref.shape[1]
    sums = dot(lower_ones(rows)[1], d_ref[...], ((1,), (1,)), lax.Precision.HIGHEST)
    totals = []
    for head in range(d_ref.shape[0]):
        columns = pl.ds(head * HD, HD)
        column = sums[:, head : head + 1]
        last = column[rows - 1 : rows, :]
        carried = (k_ref[:, columns].astype(F32) * jnp.exp(last - column)).astype(BF16)
        held[:, columns] = dot(carried, v_ref[:, columns], ((0,), (0,)))
        totals.append(jnp.broadcast_to(last, (1, HD)))
    total = jnp.concatenate(totals, axis=1)
    for out, which in ((send, 1 - low), (keep, low)):
        out[pl.ds(0, half), :] = part_of(held, which, half).astype(out.dtype)
        put_total(out, half, total)


def load_all(n, count, *refs):
    k_ref, v_ref, *plain = refs[:count]
    outs, (held, sems) = refs[count:-2], refs[-2:]
    pieces, copies, (send, keep) = outs[:n], outs[n:-2], outs[-2:]
    width = k_ref.shape[1] // n
    here = lax.axis_index("head")
    moves = list(zip(plain, copies))
    for e, piece in enumerate(pieces):
        target = lax.rem(here + e, n)
        columns = pl.ds(pl.multiple_of(target * width, LANES), width)
        moves.append((k_ref.at[:, columns], piece.at[:, pl.ds(0, width)]))
        moves.append((v_ref.at[:, columns], piece.at[:, pl.ds(width, width)]))
    running = [pltpu.make_async_copy(a, b, sems.at[i]) for i, (a, b) in enumerate(moves)]
    for one in running:
        one.start()
    for one in running[:3]:
        one.wait()
    summarize(*copies[:3], send, keep, held)
    for one in running[3:]:
        one.wait()


def pair_total(first, keep_ref, other_ref):
    kept, other = state_of(keep_ref), state_of(other_ref)
    kept_total, other_total = total_of(keep_ref), total_of(other_ref)
    late = jnp.where(first, other_total, kept_total)
    earlier, later = jnp.where(first, kept, other), jnp.where(first, other, kept)
    return jnp.exp(late) * earlier + later, kept_total + other_total


def chip_total(keep_ref, other_ref, send, keep, held):
    low, high, _ = bits()
    quarter = HD // 4
    held[...], total = pair_total(low == 0, keep_ref, other_ref)
    for out, which in ((send, 1 - high), (keep, high)):
        out[pl.ds(0, quarter), :] = part_of(held, which, quarter).astype(out.dtype)
        put_total(out, quarter, total)


def plane_total(keep_ref, other_ref, block_ref, out, block_out):
    block_out[...] = block_ref[...]
    _, high, _ = bits()
    state, total = pair_total(high == 0, keep_ref, other_ref)
    out[pl.ds(0, state.shape[0]), :] = state.astype(out.dtype)
    put_total(out, state.shape[0], total)


def chip_priors(keep_ref, other_ref, *refs):
    planes, send, keep = refs[:-2], refs[-2], refs[-1]
    _, high, depth = bits()
    entering = jnp.zeros(send.shape, F32)
    between = jnp.zeros((1, send.shape[1]), F32)
    for i, ref in enumerate(planes):
        earlier = lax.rem(lax.div(depth, 2**i), 2) == 1
        entering = entering + jnp.where(earlier, jnp.exp(between) * state_of(ref), 0.0)
        between = between + jnp.where(earlier, total_of(ref), 0.0)
    first = high == 0
    early = jnp.where(first, state_of(keep_ref), state_of(other_ref))
    early_total = jnp.where(first, total_of(keep_ref), total_of(other_ref))
    second = jnp.exp(early_total) * entering + early
    send[...] = jnp.where(first, second, entering).astype(send.dtype)
    keep[...] = jnp.where(first, entering, second).astype(keep.dtype)


def block_priors(keep_ref, other_ref, prior_ref, prior_other_ref, send, keep, held):
    low, high, _ = bits()
    quarter = prior_ref.shape[0]
    for ref, which in ((prior_ref, high), (prior_other_ref, 1 - high)):
        held[pl.ds(pl.multiple_of(which * quarter, quarter), quarter), :] = ref[...].astype(F32)
    first = low == 0
    early = jnp.where(first, state_of(keep_ref), state_of(other_ref))
    early_total = jnp.where(first, total_of(keep_ref), total_of(other_ref))
    entering = held[...]
    second = jnp.exp(early_total) * entering + early
    send[...] = jnp.where(first, second, entering).astype(send.dtype)
    keep[...] = jnp.where(first, entering, second).astype(keep.dtype)


def grow(bit, own_ref, other_ref, out):
    rows = out.shape[0] - PAD
    first = lax.rem(lax.div(bits()[2], bit), 2) == 0
    state, total = pair_total(first, own_ref, other_ref)
    out[pl.ds(0, rows), :] = state.astype(out.dtype)
    put_total(out, rows, total)


def retain_inside(q_ref, k_ref, v_ref, d_ref, inside_ref, factor_ref):
    heads, rows = d_ref.shape
    below, ones = lower_ones(rows)
    sums = dot(ones, d_ref[...], ((1,), (1,)), lax.Precision.HIGHEST)
    same = lax.broadcasted_iota(jnp.int32, (rows, rows), 0) == lax.broadcasted_iota(
        jnp.int32, (rows, rows), 1
    )
    factor_ref[...] = jnp.exp(sums)
    for head in range(heads):
        columns = pl.ds(head * HD, HD)
        column = jnp.broadcast_to(sums[:, head : head + 1], (rows, rows))
        across = jnp.sum(jnp.where(same, column, 0.0), axis=0, keepdims=True)
        spread = jnp.exp(jnp.minimum(column - across, 0.0))
        scores = dot(q_ref[:, columns], k_ref[:, columns], ((1,), (1,)))
        weights = jnp.where(below, spread * scores, 0.0).astype(BF16)
        inside_ref[:, columns] = dot(weights, v_ref[:, columns], ((1,), (0,)))


def retain_finish(q_ref, gate_ref, inside_ref, factor_ref, keep_ref, other_ref, o_ret, held, done, sem):
    low, _, _ = bits()
    half = keep_ref.shape[0]
    for ref, which in ((keep_ref, low), (other_ref, 1 - low)):
        held[pl.ds(pl.multiple_of(which * half, half), half), :] = ref[...]
    for head in range(factor_ref.shape[1]):
        columns = pl.ds(head * HD, HD)
        before = dot(q_ref[:, columns], held[:, columns], ((1,), (0,)))
        retained = inside_ref[:, columns] + factor_ref[:, head : head + 1] * before
        scale = lax.rsqrt(jnp.mean(retained * retained, axis=1, keepdims=True) + EPS)
        gate = gate_ref[:, columns].astype(F32)
        silu = gate / (1.0 + jnp.exp(-gate))
        done[:, columns] = (retained * scale * silu).astype(BF16)
    out = pltpu.make_async_copy(done, o_ret, sem)
    out.start()
    out.wait()


def finish(part_ref, part_other_ref, o_cross, done, sems):
    wide = done.shape[1]
    moves = []
    for head in range(wide // HD):
        merge(head, part_ref, part_other_ref, done)
        columns = pl.ds(head * HD, HD)
        moves.append(pltpu.make_async_copy(done.at[:, columns], o_cross.at[:, columns], sems.at[head]))
        moves[-1].start()
    for move in moves:
        move.wait()


def copy_after(source, out):
    out[...] = source[...]


def attend(hops, last, sides, *refs):
    count = len(hops)
    queries, refs = refs[: len(sides)], refs[len(sides) :]
    blocks, refs = refs[: 2 * count], refs[2 * count :]
    taken = 2 * len(sides) if last else 0
    carried, refs = refs[:taken], refs[taken:]
    outs, (keys, values) = refs[:-2], refs[-2:]
    rows, wide = queries[0].shape
    heads = wide // HD
    length, width = blocks[0].shape[0], blocks[0].shape[1] // 2
    group = wide // width
    total = 2 * count * length
    low, high, depth = bits()
    for i, block in enumerate(blocks):
        keys[pl.ds(i * length, length), :] = block[:, pl.ds(0, width)]
        values[pl.ds(i * length, length), :] = block[:, pl.ds(width, width)]
    column = lax.broadcasted_iota(jnp.int32, (1, total), 1)
    limit = jnp.zeros((1, total), jnp.int32)
    for i in range(2 * count):
        s, t = hops[i // 2], i % 2
        if s == 0:
            core = low if t == 0 else 1 - low
            at = column + ((2 * high + core) * length - i * length)
        else:
            at = jnp.where(jnp.bitwise_xor(depth, s) < depth, -1, 4 * rows)
        limit = jnp.where(column >= i * length, at, limit)
    scale = 1.0 / (math.sqrt(HD) * math.log(2.0))
    row = lax.broadcasted_iota(jnp.int32, (rows, total), 0)
    lane = lax.broadcasted_iota(jnp.int32, (rows, LANES), 1)
    for which, (query, side) in enumerate(zip(queries, sides)):
        place = jnp.bitwise_xor(high, side)
        allowed = row + (2 * place + low) * rows >= limit
        stats = jnp.zeros((rows, LANES), F32)
        if last:
            mixed_ref, stats_ref = carried[2 * which : 2 * which + 2]
            out = outs[which]
        else:
            out, stats_out = outs[2 * which : 2 * which + 2]
        for head in range(heads):
            columns = pl.ds(head * HD, HD)
            shared = pl.ds((head // group) * HD, HD)
            scores = dot(query[:, columns], keys[:, shared], ((1,), (1,))) * scale
            masked = jnp.where(allowed, scores, FAR)
            top = jnp.maximum(jnp.max(masked, axis=1, keepdims=True), NEAR)
            if last:
                old = stats_ref[:, 2 * head : 2 * head + 1]
                top = jnp.maximum(top, old)
            weights = jnp.exp2(masked - top)
            summed = jnp.sum(weights, axis=1, keepdims=True)
            mixed = dot(weights.astype(BF16), values[:, shared], ((1,), (0,)))
            if not last:
                out[:, columns] = mixed
                stats = jnp.where(lane == 2 * head, top, stats)
                stats = jnp.where(lane == 2 * head + 1, summed, stats)
                continue
            shrink = jnp.exp2(old - top)
            summed = summed + shrink * stats_ref[:, 2 * head + 1 : 2 * head + 2]
            mixed = mixed + shrink * mixed_ref[:, columns]
            some = summed > 0.0
            safe = jnp.where(some, summed, 1.0)
            out[:, columns] = (mixed / safe).astype(out.dtype)
            level = jnp.where(some, top + jnp.log2(safe), FAR)
            for i, third in enumerate(thirds(level)):
                stats = jnp.where(lane == 3 * head + i, third, stats)
        if last:
            out[:, pl.ds(wide, LANES)] = stats.astype(out.dtype)
        else:
            stats_out[...] = stats


def merge(head, keep_ref, other_ref, out):
    wide = out.shape[1]
    ins = (keep_ref, other_ref)
    columns = pl.ds(head * HD, HD)
    tiles = [ref[:, pl.ds(wide, LANES)].astype(F32) for ref in ins]
    levels = [
        tile[:, 3 * head : 3 * head + 1]
        + tile[:, 3 * head + 1 : 3 * head + 2]
        + tile[:, 3 * head + 2 : 3 * head + 3]
        for tile in tiles
    ]
    top = functools.reduce(jnp.maximum, levels)
    weights = [jnp.exp2(level - top) for level in levels]
    share = 1.0 / functools.reduce(jnp.add, weights)
    mixed = functools.reduce(
        jnp.add, [(w * share) * ref[:, columns].astype(F32) for w, ref in zip(weights, ins)]
    )
    out[:, columns] = mixed.astype(BF16)


def per_device(count, n, q_ret, k_ret, v_ret, gate_ret, log_decay, q_cross, cache_k, cache_v):
    far = count // 4
    rows, wide = q_cross.shape
    heads = wide // HD
    length, width = cache_k.shape[0], cache_k.shape[1] // n
    half, quarter = HD // 2, HD // 4

    def swap(value, bit, wanted=None):
        pairs = [(b ^ bit, b) for b in range(count) if wanted is None or wanted(b // 4)]
        return lax.ppermute(value, "ctx", pairs)

    def to_head(value, e):
        return lax.ppermute(value, "head", [(y, (y + e) % n) for y in range(n)])

    plain = (k_ret, v_ret, log_decay.T, q_ret, q_cross, gate_ret)
    loaded = call(
        functools.partial(load_all, n, 2 + len(plain)),
        [pltpu.VMEM((length, 2 * width), BF16)] * n
        + [pltpu.VMEM(a.shape, a.dtype) for a in plain]
        + [pltpu.VMEM((half + PAD, wide), BF16), pltpu.VMEM((half + PAD, wide), F32)],
        [pltpu.with_memory_space_constraint(a, pltpu.HBM) for a in (cache_k, cache_v, *plain)],
        scratch=[pltpu.VMEM((HD, wide), F32), pltpu.SemaphoreType.DMA((2 * n + len(plain),))],
        name="load_all",
        takes=HBM,
    )
    pieces = loaded[:n]
    k_ret, v_ret, decays, q_ret, q_cross, gate_ret, sum_send, sum_keep = loaded[n:]
    arrived = [pieces[0]] + [to_head(pieces[e], e) for e in range(1, n)]
    sum_other = swap(sum_send, 1)
    chip_send, chip_keep = call(
        chip_total,
        [shape((quarter + PAD, wide)), shape((quarter + PAD, wide), F32)],
        (sum_keep, sum_other),
        scratch=[pltpu.VMEM((half, wide), F32)],
        name="chip_total",
    )
    inside, factor = call(
        retain_inside,
        [shape((rows, wide), F32), shape((rows, heads), F32)],
        (q_ret, k_ret, v_ret, decays),
        name="retain_inside",
        after=(chip_send,),
    )
    blocks = {
        0: call(
            functools.partial(join_rows, n),
            [shape((n * length, 2 * width))],
            arrived,
            name="join_rows",
            flops=3000000000,
        )
    }
    chip_other = swap(chip_send, 2)
    bit = far // 2
    while bit > 1:
        for s in list(blocks):
            blocks[s ^ bit] = swap(blocks[s], 4 * bit)
        bit //= 2
    window, handed = call(
        plane_total,
        [shape((quarter + PAD, wide)), shape(blocks[0].shape)],
        (chip_keep, chip_other, blocks[0]),
        name="plane_total",
        after=(factor,),
    )
    blocks[1] = swap(handed, 4)
    q_cross = pass_on(q_cross, blocks[far // 2])
    q_other = swap(q_cross, 2)
    planes, bit = [], 1
    while bit < far:
        wanted = (lambda z, bit=bit: z & bit) if bit > 1 else None
        planes.append(swap(window, 4 * bit, wanted))
        if 2 * bit < far:
            window = call(
                functools.partial(grow, bit),
                [shape(window.shape)],
                (window, planes[-1]),
                name="grow",
                flops=3000000000,
                after=tuple(blocks[s] for s in blocks if s),
            )
        bit *= 2

    def look(hops, last, outs, queries, carried, name):
        keys = 2 * len(hops) * n * length
        both = []
        for s in hops:
            if s not in swapped:
                swapped[s] = swap(blocks[s], 1)
            both += [blocks[s], swapped[s]]
        return call(
            functools.partial(attend, hops, last, [side for _, side in queries]),
            outs,
            (*[query for query, _ in queries], *both, *carried),
            scratch=[pltpu.VMEM((keys, width), BF16) for _ in range(2)],
            name=name,
        )

    swapped = {}
    near = list(blocks)
    so_far = look(
        near,
        False,
        [shape((rows, wide), F32), shape((rows, LANES), F32)] * 2,
        ((q_other, 1), (q_cross, 0)),
        (),
        "attend_near",
    )
    prior_send, prior_keep = call(
        chip_priors,
        [shape((quarter, wide)), shape((quarter, wide), F32)],
        (chip_keep, chip_other, *planes),
        name="chip_priors",
        flops=3000000000,
        after=so_far[1:2],
    )
    for s in near:
        if s > 1:
            ready = call(copy_after, [shape(blocks[s].shape)], (blocks[s],), after=(window,))
            last = swap(ready, 4, lambda z, s=s: z ^ s ^ 1 < z)
            blocks[s ^ 1] = pass_on(last, prior_send)
    hops = [s for s in blocks if s not in near]
    packed = (rows, wide + LANES)
    part_send = look(hops, True, [shape(packed)], ((q_other, 1),), so_far[:2], "attend_far")
    part_keep = look(hops, True, [shape(packed, F32)], ((q_cross, 0),), so_far[2:], "attend_own")
    part_other = swap(part_send, 2)
    prior_other = swap(prior_send, 2)
    state_send, state_keep = call(
        block_priors,
        [shape((half, wide)), shape((half, wide))],
        (sum_keep, sum_other, prior_keep, prior_other),
        scratch=[pltpu.VMEM((half, wide), F32)],
        name="block_priors",
    )
    state_other = swap(state_send, 1)
    done = pltpu.VMEM((rows, wide), BF16)
    o_ret = call(
        retain_finish,
        [shape((rows, wide))],
        (q_ret, gate_ret, inside, factor, state_keep, state_other),
        scratch=[pltpu.VMEM((HD, wide), BF16), done, pltpu.SemaphoreType.DMA],
        name="retain_finish",
        gives=HBM,
    )
    o_cross = call(
        finish,
        [shape((rows, wide))],
        (part_keep, part_other),
        scratch=[done, pltpu.SemaphoreType.DMA((heads,))],
        name="finish",
        gives=HBM,
    )
    return o_ret, o_cross


def solution(mesh):
    split = P("ctx", "head")
    rows = P(("ctx", "head"), None)
    return jax.shard_map(
        functools.partial(per_device, mesh.shape["ctx"], mesh.shape["head"]),
        mesh=mesh,
        in_specs=(split,) * 6 + (rows,) * 2,
        out_specs=(split, split),
        check_vma=False,
    )
```

```python
import functools
import math

import jax
import jax.numpy as jnp
from jax import lax
from jax.experimental import pallas as pl
from jax.experimental.pallas import tpu as pltpu
from jax.sharding import PartitionSpec as P

HD = 256
FAR = -1e30
NEAR = -1e29
EPS = 1e-06
F32 = jnp.float32
BF16 = jnp.bfloat16
PAD = 16
LANES = 128
VMEM = pl.BlockSpec(memory_space=pltpu.VMEM)
ANY = pl.BlockSpec(memory_space=pl.ANY)
HBM = pl.BlockSpec(memory_space=pltpu.HBM)


def call(
    body, outs, args, scratch=(), name=None, flops=1000, takes=VMEM, gives=VMEM, after=(),
    aliases=None,
):
    single = len(outs) == 1
    used, total = len(args), len(args) + len(after)

    def kernel(*refs):
        body(*refs[:used], *refs[total:])

    return pl.pallas_call(
        kernel,
        out_shape=outs[0] if single else tuple(outs),
        in_specs=(takes if isinstance(takes, list) else [takes] * used) + [ANY] * len(after),
        out_specs=gives if single or isinstance(gives, tuple) else tuple(gives for _ in outs),
        scratch_shapes=scratch,
        input_output_aliases=aliases or {},
        compiler_params=pltpu.CompilerParams(vmem_limit_bytes=40 * 1024 * 1024),
        cost_estimate=pl.CostEstimate(flops=flops, bytes_accessed=1000, transcendentals=0),
        name=name,
    )(*args, *after)


def pass_on(value, *after):
    return call(
        lambda *refs: None,
        [shape(value.shape, value.dtype)],
        (value,),
        name="pass_on",
        takes=ANY,
        gives=ANY,
        after=after,
        aliases={0: 0},
    )


def shape(dims, dtype=BF16):
    return jax.ShapeDtypeStruct(dims, dtype)


def dot(a, b, contract, precision=None):
    return lax.dot_general(
        a, b, (contract, ((), ())), preferred_element_type=F32, precision=precision
    )


def thirds(value):
    high = value.astype(BF16).astype(F32)
    rest = value - high
    middle = rest.astype(BF16).astype(F32)
    return high, middle, rest - middle


def lower_ones(rows):
    below = lax.broadcasted_iota(jnp.int32, (rows, rows), 0) >= lax.broadcasted_iota(
        jnp.int32, (rows, rows), 1
    )
    return below, jnp.where(below, 1.0, 0.0).astype(F32)


def join_rows(n, *refs):
    pieces, out = refs[:n], refs[n]
    length = pieces[0].shape[0]
    here = lax.axis_index("head")
    for e, piece in enumerate(pieces):
        place = lax.rem(here + n - e, n)
        out[pl.ds(pl.multiple_of(place * length, PAD), length), :] = piece[...]


def bits():
    index = lax.axis_index("ctx")
    low = lax.rem(index, 2)
    return low, lax.rem(lax.div(index, 2), 2), lax.div(index, 4)


def put_total(out, at, total):
    wide = out.shape[1]
    if out.dtype == F32:
        out[pl.ds(at, PAD), :] = jnp.broadcast_to(total, (PAD, wide))
        return
    row = lax.broadcasted_iota(jnp.int32, (PAD, wide), 0)
    high, middle, low = thirds(total)
    tile = jnp.where(row == 0, high, jnp.where(row == 1, middle, jnp.where(row == 2, low, 0.0)))
    out[pl.ds(at, PAD), :] = tile.astype(out.dtype)


def total_of(ref):
    tile = ref[pl.ds(ref.shape[0] - PAD, PAD), :].astype(F32)
    if ref.dtype == F32:
        return tile[0:1, :]
    return tile[0:1, :] + tile[1:2, :] + tile[2:3, :]


def state_of(ref):
    return ref[pl.ds(0, ref.shape[0] - PAD), :].astype(F32)


def part_of(held, which, rows):
    return held[pl.ds(pl.multiple_of(which * rows, rows), rows), :]


def summarize(k_ref, v_ref, d_ref, send, keep, held):
    low, _, _ = bits()
    half = HD // 2
    rows = d_ref.shape[1]
    sums = dot(lower_ones(rows)[1], d_ref[...], ((1,), (1,)), lax.Precision.HIGHEST)
    totals = []
    for head in range(d_ref.shape[0]):
        columns = pl.ds(head * HD, HD)
        column = sums[:, head : head + 1]
        last = column[rows - 1 : rows, :]
        carried = (k_ref[:, columns].astype(F32) * jnp.exp(last - column)).astype(BF16)
        held[:, columns] = dot(carried, v_ref[:, columns], ((0,), (0,)))
        totals.append(jnp.broadcast_to(last, (1, HD)))
    total = jnp.concatenate(totals, axis=1)
    for out, which in ((send, 1 - low), (keep, low)):
        out[pl.ds(0, half), :] = part_of(held, which, half).astype(out.dtype)
        put_total(out, half, total)


def load_all(n, count, *refs):
    k_ref, v_ref, *plain = refs[:count]
    outs, (held, sems) = refs[count:-2], refs[-2:]
    pieces, copies, (send, keep) = outs[:n], outs[n:-2], outs[-2:]
    width = k_ref.shape[1] // n
    here = lax.axis_index("head")
    moves = list(zip(plain, copies))
    for e, piece in enumerate(pieces):
        target = lax.rem(here + e, n)
        columns = pl.ds(pl.multiple_of(target * width, LANES), width)
        moves.append((k_ref.at[:, columns], piece.at[:, pl.ds(0, width)]))
        moves.append((v_ref.at[:, columns], piece.at[:, pl.ds(width, width)]))
    running = [pltpu.make_async_copy(a, b, sems.at[i]) for i, (a, b) in enumerate(moves)]
    for one in running:
        one.start()
    for one in running[:3]:
        one.wait()
    summarize(*copies[:3], send, keep, held)
    for one in running[3:]:
        one.wait()


def pair_total(first, keep_ref, other_ref):
    kept, other = state_of(keep_ref), state_of(other_ref)
    kept_total, other_total = total_of(keep_ref), total_of(other_ref)
    late = jnp.where(first, other_total, kept_total)
    earlier, later = jnp.where(first, kept, other), jnp.where(first, other, kept)
    return jnp.exp(late) * earlier + later, kept_total + other_total


def chip_total(keep_ref, other_ref, send, keep, held):
    low, high, _ = bits()
    quarter = HD // 4
    held[...], total = pair_total(low == 0, keep_ref, other_ref)
    for out, which in ((send, 1 - high), (keep, high)):
        out[pl.ds(0, quarter), :] = part_of(held, which, quarter).astype(out.dtype)
        put_total(out, quarter, total)


def plane_total(keep_ref, other_ref, block_ref, out, block_out):
    block_out[...] = block_ref[...]
    _, high, _ = bits()
    state, total = pair_total(high == 0, keep_ref, other_ref)
    out[pl.ds(0, state.shape[0]), :] = state.astype(out.dtype)
    put_total(out, state.shape[0], total)


def chip_priors(keep_ref, other_ref, *refs):
    planes, send, keep = refs[:-2], refs[-2], refs[-1]
    _, high, depth = bits()
    entering = jnp.zeros(send.shape, F32)
    between = jnp.zeros((1, send.shape[1]), F32)
    for i, ref in enumerate(planes):
        earlier = lax.rem(lax.div(depth, 2**i), 2) == 1
        entering = entering + jnp.where(earlier, jnp.exp(between) * state_of(ref), 0.0)
        between = between + jnp.where(earlier, total_of(ref), 0.0)
    first = high == 0
    early = jnp.where(first, state_of(keep_ref), state_of(other_ref))
    early_total = jnp.where(first, total_of(keep_ref), total_of(other_ref))
    second = jnp.exp(early_total) * entering + early
    send[...] = jnp.where(first, second, entering).astype(send.dtype)
    keep[...] = jnp.where(first, entering, second).astype(keep.dtype)


def block_priors(keep_ref, other_ref, prior_ref, prior_other_ref, send, keep, held):
    low, high, _ = bits()
    quarter = prior_ref.shape[0]
    for ref, which in ((prior_ref, high), (prior_other_ref, 1 - high)):
        held[pl.ds(pl.multiple_of(which * quarter, quarter), quarter), :] = ref[...].astype(F32)
    first = low == 0
    early = jnp.where(first, state_of(keep_ref), state_of(other_ref))
    early_total = jnp.where(first, total_of(keep_ref), total_of(other_ref))
    entering = held[...]
    second = jnp.exp(early_total) * entering + early
    send[...] = jnp.where(first, second, entering).astype(send.dtype)
    keep[...] = jnp.where(first, entering, second).astype(keep.dtype)


def grow(bit, own_ref, other_ref, out):
    rows = out.shape[0] - PAD
    first = lax.rem(lax.div(bits()[2], bit), 2) == 0
    state, total = pair_total(first, own_ref, other_ref)
    out[pl.ds(0, rows), :] = state.astype(out.dtype)
    put_total(out, rows, total)


def retain_inside(q_ref, k_ref, v_ref, d_ref, inside_ref, factor_ref):
    heads, rows = d_ref.shape
    below, ones = lower_ones(rows)
    sums = dot(ones, d_ref[...], ((1,), (1,)), lax.Precision.HIGHEST)
    same = lax.broadcasted_iota(jnp.int32, (rows, rows), 0) == lax.broadcasted_iota(
        jnp.int32, (rows, rows), 1
    )
    factor_ref[...] = jnp.exp(sums)
    for head in range(heads):
        columns = pl.ds(head * HD, HD)
        column = jnp.broadcast_to(sums[:, head : head + 1], (rows, rows))
        across = jnp.sum(jnp.where(same, column, 0.0), axis=0, keepdims=True)
        spread = jnp.exp(jnp.minimum(column - across, 0.0))
        scores = dot(q_ref[:, columns], k_ref[:, columns], ((1,), (1,)))
        weights = jnp.where(below, spread * scores, 0.0).astype(BF16)
        inside_ref[:, columns] = dot(weights, v_ref[:, columns], ((1,), (0,)))


def retain_finish(q_ref, gate_ref, inside_ref, factor_ref, keep_ref, other_ref, o_ret, held, done, sem):
    low, _, _ = bits()
    half = keep_ref.shape[0]
    for ref, which in ((keep_ref, low), (other_ref, 1 - low)):
        held[pl.ds(pl.multiple_of(which * half, half), half), :] = ref[...]
    for head in range(factor_ref.shape[1]):
        columns = pl.ds(head * HD, HD)
        before = dot(q_ref[:, columns], held[:, columns], ((1,), (0,)))
        retained = inside_ref[:, columns] + factor_ref[:, head : head + 1] * before
        scale = lax.rsqrt(jnp.mean(retained * retained, axis=1, keepdims=True) + EPS)
        gate = gate_ref[:, columns].astype(F32)
        silu = gate / (1.0 + jnp.exp(-gate))
        done[:, columns] = (retained * scale * silu).astype(BF16)
    out = pltpu.make_async_copy(done, o_ret, sem)
    out.start()
    out.wait()


def finish(part_ref, part_other_ref, o_cross, done, sems):
    wide = done.shape[1]
    moves = []
    for head in range(wide // HD):
        merge(head, part_ref, part_other_ref, done)
        columns = pl.ds(head * HD, HD)
        moves.append(pltpu.make_async_copy(done.at[:, columns], o_cross.at[:, columns], sems.at[head]))
        moves[-1].start()
    for move in moves:
        move.wait()


def copy_after(source, out):
    out[...] = source[...]


def attend(hops, last, sides, *refs):
    count = len(hops)
    queries, refs = refs[: len(sides)], refs[len(sides) :]
    blocks, refs = refs[: 2 * count], refs[2 * count :]
    taken = 2 * len(sides) if last else 0
    carried, refs = refs[:taken], refs[taken:]
    outs, (keys, values) = refs[:-2], refs[-2:]
    rows, wide = queries[0].shape
    heads = wide // HD
    length, width = blocks[0].shape[0], blocks[0].shape[1] // 2
    group = wide // width
    total = 2 * count * length
    low, high, depth = bits()
    for i, block in enumerate(blocks):
        keys[pl.ds(i * length, length), :] = block[:, pl.ds(0, width)]
        values[pl.ds(i * length, length), :] = block[:, pl.ds(width, width)]
    column = lax.broadcasted_iota(jnp.int32, (1, total), 1)
    limit = jnp.zeros((1, total), jnp.int32)
    for i in range(2 * count):
        s, t = hops[i // 2], i % 2
        if s == 0:
            core = low if t == 0 else 1 - low
            at = column + ((2 * high + core) * length - i * length)
        else:
            at = jnp.where(jnp.bitwise_xor(depth, s) < depth, -1, 4 * rows)
        limit = jnp.where(column >= i * length, at, limit)
    scale = 1.0 / (math.sqrt(HD) * math.log(2.0))
    row = lax.broadcasted_iota(jnp.int32, (rows, total), 0)
    lane = lax.broadcasted_iota(jnp.int32, (rows, LANES), 1)
    for which, (query, side) in enumerate(zip(queries, sides)):
        place = jnp.bitwise_xor(high, side)
        allowed = row + (2 * place + low) * rows >= limit
        stats = jnp.zeros((rows, LANES), F32)
        if last:
            mixed_ref, stats_ref = carried[2 * which : 2 * which + 2]
            out = outs[which]
        else:
            out, stats_out = outs[2 * which : 2 * which + 2]
        for head in range(heads):
            columns = pl.ds(head * HD, HD)
            shared = pl.ds((head // group) * HD, HD)
            scores = dot(query[:, columns], keys[:, shared], ((1,), (1,))) * scale
            masked = jnp.where(allowed, scores, FAR)
            top = jnp.maximum(jnp.max(masked, axis=1, keepdims=True), NEAR)
            if last:
                old = stats_ref[:, 2 * head : 2 * head + 1]
                top = jnp.maximum(top, old)
            weights = jnp.exp2(masked - top)
            summed = jnp.sum(weights, axis=1, keepdims=True)
            mixed = dot(weights.astype(BF16), values[:, shared], ((1,), (0,)))
            if not last:
                out[:, columns] = mixed
                stats = jnp.where(lane == 2 * head, top, stats)
                stats = jnp.where(lane == 2 * head + 1, summed, stats)
                continue
            shrink = jnp.exp2(old - top)
            summed = summed + shrink * stats_ref[:, 2 * head + 1 : 2 * head + 2]
            mixed = mixed + shrink * mixed_ref[:, columns]
            some = summed > 0.0
            safe = jnp.where(some, summed, 1.0)
            out[:, columns] = (mixed / safe).astype(out.dtype)
            level = jnp.where(some, top + jnp.log2(safe), FAR)
            for i, third in enumerate(thirds(level)):
                stats = jnp.where(lane == 3 * head + i, third, stats)
        if last:
            out[:, pl.ds(wide, LANES)] = stats.astype(out.dtype)
        else:
            stats_out[...] = stats


def merge(head, keep_ref, other_ref, out):
    wide = out.shape[1]
    ins = (keep_ref, other_ref)
    columns = pl.ds(head * HD, HD)
    tiles = [ref[:, pl.ds(wide, LANES)].astype(F32) for ref in ins]
    levels = [
        tile[:, 3 * head : 3 * head + 1]
        + tile[:, 3 * head + 1 : 3 * head + 2]
        + tile[:, 3 * head + 2 : 3 * head + 3]
        for tile in tiles
    ]
    top = functools.reduce(jnp.maximum, levels)
    weights = [jnp.exp2(level - top) for level in levels]
    share = 1.0 / functools.reduce(jnp.add, weights)
    mixed = functools.reduce(
        jnp.add, [(w * share) * ref[:, columns].astype(F32) for w, ref in zip(weights, ins)]
    )
    out[:, columns] = mixed.astype(BF16)


def per_device(count, n, q_ret, k_ret, v_ret, gate_ret, log_decay, q_cross, cache_k, cache_v):
    far = count // 4
    rows, wide = q_cross.shape
    heads = wide // HD
    length, width = cache_k.shape[0], cache_k.shape[1] // n
    half, quarter = HD // 2, HD // 4

    def swap(value, bit, wanted=None):
        pairs = [
            (b ^ bit if wanted is None or wanted(b // 4) else b, b) for b in range(count)
        ]
        return lax.ppermute(value, "ctx", pairs)

    def to_head(value, e):
        return lax.ppermute(value, "head", [(y, (y + e) % n) for y in range(n)])

    plain = (k_ret, v_ret, log_decay.T, q_ret, q_cross, gate_ret)
    loaded = call(
        functools.partial(load_all, n, 2 + len(plain)),
        [pltpu.VMEM((length, 2 * width), BF16)] * n
        + [pltpu.VMEM(a.shape, a.dtype) for a in plain]
        + [pltpu.VMEM((half + PAD, wide), BF16), pltpu.VMEM((half + PAD, wide), F32)],
        [pltpu.with_memory_space_constraint(a, pltpu.HBM) for a in (cache_k, cache_v, *plain)],
        scratch=[pltpu.VMEM((HD, wide), F32), pltpu.SemaphoreType.DMA((2 * n + len(plain),))],
        name="load_all",
        takes=HBM,
    )
    pieces = loaded[:n]
    k_ret, v_ret, decays, q_ret, q_cross, gate_ret, sum_send, sum_keep = loaded[n:]
    arrived = [pieces[0]] + [to_head(pieces[e], e) for e in range(1, n)]
    sum_other = swap(sum_send, 1)
    chip_send, chip_keep = call(
        chip_total,
        [shape((quarter + PAD, wide)), shape((quarter + PAD, wide), F32)],
        (sum_keep, sum_other),
        scratch=[pltpu.VMEM((half, wide), F32)],
        name="chip_total",
    )
    inside, factor = call(
        retain_inside,
        [shape((rows, wide), F32), shape((rows, heads), F32)],
        (q_ret, k_ret, v_ret, decays),
        name="retain_inside",
        after=(chip_send,),
    )
    blocks = {
        0: call(
            functools.partial(join_rows, n),
            [shape((n * length, 2 * width))],
            arrived,
            name="join_rows",
            flops=3000000000,
        )
    }
    chip_other = swap(chip_send, 2)
    bit = far // 2
    while bit > 1:
        for s in list(blocks):
            blocks[s ^ bit] = swap(blocks[s], 4 * bit)
        bit //= 2
    window, handed = call(
        plane_total,
        [shape((quarter + PAD, wide)), shape(blocks[0].shape)],
        (chip_keep, chip_other, blocks[0]),
        name="plane_total",
        after=(factor,),
    )
    blocks[1] = swap(handed, 4)
    q_cross = pass_on(q_cross, blocks[far // 2])
    q_other = swap(q_cross, 2)
    planes, bit = [], 1
    while bit < far:
        planes.append(swap(window, 4 * bit))
        if 2 * bit < far:
            window = call(
                functools.partial(grow, bit),
                [shape(window.shape)],
                (window, planes[-1]),
                name="grow",
                flops=3000000000,
                after=tuple(blocks[s] for s in blocks if s),
            )
        bit *= 2

    def look(hops, last, outs, queries, carried, name):
        keys = 2 * len(hops) * n * length
        both = []
        for s in hops:
            if s not in swapped:
                swapped[s] = swap(blocks[s], 1)
            both += [blocks[s], swapped[s]]
        return call(
            functools.partial(attend, hops, last, [side for _, side in queries]),
            outs,
            (*[query for query, _ in queries], *both, *carried),
            scratch=[pltpu.VMEM((keys, width), BF16) for _ in range(2)],
            name=name,
        )

    swapped = {}
    near = list(blocks)
    so_far = look(
        near,
        False,
        [shape((rows, wide), F32), shape((rows, LANES), F32)] * 2,
        ((q_other, 1), (q_cross, 0)),
        (),
        "attend_near",
    )
    prior_send, prior_keep = call(
        chip_priors,
        [shape((quarter, wide)), shape((quarter, wide), F32)],
        (chip_keep, chip_other, *planes),
        name="chip_priors",
        flops=3000000000,
        after=so_far[1:2],
    )
    for s in near:
        if s > 1:
            ready = call(copy_after, [shape(blocks[s].shape)], (blocks[s],), after=(window,))
            last = swap(ready, 4, lambda z, s=s: (z ^ s ^ 1) < z)
            blocks[s ^ 1] = pass_on(last, prior_send)
    hops = [s for s in blocks if s not in near]
    packed = (rows, wide + LANES)
    part_send = look(hops, True, [shape(packed)], ((q_other, 1),), so_far[:2], "attend_far")
    part_keep = look(hops, True, [shape(packed, F32)], ((q_cross, 0),), so_far[2:], "attend_own")
    part_other = swap(part_send, 2)
    prior_other = swap(prior_send, 2)
    state_send, state_keep = call(
        block_priors,
        [shape((half, wide)), shape((half, wide))],
        (sum_keep, sum_other, prior_keep, prior_other),
        scratch=[pltpu.VMEM((half, wide), F32)],
        name="block_priors",
    )
    state_other = swap(state_send, 1)
    done = pltpu.VMEM((rows, wide), BF16)
    o_ret = call(
        retain_finish,
        [shape((rows, wide))],
        (q_ret, gate_ret, inside, factor, state_keep, state_other),
        scratch=[pltpu.VMEM((HD, wide), BF16), done, pltpu.SemaphoreType.DMA],
        name="retain_finish",
        gives=HBM,
    )
    o_cross = call(
        finish,
        [shape((rows, wide))],
        (part_keep, part_other),
        scratch=[done, pltpu.SemaphoreType.DMA((heads,))],
        name="finish",
        gives=HBM,
    )
    return o_ret, o_cross


def solution(mesh):
    split = P("ctx", "head")
    rows = P(("ctx", "head"), None)
    return jax.shard_map(
        functools.partial(per_device, mesh.shape["ctx"], mesh.shape["head"]),
        mesh=mesh,
        in_specs=(split,) * 6 + (rows,) * 2,
        out_specs=(split, split),
        check_vma=False,
    )
```

```python
import functools
import math

import jax
import jax.numpy as jnp
from jax import lax
from jax.experimental import pallas as pl
from jax.experimental.pallas import tpu as pltpu
from jax.sharding import PartitionSpec as P

HD = 256
FAR = -1e30
NEAR = -1e29
EPS = 1e-06
F32 = jnp.float32
BF16 = jnp.bfloat16
PAD = 16
LANES = 128
VMEM = pl.BlockSpec(memory_space=pltpu.VMEM)
ANY = pl.BlockSpec(memory_space=pl.ANY)
HBM = pl.BlockSpec(memory_space=pltpu.HBM)


def call(
    body, outs, args, scratch=(), name=None, flops=1000, takes=VMEM, gives=VMEM, after=(),
    aliases=None,
):
    single = len(outs) == 1
    used, total = len(args), len(args) + len(after)

    def kernel(*refs):
        body(*refs[:used], *refs[total:])

    return pl.pallas_call(
        kernel,
        out_shape=outs[0] if single else tuple(outs),
        in_specs=(takes if isinstance(takes, list) else [takes] * used) + [ANY] * len(after),
        out_specs=gives if single or isinstance(gives, tuple) else tuple(gives for _ in outs),
        scratch_shapes=scratch,
        input_output_aliases=aliases or {},
        compiler_params=pltpu.CompilerParams(vmem_limit_bytes=40 * 1024 * 1024),
        cost_estimate=pl.CostEstimate(flops=flops, bytes_accessed=1000, transcendentals=0),
        name=name,
    )(*args, *after)


def pass_on(value, *after):
    return call(
        lambda *refs: None,
        [shape(value.shape, value.dtype)],
        (value,),
        name="pass_on",
        takes=ANY,
        gives=ANY,
        after=after,
        aliases={0: 0},
    )


def shape(dims, dtype=BF16):
    return jax.ShapeDtypeStruct(dims, dtype)


def dot(a, b, contract, precision=None):
    return lax.dot_general(
        a, b, (contract, ((), ())), preferred_element_type=F32, precision=precision
    )


def thirds(value):
    high = value.astype(BF16).astype(F32)
    rest = value - high
    middle = rest.astype(BF16).astype(F32)
    return high, middle, rest - middle


def lower_ones(rows):
    below = lax.broadcasted_iota(jnp.int32, (rows, rows), 0) >= lax.broadcasted_iota(
        jnp.int32, (rows, rows), 1
    )
    return below, jnp.where(below, 1.0, 0.0).astype(F32)


def join_rows(n, *refs):
    pieces, out = refs[:n], refs[n]
    length = pieces[0].shape[0]
    here = lax.axis_index("head")
    for e, piece in enumerate(pieces):
        place = lax.rem(here + n - e, n)
        out[pl.ds(pl.multiple_of(place * length, PAD), length), :] = piece[...]


def bits():
    index = lax.axis_index("ctx")
    low = lax.rem(index, 2)
    return low, lax.rem(lax.div(index, 2), 2), lax.div(index, 4)


def put_total(out, at, total):
    wide = out.shape[1]
    if out.dtype == F32:
        out[pl.ds(at, PAD), :] = jnp.broadcast_to(total, (PAD, wide))
        return
    row = lax.broadcasted_iota(jnp.int32, (PAD, wide), 0)
    high, middle, low = thirds(total)
    tile = jnp.where(row == 0, high, jnp.where(row == 1, middle, jnp.where(row == 2, low, 0.0)))
    out[pl.ds(at, PAD), :] = tile.astype(out.dtype)


def total_of(ref):
    tile = ref[pl.ds(ref.shape[0] - PAD, PAD), :].astype(F32)
    if ref.dtype == F32:
        return tile[0:1, :]
    return tile[0:1, :] + tile[1:2, :] + tile[2:3, :]


def state_of(ref):
    return ref[pl.ds(0, ref.shape[0] - PAD), :].astype(F32)


def part_of(held, which, rows):
    return held[pl.ds(pl.multiple_of(which * rows, rows), rows), :]


def summarize(k_ref, v_ref, d_ref, send, keep, held):
    low, _, _ = bits()
    half = HD // 2
    rows = d_ref.shape[1]
    sums = dot(lower_ones(rows)[1], d_ref[...], ((1,), (1,)), lax.Precision.HIGHEST)
    totals = []
    for head in range(d_ref.shape[0]):
        columns = pl.ds(head * HD, HD)
        column = sums[:, head : head + 1]
        last = column[rows - 1 : rows, :]
        carried = (k_ref[:, columns].astype(F32) * jnp.exp(last - column)).astype(BF16)
        held[:, columns] = dot(carried, v_ref[:, columns], ((0,), (0,)))
        totals.append(jnp.broadcast_to(last, (1, HD)))
    total = jnp.concatenate(totals, axis=1)
    for out, which in ((send, 1 - low), (keep, low)):
        out[pl.ds(0, half), :] = part_of(held, which, half).astype(out.dtype)
        put_total(out, half, total)


def load_all(n, count, *refs):
    k_ref, v_ref, *plain = refs[:count]
    outs, (held, sems) = refs[count:-2], refs[-2:]
    pieces, copies, (send, keep) = outs[:n], outs[n:-2], outs[-2:]
    width = k_ref.shape[1] // n
    here = lax.axis_index("head")
    moves = list(zip(plain, copies))
    for e, piece in enumerate(pieces):
        target = lax.rem(here + e, n)
        columns = pl.ds(pl.multiple_of(target * width, LANES), width)
        moves.append((k_ref.at[:, columns], piece.at[:, pl.ds(0, width)]))
        moves.append((v_ref.at[:, columns], piece.at[:, pl.ds(width, width)]))
    running = [pltpu.make_async_copy(a, b, sems.at[i]) for i, (a, b) in enumerate(moves)]
    for one in running:
        one.start()
    for one in running[:3]:
        one.wait()
    summarize(*copies[:3], send, keep, held)
    for one in running[3:]:
        one.wait()


def pair_total(first, keep_ref, other_ref):
    kept, other = state_of(keep_ref), state_of(other_ref)
    kept_total, other_total = total_of(keep_ref), total_of(other_ref)
    late = jnp.where(first, other_total, kept_total)
    earlier, later = jnp.where(first, kept, other), jnp.where(first, other, kept)
    return jnp.exp(late) * earlier + later, kept_total + other_total


def chip_total(keep_ref, other_ref, send, keep, held):
    low, high, _ = bits()
    quarter = HD // 4
    held[...], total = pair_total(low == 0, keep_ref, other_ref)
    for out, which in ((send, 1 - high), (keep, high)):
        out[pl.ds(0, quarter), :] = part_of(held, which, quarter).astype(out.dtype)
        put_total(out, quarter, total)


def plane_total(keep_ref, other_ref, block_ref, out, block_out):
    block_out[...] = block_ref[...]
    _, high, _ = bits()
    state, total = pair_total(high == 0, keep_ref, other_ref)
    out[pl.ds(0, state.shape[0]), :] = state.astype(out.dtype)
    put_total(out, state.shape[0], total)


def chip_priors(keep_ref, other_ref, *refs):
    planes, send, keep = refs[:-2], refs[-2], refs[-1]
    _, high, depth = bits()
    entering = jnp.zeros(send.shape, F32)
    between = jnp.zeros((1, send.shape[1]), F32)
    for i, ref in enumerate(planes):
        earlier = lax.rem(lax.div(depth, 2**i), 2) == 1
        entering = entering + jnp.where(earlier, jnp.exp(between) * state_of(ref), 0.0)
        between = between + jnp.where(earlier, total_of(ref), 0.0)
    first = high == 0
    early = jnp.where(first, state_of(keep_ref), state_of(other_ref))
    early_total = jnp.where(first, total_of(keep_ref), total_of(other_ref))
    second = jnp.exp(early_total) * entering + early
    send[...] = jnp.where(first, second, entering).astype(send.dtype)
    keep[...] = jnp.where(first, entering, second).astype(keep.dtype)


def block_priors(keep_ref, other_ref, prior_ref, prior_other_ref, send, keep, held):
    low, high, _ = bits()
    quarter = prior_ref.shape[0]
    for ref, which in ((prior_ref, high), (prior_other_ref, 1 - high)):
        held[pl.ds(pl.multiple_of(which * quarter, quarter), quarter), :] = ref[...].astype(F32)
    first = low == 0
    early = jnp.where(first, state_of(keep_ref), state_of(other_ref))
    early_total = jnp.where(first, total_of(keep_ref), total_of(other_ref))
    entering = held[...]
    second = jnp.exp(early_total) * entering + early
    send[...] = jnp.where(first, second, entering).astype(send.dtype)
    keep[...] = jnp.where(first, entering, second).astype(keep.dtype)


def grow(bit, own_ref, other_ref, out):
    rows = out.shape[0] - PAD
    first = lax.rem(lax.div(bits()[2], bit), 2) == 0
    state, total = pair_total(first, own_ref, other_ref)
    out[pl.ds(0, rows), :] = state.astype(out.dtype)
    put_total(out, rows, total)


def retain_inside(q_ref, k_ref, v_ref, d_ref, inside_ref, factor_ref):
    heads, rows = d_ref.shape
    below, ones = lower_ones(rows)
    sums = dot(ones, d_ref[...], ((1,), (1,)), lax.Precision.HIGHEST)
    same = lax.broadcasted_iota(jnp.int32, (rows, rows), 0) == lax.broadcasted_iota(
        jnp.int32, (rows, rows), 1
    )
    factor_ref[...] = jnp.exp(sums)
    for head in range(heads):
        columns = pl.ds(head * HD, HD)
        column = jnp.broadcast_to(sums[:, head : head + 1], (rows, rows))
        across = jnp.sum(jnp.where(same, column, 0.0), axis=0, keepdims=True)
        spread = jnp.exp(jnp.minimum(column - across, 0.0))
        scores = dot(q_ref[:, columns], k_ref[:, columns], ((1,), (1,)))
        weights = jnp.where(below, spread * scores, 0.0).astype(BF16)
        inside_ref[:, columns] = dot(weights, v_ref[:, columns], ((1,), (0,)))


def retain_finish(q_ref, gate_ref, inside_ref, factor_ref, keep_ref, other_ref, o_ret, held, done, sem):
    low, _, _ = bits()
    half = keep_ref.shape[0]
    for ref, which in ((keep_ref, low), (other_ref, 1 - low)):
        held[pl.ds(pl.multiple_of(which * half, half), half), :] = ref[...]
    for head in range(factor_ref.shape[1]):
        columns = pl.ds(head * HD, HD)
        before = dot(q_ref[:, columns], held[:, columns], ((1,), (0,)))
        retained = inside_ref[:, columns] + factor_ref[:, head : head + 1] * before
        scale = lax.rsqrt(jnp.mean(retained * retained, axis=1, keepdims=True) + EPS)
        gate = gate_ref[:, columns].astype(F32)
        silu = gate / (1.0 + jnp.exp(-gate))
        done[:, columns] = (retained * scale * silu).astype(BF16)
    out = pltpu.make_async_copy(done, o_ret, sem)
    out.start()
    out.wait()


def finish(part_ref, part_other_ref, o_cross, done, sems):
    wide = done.shape[1]
    moves = []
    for head in range(wide // HD):
        merge(head, part_ref, part_other_ref, done)
        columns = pl.ds(head * HD, HD)
        moves.append(pltpu.make_async_copy(done.at[:, columns], o_cross.at[:, columns], sems.at[head]))
        moves[-1].start()
    for move in moves:
        move.wait()


def copy_after(source, out):
    out[...] = source[...]


def attend(hops, last, sides, *refs):
    count = len(hops)
    queries, refs = refs[: len(sides)], refs[len(sides) :]
    blocks, refs = refs[: 2 * count], refs[2 * count :]
    taken = 2 * len(sides) if last else 0
    carried, refs = refs[:taken], refs[taken:]
    outs, (keys, values) = refs[:-2], refs[-2:]
    rows, wide = queries[0].shape
    heads = wide // HD
    length, width = blocks[0].shape[0], blocks[0].shape[1] // 2
    group = wide // width
    total = 2 * count * length
    low, high, depth = bits()
    for i, block in enumerate(blocks):
        keys[pl.ds(i * length, length), :] = block[:, pl.ds(0, width)]
        values[pl.ds(i * length, length), :] = block[:, pl.ds(width, width)]
    column = lax.broadcasted_iota(jnp.int32, (1, total), 1)
    limit = jnp.zeros((1, total), jnp.int32)
    for i in range(2 * count):
        s, t = hops[i // 2], i % 2
        if s == 0:
            core = low if t == 0 else 1 - low
            at = column + ((2 * high + core) * length - i * length)
        else:
            at = jnp.where(jnp.bitwise_xor(depth, s) < depth, -1, 4 * rows)
        limit = jnp.where(column >= i * length, at, limit)
    scale = 1.0 / (math.sqrt(HD) * math.log(2.0))
    row = lax.rem(lax.broadcasted_iota(jnp.int32, (group * rows, total), 0), rows)
    lane = lax.broadcasted_iota(jnp.int32, (rows, LANES), 1)
    for which, (query, side) in enumerate(zip(queries, sides)):
        place = jnp.bitwise_xor(high, side)
        allowed = row + (2 * place + low) * rows >= limit
        stats = jnp.zeros((rows, LANES), F32)
        if last:
            mixed_ref, stats_ref = carried[2 * which : 2 * which + 2]
            out = outs[which]
        else:
            out, stats_out = outs[2 * which : 2 * which + 2]
        for first in range(0, heads, group):
            members = range(first, first + group)
            shared = pl.ds((first // group) * HD, HD)
            stacked = jnp.concatenate([query[:, pl.ds(h * HD, HD)] for h in members], axis=0)
            scores = dot(stacked, keys[:, shared], ((1,), (1,))) * scale
            masked = jnp.where(allowed, scores, FAR)
            top = jnp.maximum(jnp.max(masked, axis=1, keepdims=True), NEAR)
            if last:
                old = jnp.concatenate([stats_ref[:, 2 * h : 2 * h + 1] for h in members], axis=0)
                top = jnp.maximum(top, old)
            weights = jnp.exp2(masked - top)
            summed = jnp.sum(weights, axis=1, keepdims=True)
            mixed = dot(weights.astype(BF16), values[:, shared], ((1,), (0,)))
            for i, h in enumerate(members):
                columns, part = pl.ds(h * HD, HD), slice(i * rows, (i + 1) * rows)
                if not last:
                    out[:, columns] = mixed[part]
                    stats = jnp.where(lane == 2 * h, top[part], stats)
                    stats = jnp.where(lane == 2 * h + 1, summed[part], stats)
                    continue
                shrink = jnp.exp2(old[part] - top[part])
                whole = summed[part] + shrink * stats_ref[:, 2 * h + 1 : 2 * h + 2]
                some = whole > 0.0
                safe = jnp.where(some, whole, 1.0)
                out[:, columns] = ((mixed[part] + shrink * mixed_ref[:, columns]) / safe).astype(
                    out.dtype
                )
                level = jnp.where(some, top[part] + jnp.log2(safe), FAR)
                for k, third in enumerate(thirds(level)):
                    stats = jnp.where(lane == 3 * h + k, third, stats)
        if last:
            out[:, pl.ds(wide, LANES)] = stats.astype(out.dtype)
        else:
            stats_out[...] = stats


def merge(head, keep_ref, other_ref, out):
    wide = out.shape[1]
    ins = (keep_ref, other_ref)
    columns = pl.ds(head * HD, HD)
    tiles = [ref[:, pl.ds(wide, LANES)].astype(F32) for ref in ins]
    levels = [
        tile[:, 3 * head : 3 * head + 1]
        + tile[:, 3 * head + 1 : 3 * head + 2]
        + tile[:, 3 * head + 2 : 3 * head + 3]
        for tile in tiles
    ]
    top = functools.reduce(jnp.maximum, levels)
    weights = [jnp.exp2(level - top) for level in levels]
    share = 1.0 / functools.reduce(jnp.add, weights)
    mixed = functools.reduce(
        jnp.add, [(w * share) * ref[:, columns].astype(F32) for w, ref in zip(weights, ins)]
    )
    out[:, columns] = mixed.astype(BF16)


def per_device(count, n, q_ret, k_ret, v_ret, gate_ret, log_decay, q_cross, cache_k, cache_v):
    far = count // 4
    rows, wide = q_cross.shape
    heads = wide // HD
    length, width = cache_k.shape[0], cache_k.shape[1] // n
    half, quarter = HD // 2, HD // 4

    def swap(value, bit, wanted=None):
        pairs = [
            (b ^ bit if wanted is None or wanted(b // 4) else b, b) for b in range(count)
        ]
        return lax.ppermute(value, "ctx", pairs)

    def to_head(value, e):
        return lax.ppermute(value, "head", [(y, (y + e) % n) for y in range(n)])

    plain = (k_ret, v_ret, log_decay.T, q_ret, q_cross, gate_ret)
    loaded = call(
        functools.partial(load_all, n, 2 + len(plain)),
        [pltpu.VMEM((length, 2 * width), BF16)] * n
        + [pltpu.VMEM(a.shape, a.dtype) for a in plain]
        + [pltpu.VMEM((half + PAD, wide), BF16), pltpu.VMEM((half + PAD, wide), F32)],
        [pltpu.with_memory_space_constraint(a, pltpu.HBM) for a in (cache_k, cache_v, *plain)],
        scratch=[pltpu.VMEM((HD, wide), F32), pltpu.SemaphoreType.DMA((2 * n + len(plain),))],
        name="load_all",
        takes=HBM,
    )
    pieces = loaded[:n]
    k_ret, v_ret, decays, q_ret, q_cross, gate_ret, sum_send, sum_keep = loaded[n:]
    arrived = [pieces[0]] + [to_head(pieces[e], e) for e in range(1, n)]
    sum_other = swap(sum_send, 1)
    chip_send, chip_keep = call(
        chip_total,
        [shape((quarter + PAD, wide)), shape((quarter + PAD, wide), F32)],
        (sum_keep, sum_other),
        scratch=[pltpu.VMEM((half, wide), F32)],
        name="chip_total",
    )
    inside, factor = call(
        retain_inside,
        [shape((rows, wide), F32), shape((rows, heads), F32)],
        (q_ret, k_ret, v_ret, decays),
        name="retain_inside",
        after=(chip_send,),
    )
    blocks = {
        0: call(
            functools.partial(join_rows, n),
            [shape((n * length, 2 * width))],
            arrived,
            name="join_rows",
            flops=3000000000,
        )
    }
    chip_other = swap(chip_send, 2)
    bit = far // 2
    while bit > 1:
        for s in list(blocks):
            blocks[s ^ bit] = swap(blocks[s], 4 * bit)
        bit //= 2
    window, handed = call(
        plane_total,
        [shape((quarter + PAD, wide)), shape(blocks[0].shape)],
        (chip_keep, chip_other, blocks[0]),
        name="plane_total",
        after=(factor,),
    )
    blocks[1] = swap(handed, 4)
    q_cross = pass_on(q_cross, blocks[far // 2])
    q_other = swap(q_cross, 2)
    planes, bit = [], 1
    while bit < far:
        planes.append(swap(window, 4 * bit))
        if 2 * bit < far:
            window = call(
                functools.partial(grow, bit),
                [shape(window.shape)],
                (window, planes[-1]),
                name="grow",
                flops=3000000000,
                after=tuple(blocks[s] for s in blocks if s),
            )
        bit *= 2

    def look(hops, last, outs, queries, carried, name):
        keys = 2 * len(hops) * n * length
        both = []
        for s in hops:
            if s not in swapped:
                swapped[s] = swap(blocks[s], 1)
            both += [blocks[s], swapped[s]]
        return call(
            functools.partial(attend, hops, last, [side for _, side in queries]),
            outs,
            (*[query for query, _ in queries], *both, *carried),
            scratch=[pltpu.VMEM((keys, width), BF16) for _ in range(2)],
            name=name,
        )

    swapped = {}
    near = list(blocks)
    so_far = look(
        near,
        False,
        [shape((rows, wide), F32), shape((rows, LANES), F32)] * 2,
        ((q_other, 1), (q_cross, 0)),
        (),
        "attend_near",
    )
    prior_send, prior_keep = call(
        chip_priors,
        [shape((quarter, wide)), shape((quarter, wide), F32)],
        (chip_keep, chip_other, *planes),
        name="chip_priors",
        flops=3000000000,
        after=so_far[1:2],
    )
    for s in near:
        if s > 1:
            ready = call(copy_after, [shape(blocks[s].shape)], (blocks[s],), after=(window,))
            last = swap(ready, 4, lambda z, s=s: (z ^ s ^ 1) < z)
            blocks[s ^ 1] = pass_on(last, prior_send)
    hops = [s for s in blocks if s not in near]
    packed = (rows, wide + LANES)
    part_send = look(hops, True, [shape(packed)], ((q_other, 1),), so_far[:2], "attend_far")
    part_keep = look(hops, True, [shape(packed, F32)], ((q_cross, 0),), so_far[2:], "attend_own")
    part_other = swap(part_send, 2)
    prior_other = swap(prior_send, 2)
    state_send, state_keep = call(
        block_priors,
        [shape((half, wide)), shape((half, wide))],
        (sum_keep, sum_other, prior_keep, prior_other),
        scratch=[pltpu.VMEM((half, wide), F32)],
        name="block_priors",
    )
    state_other = swap(state_send, 1)
    done = pltpu.VMEM((rows, wide), BF16)
    o_ret = call(
        retain_finish,
        [shape((rows, wide))],
        (q_ret, gate_ret, inside, factor, state_keep, state_other),
        scratch=[pltpu.VMEM((HD, wide), BF16), done, pltpu.SemaphoreType.DMA],
        name="retain_finish",
        gives=HBM,
    )
    o_cross = call(
        finish,
        [shape((rows, wide))],
        (part_keep, part_other),
        scratch=[done, pltpu.SemaphoreType.DMA((heads,))],
        name="finish",
        gives=HBM,
    )
    return o_ret, o_cross


def solution(mesh):
    split = P("ctx", "head")
    rows = P(("ctx", "head"), None)
    return jax.shard_map(
        functools.partial(per_device, mesh.shape["ctx"], mesh.shape["head"]),
        mesh=mesh,
        in_specs=(split,) * 6 + (rows,) * 2,
        out_specs=(split, split),
        check_vma=False,
    )
```

```python
import functools
import math

import jax
import jax.numpy as jnp
from jax import lax
from jax.experimental import pallas as pl
from jax.experimental.pallas import tpu as pltpu
from jax.sharding import PartitionSpec as P

HD = 256
FAR = -1e30
NEAR = -1e29
EPS = 1e-06
F32 = jnp.float32
BF16 = jnp.bfloat16
PAD = 16
LANES = 128
VMEM = pl.BlockSpec(memory_space=pltpu.VMEM)
ANY = pl.BlockSpec(memory_space=pl.ANY)
HBM = pl.BlockSpec(memory_space=pltpu.HBM)


def call(
    body, outs, args, scratch=(), name=None, flops=1000, takes=VMEM, gives=VMEM, after=(),
    aliases=None,
):
    single = len(outs) == 1
    used, total = len(args), len(args) + len(after)

    def kernel(*refs):
        body(*refs[:used], *refs[total:])

    return pl.pallas_call(
        kernel,
        out_shape=outs[0] if single else tuple(outs),
        in_specs=(takes if isinstance(takes, list) else [takes] * used) + [ANY] * len(after),
        out_specs=gives if single or isinstance(gives, tuple) else tuple(gives for _ in outs),
        scratch_shapes=scratch,
        input_output_aliases=aliases or {},
        compiler_params=pltpu.CompilerParams(vmem_limit_bytes=40 * 1024 * 1024),
        cost_estimate=pl.CostEstimate(flops=flops, bytes_accessed=1000, transcendentals=0),
        name=name,
    )(*args, *after)


def pass_on(value, *after):
    return call(
        lambda *refs: None,
        [shape(value.shape, value.dtype)],
        (value,),
        name="pass_on",
        takes=ANY,
        gives=ANY,
        after=after,
        aliases={0: 0},
    )


def shape(dims, dtype=BF16):
    return jax.ShapeDtypeStruct(dims, dtype)


def dot(a, b, contract, precision=None):
    return lax.dot_general(
        a, b, (contract, ((), ())), preferred_element_type=F32, precision=precision
    )


def thirds(value):
    high = value.astype(BF16).astype(F32)
    rest = value - high
    middle = rest.astype(BF16).astype(F32)
    return high, middle, rest - middle


def lower_ones(rows):
    below = lax.broadcasted_iota(jnp.int32, (rows, rows), 0) >= lax.broadcasted_iota(
        jnp.int32, (rows, rows), 1
    )
    return below, jnp.where(below, 1.0, 0.0).astype(F32)


def join_rows(n, *refs):
    pieces, out = refs[:n], refs[n]
    length = pieces[0].shape[0]
    here = lax.axis_index("head")
    for e, piece in enumerate(pieces):
        place = lax.rem(here + n - e, n)
        out[pl.ds(pl.multiple_of(place * length, PAD), length), :] = piece[...]


def bits():
    index = lax.axis_index("ctx")
    low = lax.rem(index, 2)
    return low, lax.rem(lax.div(index, 2), 2), lax.div(index, 4)


def put_total(out, at, total):
    wide = out.shape[1]
    if out.dtype == F32:
        out[pl.ds(at, PAD), :] = jnp.broadcast_to(total, (PAD, wide))
        return
    row = lax.broadcasted_iota(jnp.int32, (PAD, wide), 0)
    high, middle, low = thirds(total)
    tile = jnp.where(row == 0, high, jnp.where(row == 1, middle, jnp.where(row == 2, low, 0.0)))
    out[pl.ds(at, PAD), :] = tile.astype(out.dtype)


def total_of(ref):
    tile = ref[pl.ds(ref.shape[0] - PAD, PAD), :].astype(F32)
    if ref.dtype == F32:
        return tile[0:1, :]
    return tile[0:1, :] + tile[1:2, :] + tile[2:3, :]


def state_of(ref):
    return ref[pl.ds(0, ref.shape[0] - PAD), :].astype(F32)


def part_of(held, which, rows):
    return held[pl.ds(pl.multiple_of(which * rows, rows), rows), :]


def summarize(k_ref, v_ref, d_ref, send, keep, held):
    low, _, _ = bits()
    half = HD // 2
    rows = d_ref.shape[1]
    sums = dot(lower_ones(rows)[1], d_ref[...], ((1,), (1,)), lax.Precision.HIGHEST)
    totals = []
    for head in range(d_ref.shape[0]):
        columns = pl.ds(head * HD, HD)
        column = sums[:, head : head + 1]
        last = column[rows - 1 : rows, :]
        carried = (k_ref[:, columns].astype(F32) * jnp.exp(last - column)).astype(BF16)
        held[:, columns] = dot(carried, v_ref[:, columns], ((0,), (0,)))
        totals.append(jnp.broadcast_to(last, (1, HD)))
    total = jnp.concatenate(totals, axis=1)
    for out, which in ((send, 1 - low), (keep, low)):
        out[pl.ds(0, half), :] = part_of(held, which, half).astype(out.dtype)
        put_total(out, half, total)


def load_all(n, count, *refs):
    k_ref, v_ref, *plain = refs[:count]
    outs, (held, sems) = refs[count:-2], refs[-2:]
    pieces, copies, (send, keep) = outs[:n], outs[n:-2], outs[-2:]
    width = k_ref.shape[1] // n
    here = lax.axis_index("head")
    moves = list(zip(plain, copies))
    for e, piece in enumerate(pieces):
        target = lax.rem(here + e, n)
        columns = pl.ds(pl.multiple_of(target * width, LANES), width)
        moves.append((k_ref.at[:, columns], piece.at[:, pl.ds(0, width)]))
        moves.append((v_ref.at[:, columns], piece.at[:, pl.ds(width, width)]))
    running = [pltpu.make_async_copy(a, b, sems.at[i]) for i, (a, b) in enumerate(moves)]
    for one in running:
        one.start()
    for one in running[:3]:
        one.wait()
    summarize(*copies[:3], send, keep, held)
    for one in running[3:]:
        one.wait()


def pair_total(first, keep_ref, other_ref):
    kept, other = state_of(keep_ref), state_of(other_ref)
    kept_total, other_total = total_of(keep_ref), total_of(other_ref)
    late = jnp.where(first, other_total, kept_total)
    earlier, later = jnp.where(first, kept, other), jnp.where(first, other, kept)
    return jnp.exp(late) * earlier + later, kept_total + other_total


def chip_total(keep_ref, other_ref, send, keep, held):
    low, high, _ = bits()
    quarter = HD // 4
    held[...], total = pair_total(low == 0, keep_ref, other_ref)
    for out, which in ((send, 1 - high), (keep, high)):
        out[pl.ds(0, quarter), :] = part_of(held, which, quarter).astype(out.dtype)
        put_total(out, quarter, total)


def plane_total(keep_ref, other_ref, block_ref, out, block_out):
    block_out[...] = block_ref[...]
    _, high, _ = bits()
    state, total = pair_total(high == 0, keep_ref, other_ref)
    out[pl.ds(0, state.shape[0]), :] = state.astype(out.dtype)
    put_total(out, state.shape[0], total)


def chip_priors(keep_ref, other_ref, *refs):
    planes, send, keep = refs[:-2], refs[-2], refs[-1]
    _, high, depth = bits()
    entering = jnp.zeros(send.shape, F32)
    between = jnp.zeros((1, send.shape[1]), F32)
    for i, ref in enumerate(planes):
        earlier = lax.rem(lax.div(depth, 2**i), 2) == 1
        entering = entering + jnp.where(earlier, jnp.exp(between) * state_of(ref), 0.0)
        between = between + jnp.where(earlier, total_of(ref), 0.0)
    first = high == 0
    early = jnp.where(first, state_of(keep_ref), state_of(other_ref))
    early_total = jnp.where(first, total_of(keep_ref), total_of(other_ref))
    second = jnp.exp(early_total) * entering + early
    send[...] = jnp.where(first, second, entering).astype(send.dtype)
    keep[...] = jnp.where(first, entering, second).astype(keep.dtype)


def block_priors(keep_ref, other_ref, prior_ref, prior_other_ref, send, keep, held):
    low, high, _ = bits()
    quarter = prior_ref.shape[0]
    for ref, which in ((prior_ref, high), (prior_other_ref, 1 - high)):
        held[pl.ds(pl.multiple_of(which * quarter, quarter), quarter), :] = ref[...].astype(F32)
    first = low == 0
    early = jnp.where(first, state_of(keep_ref), state_of(other_ref))
    early_total = jnp.where(first, total_of(keep_ref), total_of(other_ref))
    entering = held[...]
    second = jnp.exp(early_total) * entering + early
    send[...] = jnp.where(first, second, entering).astype(send.dtype)
    keep[...] = jnp.where(first, entering, second).astype(keep.dtype)


def grow(bit, own_ref, other_ref, out):
    rows = out.shape[0] - PAD
    first = lax.rem(lax.div(bits()[2], bit), 2) == 0
    state, total = pair_total(first, own_ref, other_ref)
    out[pl.ds(0, rows), :] = state.astype(out.dtype)
    put_total(out, rows, total)


def retain_inside(q_ref, k_ref, v_ref, d_ref, inside_ref, factor_ref):
    heads, rows = d_ref.shape
    below, ones = lower_ones(rows)
    sums = dot(ones, d_ref[...], ((1,), (1,)), lax.Precision.HIGHEST)
    same = lax.broadcasted_iota(jnp.int32, (rows, rows), 0) == lax.broadcasted_iota(
        jnp.int32, (rows, rows), 1
    )
    factor_ref[...] = jnp.exp(sums)
    for head in range(heads):
        columns = pl.ds(head * HD, HD)
        column = jnp.broadcast_to(sums[:, head : head + 1], (rows, rows))
        across = jnp.sum(jnp.where(same, column, 0.0), axis=0, keepdims=True)
        spread = jnp.exp(jnp.minimum(column - across, 0.0))
        scores = dot(q_ref[:, columns], k_ref[:, columns], ((1,), (1,)))
        weights = jnp.where(below, spread * scores, 0.0).astype(BF16)
        inside_ref[:, columns] = dot(weights, v_ref[:, columns], ((1,), (0,)))


def retain_finish(q_ref, gate_ref, inside_ref, factor_ref, keep_ref, other_ref, o_ret, held, done, sem):
    low, _, _ = bits()
    half = keep_ref.shape[0]
    for ref, which in ((keep_ref, low), (other_ref, 1 - low)):
        held[pl.ds(pl.multiple_of(which * half, half), half), :] = ref[...]
    for head in range(factor_ref.shape[1]):
        columns = pl.ds(head * HD, HD)
        before = dot(q_ref[:, columns], held[:, columns], ((1,), (0,)))
        retained = inside_ref[:, columns] + factor_ref[:, head : head + 1] * before
        scale = lax.rsqrt(jnp.mean(retained * retained, axis=1, keepdims=True) + EPS)
        gate = gate_ref[:, columns].astype(F32)
        silu = gate / (1.0 + jnp.exp(-gate))
        done[:, columns] = (retained * scale * silu).astype(BF16)
    out = pltpu.make_async_copy(done, o_ret, sem)
    out.start()
    out.wait()


def finish(part_ref, part_other_ref, o_cross, done, sems):
    wide = done.shape[1]
    moves = []
    for head in range(wide // HD):
        merge(head, part_ref, part_other_ref, done)
        columns = pl.ds(head * HD, HD)
        moves.append(pltpu.make_async_copy(done.at[:, columns], o_cross.at[:, columns], sems.at[head]))
        moves[-1].start()
    for move in moves:
        move.wait()


def copy_after(source, out):
    out[...] = source[...]


def diagonal(rows):
    dims = (rows, rows)
    return lax.broadcasted_iota(jnp.int32, dims, 0) == lax.broadcasted_iota(jnp.int32, dims, 1)


def attend(hops, last, sides, *refs):
    count = len(hops)
    queries, refs = refs[: len(sides)], refs[len(sides) :]
    blocks, refs = refs[: 2 * count], refs[2 * count :]
    taken = 2 * len(sides) if last else 0
    carried, refs = refs[:taken], refs[taken:]
    outs, (keys, values) = refs[:-2], refs[-2:]
    rows, wide = queries[0].shape
    heads = wide // HD
    length, width = blocks[0].shape[0], blocks[0].shape[1] // 2
    group = wide // width
    total = 2 * count * length
    low, high, depth = bits()
    for i, block in enumerate(blocks):
        keys[pl.ds(i * length, length), :] = block[:, pl.ds(0, width)]
        values[pl.ds(i * length, length), :] = block[:, pl.ds(width, width)]
    column = lax.broadcasted_iota(jnp.int32, (1, total), 1)
    limit = jnp.zeros((1, total), jnp.int32)
    for i in range(2 * count):
        s, t = hops[i // 2], i % 2
        if s == 0:
            core = low if t == 0 else 1 - low
            at = column + ((2 * high + core) * length - i * length)
        else:
            at = jnp.where(jnp.bitwise_xor(depth, s) < depth, -1, 4 * rows)
        limit = jnp.where(column >= i * length, at, limit)
    scale = 1.0 / (math.sqrt(HD) * math.log(2.0))
    row = lax.rem(lax.broadcasted_iota(jnp.int32, (group * rows, total), 0), rows)
    lane = lax.broadcasted_iota(jnp.int32, (rows, LANES), 1)
    for which, (query, side) in enumerate(zip(queries, sides)):
        place = jnp.bitwise_xor(high, side)
        allowed = row + (2 * place + low) * rows >= limit
        stats = jnp.zeros((rows, LANES), F32)
        levels = jnp.zeros((PAD, rows), F32)
        line = lax.broadcasted_iota(jnp.int32, (PAD, rows), 0)
        if last:
            mixed_ref, stats_ref = carried[2 * which : 2 * which + 2]
            out = outs[which]
        else:
            out, stats_out = outs[2 * which : 2 * which + 2]
        for first in range(0, heads, group):
            members = range(first, first + group)
            shared = pl.ds((first // group) * HD, HD)
            stacked = jnp.concatenate([query[:, pl.ds(h * HD, HD)] for h in members], axis=0)
            scores = dot(stacked, keys[:, shared], ((1,), (1,))) * scale
            masked = jnp.where(allowed, scores, FAR)
            top = jnp.maximum(jnp.max(masked, axis=1, keepdims=True), NEAR)
            if last:
                old = jnp.concatenate([stats_ref[:, 2 * h : 2 * h + 1] for h in members], axis=0)
                top = jnp.maximum(top, old)
            weights = jnp.exp2(masked - top)
            summed = jnp.sum(weights, axis=1, keepdims=True)
            mixed = dot(weights.astype(BF16), values[:, shared], ((1,), (0,)))
            for i, h in enumerate(members):
                columns, part = pl.ds(h * HD, HD), slice(i * rows, (i + 1) * rows)
                if not last:
                    out[:, columns] = mixed[part]
                    stats = jnp.where(lane == 2 * h, top[part], stats)
                    stats = jnp.where(lane == 2 * h + 1, summed[part], stats)
                    continue
                shrink = jnp.exp2(old[part] - top[part])
                whole = summed[part] + shrink * stats_ref[:, 2 * h + 1 : 2 * h + 2]
                some = whole > 0.0
                safe = jnp.where(some, whole, 1.0)
                out[pl.ds(0, rows), columns] = ((mixed[part] + shrink * mixed_ref[:, columns]) / safe).astype(
                    out.dtype
                )
                level = jnp.where(some, top[part] + jnp.log2(safe), FAR)
                across = jnp.sum(jnp.where(diagonal(rows), level, 0.0), axis=0, keepdims=True)
                for k, third in enumerate(thirds(across)):
                    levels = jnp.where(line == 3 * h + k, third, levels)
        if last:
            out[pl.ds(rows, PAD), :] = jnp.zeros((PAD, wide), out.dtype)
            out[pl.ds(rows, PAD), pl.ds(0, rows)] = levels.astype(out.dtype)
        else:
            stats_out[...] = stats


def merge(head, keep_ref, other_ref, out):
    wide = out.shape[1]
    ins = (keep_ref, other_ref)
    columns = pl.ds(head * HD, HD)
    rows = out.shape[0]
    tiles = [ref[pl.ds(rows, PAD), pl.ds(0, rows)].astype(F32) for ref in ins]
    across = [
        tile[3 * head : 3 * head + 1, :]
        + tile[3 * head + 1 : 3 * head + 2, :]
        + tile[3 * head + 2 : 3 * head + 3, :]
        for tile in tiles
    ]
    levels = [
        jnp.sum(jnp.where(diagonal(rows), row, 0.0), axis=1, keepdims=True) for row in across
    ]
    top = functools.reduce(jnp.maximum, levels)
    weights = [jnp.exp2(level - top) for level in levels]
    share = 1.0 / functools.reduce(jnp.add, weights)
    mixed = functools.reduce(
        jnp.add, [(w * share) * ref[pl.ds(0, rows), columns].astype(F32) for w, ref in zip(weights, ins)]
    )
    out[:, columns] = mixed.astype(BF16)


def per_device(count, n, q_ret, k_ret, v_ret, gate_ret, log_decay, q_cross, cache_k, cache_v):
    far = count // 4
    rows, wide = q_cross.shape
    heads = wide // HD
    length, width = cache_k.shape[0], cache_k.shape[1] // n
    half, quarter = HD // 2, HD // 4

    def swap(value, bit, wanted=None):
        pairs = [
            (b ^ bit if wanted is None or wanted(b // 4) else b, b) for b in range(count)
        ]
        return lax.ppermute(value, "ctx", pairs)

    def to_head(value, e):
        return lax.ppermute(value, "head", [(y, (y + e) % n) for y in range(n)])

    plain = (k_ret, v_ret, log_decay.T, q_ret, q_cross, gate_ret)
    loaded = call(
        functools.partial(load_all, n, 2 + len(plain)),
        [pltpu.VMEM((length, 2 * width), BF16)] * n
        + [pltpu.VMEM(a.shape, a.dtype) for a in plain]
        + [pltpu.VMEM((half + PAD, wide), BF16), pltpu.VMEM((half + PAD, wide), F32)],
        [pltpu.with_memory_space_constraint(a, pltpu.HBM) for a in (cache_k, cache_v, *plain)],
        scratch=[pltpu.VMEM((HD, wide), F32), pltpu.SemaphoreType.DMA((2 * n + len(plain),))],
        name="load_all",
        takes=HBM,
    )
    pieces = loaded[:n]
    k_ret, v_ret, decays, q_ret, q_cross, gate_ret, sum_send, sum_keep = loaded[n:]
    arrived = [pieces[0]] + [to_head(pieces[e], e) for e in range(1, n)]
    sum_other = swap(sum_send, 1)
    chip_send, chip_keep = call(
        chip_total,
        [shape((quarter + PAD, wide)), shape((quarter + PAD, wide), F32)],
        (sum_keep, sum_other),
        scratch=[pltpu.VMEM((half, wide), F32)],
        name="chip_total",
    )
    inside, factor = call(
        retain_inside,
        [shape((rows, wide), F32), shape((rows, heads), F32)],
        (q_ret, k_ret, v_ret, decays),
        name="retain_inside",
        after=(chip_send,),
    )
    blocks = {
        0: call(
            functools.partial(join_rows, n),
            [shape((n * length, 2 * width))],
            arrived,
            name="join_rows",
            flops=3000000000,
        )
    }
    chip_other = swap(chip_send, 2)
    bit = far // 2
    while bit > 1:
        for s in list(blocks):
            blocks[s ^ bit] = swap(blocks[s], 4 * bit)
        bit //= 2
    window, handed = call(
        plane_total,
        [shape((quarter + PAD, wide)), shape(blocks[0].shape)],
        (chip_keep, chip_other, blocks[0]),
        name="plane_total",
        after=(factor,),
    )
    blocks[1] = swap(handed, 4)
    q_cross = pass_on(q_cross, blocks[far // 2])
    q_other = swap(q_cross, 2)
    planes, bit = [], 1
    while bit < far:
        planes.append(swap(window, 4 * bit))
        if 2 * bit < far:
            window = call(
                functools.partial(grow, bit),
                [shape(window.shape)],
                (window, planes[-1]),
                name="grow",
                flops=3000000000,
                after=tuple(blocks[s] for s in blocks if s),
            )
        bit *= 2

    def look(hops, last, outs, queries, carried, name):
        keys = 2 * len(hops) * n * length
        both = []
        for s in hops:
            if s not in swapped:
                swapped[s] = swap(blocks[s], 1)
            both += [blocks[s], swapped[s]]
        return call(
            functools.partial(attend, hops, last, [side for _, side in queries]),
            outs,
            (*[query for query, _ in queries], *both, *carried),
            scratch=[pltpu.VMEM((keys, width), BF16) for _ in range(2)],
            name=name,
        )

    swapped = {}
    near = list(blocks)
    so_far = look(
        near,
        False,
        [shape((rows, wide), F32), shape((rows, LANES), F32)] * 2,
        ((q_other, 1), (q_cross, 0)),
        (),
        "attend_near",
    )
    prior_send, prior_keep = call(
        chip_priors,
        [shape((quarter, wide)), shape((quarter, wide), F32)],
        (chip_keep, chip_other, *planes),
        name="chip_priors",
        flops=3000000000,
        after=so_far[1:2],
    )
    for s in near:
        if s > 1:
            ready = call(copy_after, [shape(blocks[s].shape)], (blocks[s],), after=(window,))
            last = swap(ready, 4, lambda z, s=s: (z ^ s ^ 1) < z)
            blocks[s ^ 1] = pass_on(last, prior_send)
    hops = [s for s in blocks if s not in near]
    packed = (rows + PAD, wide)
    part_send = look(hops, True, [shape(packed)], ((q_other, 1),), so_far[:2], "attend_far")
    part_keep = look(hops, True, [shape(packed, F32)], ((q_cross, 0),), so_far[2:], "attend_own")
    part_other = swap(part_send, 2)
    prior_other = swap(prior_send, 2)
    state_send, state_keep = call(
        block_priors,
        [shape((half, wide)), shape((half, wide))],
        (sum_keep, sum_other, prior_keep, prior_other),
        scratch=[pltpu.VMEM((half, wide), F32)],
        name="block_priors",
    )
    state_other = swap(state_send, 1)
    done = pltpu.VMEM((rows, wide), BF16)
    o_ret = call(
        retain_finish,
        [shape((rows, wide))],
        (q_ret, gate_ret, inside, factor, state_keep, state_other),
        scratch=[pltpu.VMEM((HD, wide), BF16), done, pltpu.SemaphoreType.DMA],
        name="retain_finish",
        gives=HBM,
    )
    o_cross = call(
        finish,
        [shape((rows, wide))],
        (part_keep, part_other),
        scratch=[done, pltpu.SemaphoreType.DMA((heads,))],
        name="finish",
        gives=HBM,
    )
    return o_ret, o_cross


def solution(mesh):
    split = P("ctx", "head")
    rows = P(("ctx", "head"), None)
    return jax.shard_map(
        functools.partial(per_device, mesh.shape["ctx"], mesh.shape["head"]),
        mesh=mesh,
        in_specs=(split,) * 6 + (rows,) * 2,
        out_specs=(split, split),
        check_vma=False,
    )
```

```python
import functools
import math

import jax
import jax.numpy as jnp
from jax import lax
from jax.experimental import pallas as pl
from jax.experimental.pallas import tpu as pltpu
from jax.sharding import PartitionSpec as P

HD = 256
FAR = -1e30
NEAR = -1e29
EPS = 1e-06
F32 = jnp.float32
BF16 = jnp.bfloat16
PAD = 16
LANES = 128
VMEM = pl.BlockSpec(memory_space=pltpu.VMEM)
ANY = pl.BlockSpec(memory_space=pl.ANY)
HBM = pl.BlockSpec(memory_space=pltpu.HBM)


def call(
    body, outs, args, scratch=(), name=None, flops=1000, takes=VMEM, gives=VMEM, after=(),
    aliases=None,
):
    single = len(outs) == 1
    used, total = len(args), len(args) + len(after)

    def kernel(*refs):
        body(*refs[:used], *refs[total:])

    return pl.pallas_call(
        kernel,
        out_shape=outs[0] if single else tuple(outs),
        in_specs=(takes if isinstance(takes, list) else [takes] * used) + [ANY] * len(after),
        out_specs=gives if single or isinstance(gives, tuple) else tuple(gives for _ in outs),
        scratch_shapes=scratch,
        input_output_aliases=aliases or {},
        compiler_params=pltpu.CompilerParams(vmem_limit_bytes=40 * 1024 * 1024),
        cost_estimate=pl.CostEstimate(flops=flops, bytes_accessed=1000, transcendentals=0),
        name=name,
    )(*args, *after)


def pass_on(value, *after):
    return call(
        lambda *refs: None,
        [shape(value.shape, value.dtype)],
        (value,),
        name="pass_on",
        takes=ANY,
        gives=ANY,
        after=after,
        aliases={0: 0},
    )


def shape(dims, dtype=BF16):
    return jax.ShapeDtypeStruct(dims, dtype)


def dot(a, b, contract, precision=None):
    return lax.dot_general(
        a, b, (contract, ((), ())), preferred_element_type=F32, precision=precision
    )


def thirds(value):
    high = value.astype(BF16).astype(F32)
    rest = value - high
    middle = rest.astype(BF16).astype(F32)
    return high, middle, rest - middle


def lower_ones(rows):
    below = lax.broadcasted_iota(jnp.int32, (rows, rows), 0) >= lax.broadcasted_iota(
        jnp.int32, (rows, rows), 1
    )
    return below, jnp.where(below, 1.0, 0.0).astype(F32)


def join_rows(n, *refs):
    pieces, out = refs[:n], refs[n]
    length = pieces[0].shape[0]
    here = lax.axis_index("head")
    for e, piece in enumerate(pieces):
        place = lax.rem(here + n - e, n)
        out[pl.ds(pl.multiple_of(place * length, PAD), length), :] = piece[...]


def bits():
    index = lax.axis_index("ctx")
    low = lax.rem(index, 2)
    return low, lax.rem(lax.div(index, 2), 2), lax.div(index, 4)


def put_total(out, at, total):
    wide = out.shape[1]
    if out.dtype == F32:
        out[pl.ds(at, PAD), :] = jnp.broadcast_to(total, (PAD, wide))
        return
    row = lax.broadcasted_iota(jnp.int32, (PAD, wide), 0)
    high, middle, low = thirds(total)
    tile = jnp.where(row == 0, high, jnp.where(row == 1, middle, jnp.where(row == 2, low, 0.0)))
    out[pl.ds(at, PAD), :] = tile.astype(out.dtype)


def total_of(ref):
    tile = ref[pl.ds(ref.shape[0] - PAD, PAD), :].astype(F32)
    if ref.dtype == F32:
        return tile[0:1, :]
    return tile[0:1, :] + tile[1:2, :] + tile[2:3, :]


def state_of(ref):
    return ref[pl.ds(0, ref.shape[0] - PAD), :].astype(F32)


def part_of(held, which, rows):
    return held[pl.ds(pl.multiple_of(which * rows, rows), rows), :]


def summarize(k_ref, v_ref, d_ref, send, keep, held):
    low, _, _ = bits()
    half = HD // 2
    rows = d_ref.shape[1]
    sums = dot(lower_ones(rows)[1], d_ref[...], ((1,), (1,)), lax.Precision.HIGHEST)
    totals = []
    for head in range(d_ref.shape[0]):
        columns = pl.ds(head * HD, HD)
        column = sums[:, head : head + 1]
        last = column[rows - 1 : rows, :]
        carried = (k_ref[:, columns].astype(F32) * jnp.exp(last - column)).astype(BF16)
        held[:, columns] = dot(carried, v_ref[:, columns], ((0,), (0,)))
        totals.append(jnp.broadcast_to(last, (1, HD)))
    total = jnp.concatenate(totals, axis=1)
    for out, which in ((send, 1 - low), (keep, low)):
        out[pl.ds(0, half), :] = part_of(held, which, half).astype(out.dtype)
        put_total(out, half, total)


def load_all(n, count, *refs):
    k_ref, v_ref, *plain = refs[:count]
    outs, (held, sems) = refs[count:-2], refs[-2:]
    pieces, copies, (send, keep) = outs[:n], outs[n:-2], outs[-2:]
    width = k_ref.shape[1] // n
    here = lax.axis_index("head")
    moves = list(zip(plain, copies))
    for e, piece in enumerate(pieces):
        target = lax.rem(here + e, n)
        columns = pl.ds(pl.multiple_of(target * width, LANES), width)
        moves.append((k_ref.at[:, columns], piece.at[:, pl.ds(0, width)]))
        moves.append((v_ref.at[:, columns], piece.at[:, pl.ds(width, width)]))
    running = [pltpu.make_async_copy(a, b, sems.at[i]) for i, (a, b) in enumerate(moves)]
    for one in running:
        one.start()
    for one in running[:3]:
        one.wait()
    summarize(*copies[:3], send, keep, held)
    for one in running[3:]:
        one.wait()


def pair_total(first, keep_ref, other_ref):
    kept, other = state_of(keep_ref), state_of(other_ref)
    kept_total, other_total = total_of(keep_ref), total_of(other_ref)
    late = jnp.where(first, other_total, kept_total)
    earlier, later = jnp.where(first, kept, other), jnp.where(first, other, kept)
    return jnp.exp(late) * earlier + later, kept_total + other_total


def chip_total(keep_ref, other_ref, send, keep, held):
    low, high, _ = bits()
    quarter = HD // 4
    held[...], total = pair_total(low == 0, keep_ref, other_ref)
    for out, which in ((send, 1 - high), (keep, high)):
        out[pl.ds(0, quarter), :] = part_of(held, which, quarter).astype(out.dtype)
        put_total(out, quarter, total)


def plane_total(keep_ref, other_ref, block_ref, out, block_out):
    block_out[...] = block_ref[...]
    _, high, _ = bits()
    state, total = pair_total(high == 0, keep_ref, other_ref)
    out[pl.ds(0, state.shape[0]), :] = state.astype(out.dtype)
    put_total(out, state.shape[0], total)


def chip_priors(keep_ref, other_ref, *refs):
    planes, send, keep = refs[:-2], refs[-2], refs[-1]
    _, high, depth = bits()
    entering = jnp.zeros(send.shape, F32)
    between = jnp.zeros((1, send.shape[1]), F32)
    for i, ref in enumerate(planes):
        earlier = lax.rem(lax.div(depth, 2**i), 2) == 1
        entering = entering + jnp.where(earlier, jnp.exp(between) * state_of(ref), 0.0)
        between = between + jnp.where(earlier, total_of(ref), 0.0)
    first = high == 0
    early = jnp.where(first, state_of(keep_ref), state_of(other_ref))
    early_total = jnp.where(first, total_of(keep_ref), total_of(other_ref))
    second = jnp.exp(early_total) * entering + early
    send[...] = jnp.where(first, second, entering).astype(send.dtype)
    keep[...] = jnp.where(first, entering, second).astype(keep.dtype)


def block_priors(keep_ref, other_ref, prior_ref, prior_other_ref, send, keep, held):
    low, high, _ = bits()
    quarter = prior_ref.shape[0]
    for ref, which in ((prior_ref, high), (prior_other_ref, 1 - high)):
        held[pl.ds(pl.multiple_of(which * quarter, quarter), quarter), :] = ref[...].astype(F32)
    first = low == 0
    early = jnp.where(first, state_of(keep_ref), state_of(other_ref))
    early_total = jnp.where(first, total_of(keep_ref), total_of(other_ref))
    entering = held[...]
    second = jnp.exp(early_total) * entering + early
    send[...] = jnp.where(first, second, entering).astype(send.dtype)
    keep[...] = jnp.where(first, entering, second).astype(keep.dtype)


def grow(bit, own_ref, other_ref, out):
    rows = out.shape[0] - PAD
    first = lax.rem(lax.div(bits()[2], bit), 2) == 0
    state, total = pair_total(first, own_ref, other_ref)
    out[pl.ds(0, rows), :] = state.astype(out.dtype)
    put_total(out, rows, total)


def retain_inside(q_ref, k_ref, v_ref, d_ref, inside_ref, factor_ref):
    heads, rows = d_ref.shape
    below, ones = lower_ones(rows)
    sums = dot(ones, d_ref[...], ((1,), (1,)), lax.Precision.HIGHEST)
    same = lax.broadcasted_iota(jnp.int32, (rows, rows), 0) == lax.broadcasted_iota(
        jnp.int32, (rows, rows), 1
    )
    factor_ref[...] = jnp.exp(sums)
    for head in range(heads):
        columns = pl.ds(head * HD, HD)
        column = jnp.broadcast_to(sums[:, head : head + 1], (rows, rows))
        across = jnp.sum(jnp.where(same, column, 0.0), axis=0, keepdims=True)
        spread = jnp.exp(jnp.minimum(column - across, 0.0))
        scores = dot(q_ref[:, columns], k_ref[:, columns], ((1,), (1,)))
        weights = jnp.where(below, spread * scores, 0.0).astype(BF16)
        inside_ref[:, columns] = dot(weights, v_ref[:, columns], ((1,), (0,)))


def retain_finish(q_ref, gate_ref, inside_ref, factor_ref, keep_ref, other_ref, o_ret, held, done, sem):
    low, _, _ = bits()
    half = keep_ref.shape[0]
    for ref, which in ((keep_ref, low), (other_ref, 1 - low)):
        held[pl.ds(pl.multiple_of(which * half, half), half), :] = ref[...]
    for head in range(factor_ref.shape[1]):
        columns = pl.ds(head * HD, HD)
        before = dot(q_ref[:, columns], held[:, columns], ((1,), (0,)))
        retained = inside_ref[:, columns] + factor_ref[:, head : head + 1] * before
        scale = lax.rsqrt(jnp.mean(retained * retained, axis=1, keepdims=True) + EPS)
        gate = gate_ref[:, columns].astype(F32)
        silu = gate / (1.0 + jnp.exp(-gate))
        done[:, columns] = (retained * scale * silu).astype(BF16)
    out = pltpu.make_async_copy(done, o_ret, sem)
    out.start()
    out.wait()


def finish(part_ref, part_other_ref, o_cross, done, sems):
    wide = done.shape[1]
    moves = []
    for head in range(wide // HD):
        merge(head, part_ref, part_other_ref, done)
        columns = pl.ds(head * HD, HD)
        moves.append(pltpu.make_async_copy(done.at[:, columns], o_cross.at[:, columns], sems.at[head]))
        moves[-1].start()
    for move in moves:
        move.wait()


def copy_after(source, out):
    out[...] = source[...]


def diagonal(rows):
    dims = (rows, rows)
    return lax.broadcasted_iota(jnp.int32, dims, 0) == lax.broadcasted_iota(jnp.int32, dims, 1)


def attend(hops, last, sides, *refs):
    count = len(hops)
    queries, refs = refs[: len(sides)], refs[len(sides) :]
    blocks, refs = refs[: 2 * count], refs[2 * count :]
    taken = 2 * len(sides) if last else 0
    carried, refs = refs[:taken], refs[taken:]
    outs, (keys, values) = refs[:-2], refs[-2:]
    rows, wide = queries[0].shape
    heads = wide // HD
    length, width = blocks[0].shape[0], blocks[0].shape[1] // 2
    group = wide // width
    total = 2 * count * length
    low, high, depth = bits()
    for i, block in enumerate(blocks):
        keys[pl.ds(i * length, length), :] = block[:, pl.ds(0, width)]
        values[pl.ds(i * length, length), :] = block[:, pl.ds(width, width)]
    column = lax.broadcasted_iota(jnp.int32, (1, total), 1)
    limit = jnp.zeros((1, total), jnp.int32)
    for i in range(2 * count):
        s, t = hops[i // 2], i % 2
        if s == 0:
            core = low if t == 0 else 1 - low
            at = column + ((2 * high + core) * length - i * length)
        else:
            at = jnp.where(jnp.bitwise_xor(depth, s) < depth, -1, 4 * rows)
        limit = jnp.where(column >= i * length, at, limit)
    scale = 1.0 / (math.sqrt(HD) * math.log(2.0))
    row = lax.rem(lax.broadcasted_iota(jnp.int32, (group * rows, total), 0), rows)
    lane = lax.broadcasted_iota(jnp.int32, (rows, LANES), 1)
    for which, (query, side) in enumerate(zip(queries, sides)):
        place = jnp.bitwise_xor(high, side)
        allowed = row + (2 * place + low) * rows >= limit
        stats = jnp.zeros((rows, LANES), F32)
        levels = jnp.zeros((PAD, rows), F32)
        line = lax.broadcasted_iota(jnp.int32, (PAD, rows), 0)
        if last:
            mixed_ref, stats_ref = carried[2 * which : 2 * which + 2]
            out = outs[which]
        else:
            out, stats_out = outs[2 * which : 2 * which + 2]
        for first in range(0, heads, group):
            members = range(first, first + group)
            shared = pl.ds((first // group) * HD, HD)
            stacked = jnp.concatenate([query[:, pl.ds(h * HD, HD)] for h in members], axis=0)
            scores = dot(stacked, keys[:, shared], ((1,), (1,))) * scale
            masked = jnp.where(allowed, scores, FAR)
            top = jnp.maximum(jnp.max(masked, axis=1, keepdims=True), NEAR)
            if last:
                old = jnp.concatenate([stats_ref[:, 2 * h : 2 * h + 1] for h in members], axis=0)
                top = jnp.maximum(top, old)
            weights = jnp.exp2(masked - top)
            summed = jnp.sum(weights, axis=1, keepdims=True)
            mixed = dot(weights.astype(BF16), values[:, shared], ((1,), (0,)))
            for i, h in enumerate(members):
                columns, part = pl.ds(h * HD, HD), slice(i * rows, (i + 1) * rows)
                if not last:
                    out[:, columns] = mixed[part]
                    stats = jnp.where(lane == 2 * h, top[part], stats)
                    stats = jnp.where(lane == 2 * h + 1, summed[part], stats)
                    continue
                shrink = jnp.exp2(old[part] - top[part])
                whole = summed[part] + shrink * stats_ref[:, 2 * h + 1 : 2 * h + 2]
                some = whole > 0.0
                safe = jnp.where(some, whole, 1.0)
                out[pl.ds(0, rows), columns] = ((mixed[part] + shrink * mixed_ref[:, columns]) / safe).astype(
                    out.dtype
                )
                level = jnp.where(some, top[part] + jnp.log2(safe), FAR)
                across = jnp.sum(jnp.where(diagonal(rows), level, 0.0), axis=0, keepdims=True)
                for k, third in enumerate(thirds(across)):
                    levels = jnp.where(line == 3 * h + k, third, levels)
        if last:
            out[pl.ds(rows, PAD), :] = jnp.zeros((PAD, wide), out.dtype)
            out[pl.ds(rows, PAD), pl.ds(0, rows)] = levels.astype(out.dtype)
        else:
            stats_out[...] = stats


def merge(head, keep_ref, other_ref, out):
    wide = out.shape[1]
    ins = (keep_ref, other_ref)
    columns = pl.ds(head * HD, HD)
    rows = out.shape[0]
    tiles = [ref[pl.ds(rows, PAD), pl.ds(0, rows)].astype(F32) for ref in ins]
    across = [
        tile[3 * head : 3 * head + 1, :]
        + tile[3 * head + 1 : 3 * head + 2, :]
        + tile[3 * head + 2 : 3 * head + 3, :]
        for tile in tiles
    ]
    levels = [
        jnp.sum(jnp.where(diagonal(rows), row, 0.0), axis=1, keepdims=True) for row in across
    ]
    top = functools.reduce(jnp.maximum, levels)
    weights = [jnp.exp2(level - top) for level in levels]
    share = 1.0 / functools.reduce(jnp.add, weights)
    mixed = functools.reduce(
        jnp.add, [(w * share) * ref[pl.ds(0, rows), columns].astype(F32) for w, ref in zip(weights, ins)]
    )
    out[:, columns] = mixed.astype(BF16)


def per_device(count, n, q_ret, k_ret, v_ret, gate_ret, log_decay, q_cross, cache_k, cache_v):
    far = count // 4
    rows, wide = q_cross.shape
    heads = wide // HD
    length, width = cache_k.shape[0], cache_k.shape[1] // n
    half, quarter = HD // 2, HD // 4

    def swap(value, bit, wanted=None):
        pairs = [
            (b ^ bit if wanted is None or wanted(b // 4) else b, b) for b in range(count)
        ]
        return lax.ppermute(value, "ctx", pairs)

    def to_head(value, e):
        return lax.ppermute(value, "head", [(y, (y + e) % n) for y in range(n)])

    plain = (k_ret, v_ret, log_decay.T, q_ret, q_cross, gate_ret)
    loaded = call(
        functools.partial(load_all, n, 2 + len(plain)),
        [pltpu.VMEM((length, 2 * width), BF16)] * n
        + [pltpu.VMEM(a.shape, a.dtype) for a in plain]
        + [pltpu.VMEM((half + PAD, wide), BF16), pltpu.VMEM((half + PAD, wide), F32)],
        [pltpu.with_memory_space_constraint(a, pltpu.HBM) for a in (cache_k, cache_v, *plain)],
        scratch=[pltpu.VMEM((HD, wide), F32), pltpu.SemaphoreType.DMA((2 * n + len(plain),))],
        name="load_all",
        takes=HBM,
    )
    pieces = loaded[:n]
    k_ret, v_ret, decays, q_ret, q_cross, gate_ret, sum_send, sum_keep = loaded[n:]
    arrived = [pieces[0]] + [to_head(pieces[e], e) for e in range(1, n)]
    sum_other = swap(sum_send, 1)
    chip_send, chip_keep = call(
        chip_total,
        [shape((quarter + PAD, wide)), shape((quarter + PAD, wide), F32)],
        (sum_keep, sum_other),
        scratch=[pltpu.VMEM((half, wide), F32)],
        name="chip_total",
    )
    blocks = {
        0: call(
            functools.partial(join_rows, n),
            [shape((n * length, 2 * width))],
            arrived,
            name="join_rows",
            flops=3000000000,
        )
    }
    chip_other = swap(chip_send, 2)
    bit = far // 2
    while bit > 1:
        for s in list(blocks):
            blocks[s ^ bit] = swap(blocks[s], 4 * bit)
        bit //= 2
    window, handed = call(
        plane_total,
        [shape((quarter + PAD, wide)), shape(blocks[0].shape)],
        (chip_keep, chip_other, blocks[0]),
        name="plane_total",
    )
    blocks[1] = swap(handed, 4)
    q_cross = pass_on(q_cross, blocks[far // 2])
    q_other = swap(q_cross, 2)
    planes, bit = [], 1
    while bit < far:
        planes.append(swap(window, 4 * bit))
        if 2 * bit < far:
            window = call(
                functools.partial(grow, bit),
                [shape(window.shape)],
                (window, planes[-1]),
                name="grow",
                flops=3000000000,
                after=tuple(blocks[s] for s in blocks if s),
            )
        bit *= 2

    def look(hops, last, outs, queries, carried, name):
        keys = 2 * len(hops) * n * length
        both = []
        for s in hops:
            if s not in swapped:
                swapped[s] = swap(blocks[s], 1)
            both += [blocks[s], swapped[s]]
        return call(
            functools.partial(attend, hops, last, [side for _, side in queries]),
            outs,
            (*[query for query, _ in queries], *both, *carried),
            scratch=[pltpu.VMEM((keys, width), BF16) for _ in range(2)],
            name=name,
        )

    swapped = {}
    near = list(blocks)
    so_far = look(
        near,
        False,
        [shape((rows, wide), F32), shape((rows, LANES), F32)] * 2,
        ((q_other, 1), (q_cross, 0)),
        (),
        "attend_near",
    )
    inside, factor = call(
        retain_inside,
        [shape((rows, wide), F32), shape((rows, heads), F32)],
        (q_ret, k_ret, v_ret, decays),
        name="retain_inside",
        after=so_far[1:2],
    )
    prior_send, prior_keep = call(
        chip_priors,
        [shape((quarter, wide)), shape((quarter, wide), F32)],
        (chip_keep, chip_other, *planes),
        name="chip_priors",
        flops=3000000000,
        after=(so_far[1], factor),
    )
    for s in near:
        if s > 1:
            ready = call(copy_after, [shape(blocks[s].shape)], (blocks[s],), after=(window,))
            last = swap(ready, 4, lambda z, s=s: (z ^ s ^ 1) < z)
            blocks[s ^ 1] = pass_on(last, prior_send)
    hops = [s for s in blocks if s not in near]
    packed = (rows + PAD, wide)
    part_send = look(hops, True, [shape(packed)], ((q_other, 1),), so_far[:2], "attend_far")
    part_keep = look(hops, True, [shape(packed, F32)], ((q_cross, 0),), so_far[2:], "attend_own")
    part_other = swap(part_send, 2)
    prior_other = swap(prior_send, 2)
    state_send, state_keep = call(
        block_priors,
        [shape((half, wide)), shape((half, wide))],
        (sum_keep, sum_other, prior_keep, prior_other),
        scratch=[pltpu.VMEM((half, wide), F32)],
        name="block_priors",
    )
    state_other = swap(state_send, 1)
    done = pltpu.VMEM((rows, wide), BF16)
    o_ret = call(
        retain_finish,
        [shape((rows, wide))],
        (q_ret, gate_ret, inside, factor, state_keep, state_other),
        scratch=[pltpu.VMEM((HD, wide), BF16), done, pltpu.SemaphoreType.DMA],
        name="retain_finish",
        gives=HBM,
    )
    o_cross = call(
        finish,
        [shape((rows, wide))],
        (part_keep, part_other),
        scratch=[done, pltpu.SemaphoreType.DMA((heads,))],
        name="finish",
        gives=HBM,
    )
    return o_ret, o_cross


def solution(mesh):
    split = P("ctx", "head")
    rows = P(("ctx", "head"), None)
    return jax.shard_map(
        functools.partial(per_device, mesh.shape["ctx"], mesh.shape["head"]),
        mesh=mesh,
        in_specs=(split,) * 6 + (rows,) * 2,
        out_specs=(split, split),
        check_vma=False,
    )
```
